128 devices in a mesh: particle: 16 (over x, z), tensor: 8 (over y, core).
Axes of the slice: x: 4, y: 4, z: 4, core: 2. Of those that a mesh axis runs over, the one named last changes fastest.
Arguments:
- inputs: bfloat16 [256, 2, 8192], P('particle'), may hold values from -6 to 6
- norm_gain: float32 [8192], replicated, may hold values from 0.125 to 2
- query_proj: bfloat16 [256, 2, 8192], P('particle', None, 'tensor'), may hold values from -6 to 6
- w_key: bfloat16 [8192, 1024], P(None, 'tensor'), may hold values from -0.5 to 0.5
- w_value: bfloat16 [8192, 1024], P(None, 'tensor'), may hold values from -0.125 to 0.125
- w_out: bfloat16 [8192, 8192], P('tensor'), may hold values from -0.0625 to 0.0625
- kv_cache: bfloat16 [256, 8, 512, 256], P('particle', 'tensor'), may hold values from -200 to 200
- ancestors: int32 [256], P('particle'), may hold values from 0 to 255, as said below
Outputs:
- attn_out: bfloat16 [256, 2, 8192], P('particle', None, 'tensor')
The draws below stay inside these ranges and needn't reach their ends.
Inputs may be any that keep to these rules, and one draw needn't show every extreme that they name: The 16 particles of one device (aligned blocks of ancestors) take their ancestors from exactly 8 distinct devices, 2 particles from each; two of them may share an ancestor.
All inputs are finite; a program needn't handle non-finite values.
Results may differ from the reference program's by a relative error of at most 0.019.
Values may be sent and summed in bfloat16 or wider, within the bound.
No kernel may reach another device: no remote copies, remote signals or barrier semaphores. Data moves between devices by JAX's collectives and lax.ppermute only.
A program may use at most 128 MiB of HBM per device.

```python
import math
import jax
import jax.numpy as jnp
from jax import lax

D = 8192
HD = 128
Q_HEADS = 64
KV_HEADS = 8
CTX = 512
STEPS = 2
PAIR = 2
PART_DEV = 16
PARTICLES = 256


def draw_ancestors(key, part):
    key = jax.random.fold_in(key, 11)
    key_perm, key_first, key_other, key_same, key_order = jax.random.split(key, 5)
    devices_count = PARTICLES // PART_DEV
    groups = PART_DEV // PAIR
    perms = jax.vmap(lambda single: jax.random.permutation(single, devices_count))(jax.random.split(key_perm, devices_count))
    sources = jnp.repeat(perms[:, :groups, None], PAIR, axis=2)
    first = jax.random.randint(key_first, (devices_count, groups, 1), 0, PART_DEV)
    other = jax.random.randint(key_other, (devices_count, groups, PAIR), 0, PART_DEV)
    same = jax.random.randint(key_same, (devices_count, groups, PAIR), 0, 3) == 0
    slot_index = jnp.arange(PAIR).reshape(1, 1, PAIR)
    local = jnp.where((slot_index == 0) | same, first, other)
    chosen = (sources * PART_DEV + local).reshape(devices_count, PART_DEV)
    orders = jax.vmap(lambda single: jax.random.permutation(single, PART_DEV))(jax.random.split(key_order, devices_count))
    chosen = jnp.take_along_axis(chosen, orders, axis=1)
    return chosen.reshape(PARTICLES).astype(jnp.int32)


def draw_kv_cache(key, part):
    key = jax.random.fold_in(key, 23)
    key_keys, key_vals = jax.random.split(key, 2)
    shape = (PARTICLES, KV_HEADS, CTX, HD)
    keys = jax.random.truncated_normal(key_keys, -4.0, 4.0, shape, jnp.float32)
    values = 3.0 * jax.random.truncated_normal(key_vals, -4.0, 4.0, shape, jnp.float32)
    return jnp.concatenate([keys, values], -1).astype(jnp.bfloat16)


def shard_levels(rng, extent, cuts, least, high):
    factor_of = 1.0
    for dim, parts in cuts:
        steps = jax.random.uniform(jax.random.fold_in(jax.random.fold_in(rng, 6), dim), (parts,), jnp.float32, least / len(cuts), high / len(cuts))
        factor_of = factor_of * jnp.repeat(jnp.exp(steps), extent[dim] // parts).reshape((-1,) + (1,) * (len(extent) - 1 - dim))
    return factor_of


def normal_values(own_key, extent, deviation, reach, cuts=(), held_as=jnp.bfloat16):
    drawn = deviation * jax.random.normal(own_key, extent, jnp.float32)
    if cuts:
        drawn = drawn * shard_levels(own_key, extent, cuts, -0.22, 0.18)
    return jnp.clip(drawn, -reach, reach).astype(held_as)


def setup_inputs(seed: int = 0) -> dict:
    splits = jax.random.split(jax.random.key(seed), 9)
    return {
        "inputs": normal_values(splits[0], (PARTICLES, STEPS, D), 1.0, 6.0, ((0, 16),)),
        "norm_gain": jnp.clip(jnp.exp(jax.random.uniform(splits[1], (D,), jnp.float32, math.log(0.125), math.log(2.0))), 0.125, 2.0),
        "query_proj": normal_values(splits[2], (PARTICLES, STEPS, Q_HEADS * HD), 1.0, 6.0, ((0, 16), (2, 8))),
        "w_key": normal_values(splits[3], (D, KV_HEADS * HD), (D // 64) ** -0.5, 0.5, ((1, 8),)),
        "w_value": normal_values(splits[4], (D, KV_HEADS * HD), (D // 4) ** -0.5, 0.125, ((1, 8),)),
        "w_out": normal_values(splits[5], (Q_HEADS * HD, D), (Q_HEADS * HD) ** -0.5, 0.0625, ((0, 8),)),
        "kv_cache": draw_kv_cache(jax.random.fold_in(splits[8], 71), 0),
        "ancestors": draw_ancestors(jax.random.fold_in(splits[8], 71), 0),
    }


theta_base = 500000.0
epsilon = 1e-05

def rotate(values, offset):
    half = values.shape[-1] // 2
    step_count = values.shape[1]
    freqs = theta_base ** (-jnp.arange(half, dtype=jnp.float32) * 2.0 / values.shape[-1])
    position = (offset + jnp.arange(step_count, dtype=jnp.float32)).reshape(1, step_count, 1, 1)
    angles = position * freqs
    cosine = jnp.cos(angles)
    sine = jnp.sin(angles)
    first = values[..., :half]
    second = values[..., half:]
    return jnp.concatenate([first * cosine - second * sine, second * cosine + first * sine], -1)

def reference(inputs, norm_gain, query_proj, w_key, w_value, w_out, kv_cache, ancestors):
    group = Q_HEADS // KV_HEADS
    scale = HD ** (-0.5)
    floats = inputs.astype(jnp.float32)
    normed = (floats * lax.rsqrt(lax.optimization_barrier(jnp.mean(floats * floats, -1, keepdims=True)) + epsilon) * norm_gain).astype(jnp.bfloat16)
    flat = normed.reshape(PARTICLES * STEPS, D)
    offset = jnp.float32(CTX)
    queries = rotate(query_proj.astype(jnp.float32).reshape(PARTICLES, STEPS, Q_HEADS, HD), offset).astype(jnp.bfloat16)
    queries = queries.reshape(PARTICLES, STEPS, KV_HEADS, group, HD)
    new_keys = rotate(jnp.dot(flat, w_key, preferred_element_type=jnp.float32).reshape(PARTICLES, STEPS, KV_HEADS, HD), offset).astype(jnp.bfloat16)
    new_values = jnp.dot(flat, w_value, preferred_element_type=jnp.float32).astype(jnp.bfloat16).reshape(PARTICLES, STEPS, KV_HEADS, HD)

    def cache_part(pair):
        query_one, anchor = pair
        cache = lax.dynamic_index_in_dim(kv_cache, anchor.astype(jnp.int32), 0, keepdims=False)
        keys = cache[..., :HD].astype(jnp.float32)
        vals = cache[..., HD:].astype(jnp.float32)
        scores = jnp.einsum('skgd,kcd->skgc', query_one.astype(jnp.float32), keys) * scale
        top_score = lax.optimization_barrier(jnp.max(scores, -1))
        expo = jnp.exp(scores - top_score[..., None])
        total = lax.optimization_barrier(jnp.sum(expo, -1))
        rounded = lax.optimization_barrier(expo.astype(jnp.bfloat16)).astype(jnp.float32)
        vector = jnp.einsum('skgc,kcd->skgd', rounded, vals)
        return (vector, total, top_score)
    cache_vec, cache_sum, cache_max = lax.map(cache_part, (queries, ancestors))
    fresh = jnp.einsum('rskgd,rtkd->rskgt', queries.astype(jnp.float32), new_keys.astype(jnp.float32)) * scale
    allowed = (jnp.arange(STEPS)[:, None] >= jnp.arange(STEPS)[None, :]).reshape(1, STEPS, 1, 1, STEPS)
    fresh = jnp.where(allowed, fresh, jnp.float32(-1e+30))
    fresh_max = lax.optimization_barrier(jnp.max(fresh, -1))
    fresh_exp = jnp.exp(fresh - fresh_max[..., None])
    fresh_sum = lax.optimization_barrier(jnp.sum(fresh_exp, -1))
    fresh_rounded = lax.optimization_barrier(fresh_exp.astype(jnp.bfloat16)).astype(jnp.float32)
    fresh_vec = jnp.einsum('rskgt,rtkd->rskgd', fresh_rounded, new_values.astype(jnp.float32))
    highest = jnp.maximum(cache_max, fresh_max)
    cache_factor = jnp.exp(cache_max - highest)
    fresh_factor = jnp.exp(fresh_max - highest)
    heads = (cache_vec * cache_factor[..., None] + fresh_vec * fresh_factor[..., None]) / (cache_sum * cache_factor + fresh_sum * fresh_factor)[..., None]
    heads = heads.astype(jnp.bfloat16).reshape(PARTICLES * STEPS, Q_HEADS * HD)
    return jnp.dot(heads, w_out, preferred_element_type=jnp.float32).astype(jnp.bfloat16).reshape(PARTICLES, STEPS, D)
```

```python
import functools

import jax
import jax.numpy as jnp
import numpy as np
from jax import lax
from jax.experimental import pallas as pl
from jax.experimental.pallas import tpu as pltpu
from jax.sharding import PartitionSpec as P

PAIR = 2
THETA = 500000.0
EPSILON = 1e-05
F32 = jnp.float32
BF16 = jnp.bfloat16
MIB = 1 << 20
NT = (((1,), (1,)), ((), ()))


def rotary_tables(context, steps, head_dim):
    half = head_dim // 2
    freqs = np.float32(THETA) ** (-np.arange(half, dtype=np.float32) * np.float32(2.0) / np.float32(head_dim))
    position = (np.float32(context) + np.arange(steps, dtype=np.float32)).reshape(steps, 1)
    angles = (position * freqs.astype(np.float32)).astype(np.float32)
    cosine, sine = np.cos(angles), np.sin(angles)
    return (
        np.concatenate([cosine, cosine], 1).astype(np.float32),
        np.concatenate([-sine, sine], 1).astype(np.float32),
    )


def slot_of(anc, row, rows, count):
    source = lax.div(anc[row], rows)
    rank = count[source]
    count[source] = rank + 1
    return source, rank


def pack_kernel(anc, qp, cosine, sine, send, queries, grid_ref, count, spots):
    rows, steps, width = qp.shape
    head_dim = cosine.shape[1]
    heads = width // head_dim
    devices = send.shape[0]
    for h in range(heads):
        grid_ref[:, steps * h : steps * (h + 1), :] = qp[:, :, head_dim * h : head_dim * (h + 1)].astype(F32)
    flat = grid_ref[...].reshape(rows * heads * steps, head_dim)
    swapped = pltpu.roll(flat, head_dim // 2, 1)
    shape = (rows, heads * steps, head_dim)
    turned = flat.reshape(shape) * cosine[...][None] + swapped.reshape(shape) * sine[...][None]
    queries[...] = turned.astype(BF16)
    send[...] = jnp.zeros(send.shape, BF16)
    for d in range(devices):
        count[d] = 0
        for j in range(PAIR):
            spots[PAIR * d + j] = 0
    for r in range(rows):
        source, rank = slot_of(anc, r, rows, count)
        spots[source * PAIR + rank] = lax.rem(anc[r], rows)
        send[source, rank] = queries[r]
    lane = lax.broadcasted_iota(jnp.int32, (heads * steps, head_dim), 1)
    for d in range(devices):
        send[d, PAIR] = jnp.where(
            lane < head_dim // 2, spots[PAIR * d].astype(F32), spots[PAIR * d + 1].astype(F32)
        ).astype(BF16)


def fresh_kernel(x, gain, wk, wv, queries, cosine, sine, vec, stat):
    tokens = x.shape[0]
    head_dim = wk.shape[1]
    rows, per_row, _ = queries.shape
    steps = tokens // rows
    floats = x[...].astype(F32)
    mean = jnp.mean(floats * floats, -1, keepdims=True)
    normed = (floats * lax.rsqrt(mean + EPSILON) * gain[...]).astype(BF16)
    keys = jnp.dot(normed, wk[...], preferred_element_type=F32)
    keys = (keys * cosine[...] + pltpu.roll(keys, head_dim // 2, 1) * sine[...]).astype(BF16)
    vals = jnp.dot(normed, wv[...], preferred_element_type=F32).astype(BF16)
    flat = queries[...].reshape(rows * per_row, head_dim)
    scores = lax.dot_general(flat, keys, NT, preferred_element_type=F32) * head_dim ** (-0.5)
    row = lax.broadcasted_iota(jnp.int32, scores.shape, 0)
    col = lax.broadcasted_iota(jnp.int32, scores.shape, 1)
    seen = (lax.div(row, per_row) == lax.div(col, steps)) & (lax.rem(col, steps) <= lax.rem(row, steps))
    top = jnp.max(jnp.where(seen, scores, -jnp.inf), -1, keepdims=True)
    expo = jnp.where(seen, jnp.exp(jnp.where(seen, scores - top, 0.0)), 0.0)
    vec[...] = jnp.dot(expo.astype(BF16), vals, preferred_element_type=F32)
    lane = lax.broadcasted_iota(jnp.int32, stat.shape, 1)
    stat[...] = jnp.where(lane == 0, top, jnp.sum(expo, -1, keepdims=True))


def cache_kernel(recv, kv, back):
    devices, _, per_row, head_dim = recv.shape
    lane = lax.broadcasted_iota(jnp.int32, (per_row, head_dim), 1)
    for d in range(devices):
        spot = recv[d, PAIR].astype(F32)
        stat = jnp.zeros((per_row, head_dim), F32)
        for j in range(PAIR):
            base = j * (head_dim // PAIR)
            at = spot[0, base].astype(jnp.int32)
            keys = kv[at, 0, :, :head_dim]
            vals = kv[at, 0, :, head_dim:]
            scores = lax.dot_general(recv[d, j], keys, NT, preferred_element_type=F32) * head_dim ** (-0.5)
            top = jnp.max(scores, -1, keepdims=True)
            expo = jnp.exp(scores - top)
            total = jnp.sum(expo, -1, keepdims=True)
            vector = jnp.dot(expo.astype(BF16), vals, preferred_element_type=F32)
            back[d, j] = (vector / total).astype(BF16)
            at_lane = base
            for value, parts in ((top, 3), (total, 2)):
                for _ in range(parts):
                    part = value.astype(BF16).astype(F32)
                    stat = jnp.where(lane == at_lane, part, stat)
                    value = value - part
                    at_lane += 1
        back[d, PAIR] = stat.astype(BF16)


def project(heads, w, out, place):
    out[place] = jnp.dot(heads[...], w[...], preferred_element_type=F32).astype(BF16)


def merge_kernel(scalars, recv, vec, stat, w, out, heads, grid_ref, sums, count):
    rows = recv.shape[0]
    _, _, per_row, head_dim = recv.shape
    steps = heads.shape[0] // rows
    step = pl.program_id(0)

    @pl.when(step == 0)
    def _():
        for d in range(recv.shape[0]):
            count[d] = 0
        for r in range(rows):
            source, rank = slot_of(scalars, r, rows, count)
            grid_ref[pl.ds(r * per_row, per_row), :] = recv[source, rank].astype(F32)
            both = recv[source, PAIR].astype(F32)
            sums[pl.ds(r * per_row, per_row), :] = jnp.where(rank == 0, both, pltpu.roll(both, head_dim // 2, 1))
        parts = sums[...]
        top_c = parts[:, 0:1] + parts[:, 1:2] + parts[:, 2:3]
        sum_c = parts[:, 3:4] + parts[:, 4:5]
        fresh = stat[...]
        top_f, sum_f = fresh[:, 0:1], fresh[:, 1:2]
        top = jnp.maximum(top_c, top_f)
        factor_c = sum_c * jnp.exp(top_c - top)
        factor_f = jnp.exp(top_f - top)
        share = 1.0 / (factor_c + sum_f * factor_f)
        grid_ref[...] = grid_ref[...] * (factor_c * share) + vec[...] * (factor_f * share)
        for h in range(per_row // steps):
            for s in range(steps):
                heads[pl.ds(s * rows, rows), pl.ds(h * head_dim, head_dim)] = grid_ref[
                    pl.ds(h * steps + s, rows, stride=per_row), :
                ].astype(BF16)

    project(heads, w, out, step)


def second_kernel(scalars, heads, w, out):
    project(heads, w, out, pl.program_id(0))


def whole(shape):
    return pl.BlockSpec(shape, lambda *_: (0,) * len(shape))


def shards(inputs, norm_gain, query_proj, w_key, w_value, w_out, kv_cache, ancestors):
    rows, steps, width = inputs.shape
    context = kv_cache.shape[2]
    head_dim = kv_cache.shape[3] // 2
    local = query_proj.shape[2]
    heads = local // head_dim
    per_row = heads * steps
    devices = lax.axis_size("particle")
    tensor = lax.axis_size("tensor")
    column = width // tensor
    cosine, sine = rotary_tables(context, steps, head_dim)
    smem = pl.BlockSpec(memory_space=pltpu.SMEM)
    vmem = pl.BlockSpec(memory_space=pltpu.VMEM)

    packed = (devices, PAIR + 1, per_row, head_dim)
    send, queries = pl.pallas_call(
        pack_kernel,
        out_shape=(
            jax.ShapeDtypeStruct(packed, BF16),
            jax.ShapeDtypeStruct((rows, per_row, head_dim), BF16),
        ),
        in_specs=[smem, vmem, vmem, vmem],
        out_specs=(vmem, vmem),
        scratch_shapes=[
            pltpu.VMEM((rows, per_row, head_dim), F32),
            pltpu.SMEM((devices,), jnp.int32),
            pltpu.SMEM((devices * PAIR,), jnp.int32),
        ],
        compiler_params=pltpu.CompilerParams(vmem_limit_bytes=8 * MIB),
        name="pack_queries",
    )(ancestors, query_proj, np.tile(cosine, (heads, 1)), np.tile(sine, (heads, 1)))

    recv = lax.all_to_all(send, "particle", split_axis=0, concat_axis=0, tiled=True)

    vec, stat = pl.pallas_call(
        fresh_kernel,
        out_shape=(
            jax.ShapeDtypeStruct((rows * per_row, head_dim), F32),
            jax.ShapeDtypeStruct((rows * per_row, head_dim), F32),
        ),
        in_specs=[vmem] * 7,
        out_specs=(vmem, vmem),
        compiler_params=pltpu.CompilerParams(vmem_limit_bytes=16 * MIB),
        cost_estimate=pl.CostEstimate(
            flops=4 * rows * steps * width * head_dim, bytes_accessed=5 * MIB, transcendentals=0
        ),
        name="new_tokens",
    )(
        inputs.reshape(rows * steps, width),
        norm_gain.reshape(1, width),
        w_key,
        w_value,
        queries,
        np.tile(cosine, (rows, 1)),
        np.tile(sine, (rows, 1)),
    )

    back = pl.pallas_call(
        cache_kernel,
        out_shape=jax.ShapeDtypeStruct(packed, BF16),
        in_specs=[vmem, vmem],
        out_specs=vmem,
        compiler_params=pltpu.CompilerParams(vmem_limit_bytes=12 * MIB),
        cost_estimate=pl.CostEstimate(
            flops=4 * devices * PAIR * per_row * context * head_dim, bytes_accessed=5 * MIB, transcendentals=0
        ),
        name="cache_attention",
    )(recv, kv_cache)
    home = lax.all_to_all(back, "particle", split_axis=0, concat_axis=0, tiled=True)

    place = lax.axis_index("tensor")
    y, core = place // 2, place % 2
    scalars = jnp.concatenate([ancestors, jnp.stack([y, core]).astype(jnp.int32)])
    groups = tensor // 2
    w_spec = lambda own: pl.BlockSpec(
        (local, column),
        lambda i, sc: (0, 2 * lax.rem(sc[rows] + i, groups) + (sc[rows + 1] if own else 1 - sc[rows + 1])),
    )
    block = (groups, rows * steps, column)
    params = pltpu.CompilerParams(vmem_limit_bytes=16 * MIB)
    cost = pl.CostEstimate(
        flops=rows * steps * local * width, bytes_accessed=local * width, transcendentals=0
    )
    other, heads_out = pl.pallas_call(
        merge_kernel,
        out_shape=(
            jax.ShapeDtypeStruct(block, BF16),
            jax.ShapeDtypeStruct((rows * steps, local), BF16),
        ),
        grid_spec=pltpu.PrefetchScalarGridSpec(
            num_scalar_prefetch=1,
            grid=(groups,),
            in_specs=[whole(packed), whole(vec.shape), whole(stat.shape), w_spec(False)],
            out_specs=(whole(block), whole((rows * steps, local))),
            scratch_shapes=[
                pltpu.VMEM((rows * per_row, head_dim), F32),
                pltpu.VMEM((rows * per_row, head_dim), F32),
                pltpu.SMEM((devices,), jnp.int32),
            ],
        ),
        compiler_params=params,
        cost_estimate=cost,
        name="merge_project_sibling",
    )(scalars, home, vec, stat, w_out)
    given = lax.ppermute(other, "tensor", [(i, i ^ 1) for i in range(tensor)])
    mine = pl.pallas_call(
        second_kernel,
        out_shape=jax.ShapeDtypeStruct(block, BF16),
        grid_spec=pltpu.PrefetchScalarGridSpec(
            num_scalar_prefetch=1,
            grid=(groups,),
            in_specs=[whole((rows * steps, local)), w_spec(True)],
            out_specs=whole(block),
        ),
        compiler_params=params,
        cost_estimate=cost,
        name="project_own",
    )(scalars, heads_out, w_out)
    pair = [(mine[k].astype(F32) + given[k].astype(F32)) for k in range(groups)]
    total = pair[0]
    for k in range(1, groups):
        ring = [(i, ((i // 2 + k) % groups) * 2 + i % 2) for i in range(tensor)]
        total = total + lax.ppermute(pair[k].astype(BF16), "tensor", ring).astype(F32)
    return total.astype(BF16).reshape(steps, rows, column).swapaxes(0, 1)


def solution(mesh):
    in_specs = (
        P("particle", None, None),
        P(),
        P("particle", None, "tensor"),
        P(None, "tensor"),
        P(None, "tensor"),
        P("tensor", None),
        P("particle", "tensor", None, None),
        P("particle"),
    )
    out_specs = P("particle", None, "tensor")
    return jax.shard_map(shards, mesh=mesh, in_specs=in_specs, out_specs=out_specs, check_vma=False)
```

```python
import jax
import jax.numpy as jnp
import numpy as np
from jax import lax
from jax.experimental import pallas as pl
from jax.experimental.pallas import tpu as pltpu
from jax.sharding import PartitionSpec as P

PAIR = 2
THETA = 500000.0
EPSILON = 1e-05
F32 = jnp.float32
BF16 = jnp.bfloat16
MIB = 1 << 20
NT = (((1,), (1,)), ((), ()))


def rotary_tables(context, steps, head_dim):
    half = head_dim // 2
    freqs = np.float32(THETA) ** (-np.arange(half, dtype=np.float32) * np.float32(2.0) / np.float32(head_dim))
    position = (np.float32(context) + np.arange(steps, dtype=np.float32)).reshape(steps, 1)
    angles = (position * freqs.astype(np.float32)).astype(np.float32)
    cosine, sine = np.cos(angles), np.sin(angles)
    return (
        np.concatenate([cosine, cosine], 1).astype(np.float32),
        np.concatenate([-sine, sine], 1).astype(np.float32),
    )


def slot_of(anc, row, rows, count):
    source = lax.div(anc[row], rows)
    rank = count[source]
    count[source] = rank + 1
    return source, rank


def pack_kernel(anc_hbm, qp_hbm, tables_hbm, send, queries, grid_ref, qp, tables, anc, count, spots, sems):
    copies = [
        pltpu.make_async_copy(src, dst, sems.at[i])
        for i, (src, dst) in enumerate(((qp_hbm, qp), (tables_hbm, tables), (anc_hbm, anc)))
    ]
    for copy in copies:
        copy.start()
    rows, steps, width = qp.shape
    _, per_row, head_dim = tables.shape
    devices = send.shape[0]
    send[...] = jnp.zeros(send.shape, BF16)
    for d in range(devices):
        count[d] = 0
        for j in range(PAIR):
            spots[PAIR * d + j] = 0
    for copy in copies:
        copy.wait()
    for h in range(width // head_dim):
        grid_ref[:, steps * h : steps * (h + 1), :] = qp[:, :, head_dim * h : head_dim * (h + 1)].astype(F32)
    flat = grid_ref[...].reshape(rows * per_row, head_dim)
    swapped = pltpu.roll(flat, head_dim // 2, 1)
    shape = (rows, per_row, head_dim)
    turned = flat.reshape(shape) * tables[0][None] + swapped.reshape(shape) * tables[1][None]
    queries[...] = turned.astype(BF16)
    for r in range(rows):
        source, rank = slot_of(anc, r, rows, count)
        spots[source * PAIR + rank] = lax.rem(anc[r], rows)
        send[source, rank] = queries[r]
    lane = lax.broadcasted_iota(jnp.int32, (per_row, head_dim), 1)
    for d in range(devices):
        send[d, PAIR] = jnp.where(
            lane < head_dim // 2, spots[PAIR * d].astype(F32), spots[PAIR * d + 1].astype(F32)
        ).astype(BF16)


def fresh_kernel(
    x, gain_hbm, wk_hbm, wv_hbm, queries, tables_hbm, kv_hbm, vec, stat, old, wk, wv, gain, tables, sems
):
    copies = [
        pltpu.make_async_copy(src, dst, sems.at[i])
        for i, (src, dst) in enumerate(
            ((gain_hbm, gain), (tables_hbm, tables), (wk_hbm, wk), (wv_hbm, wv), (kv_hbm.at[:, 0, :, : wk.shape[1]], old))
        )
    ]
    for copy in copies:
        copy.start()
    tokens = x.shape[0]
    rows, per_row, head_dim = queries.shape
    steps = tokens // rows
    floats = x[...].astype(F32)
    inverse = lax.rsqrt(jnp.mean(floats * floats, -1, keepdims=True) + EPSILON)
    copies[0].wait()
    normed = (floats * inverse * gain[...]).astype(BF16)
    for copy in copies[1:3]:
        copy.wait()
    repeat = tokens // per_row
    cosine, sine = (jnp.concatenate([tables[i]] * repeat, 0) for i in range(2))
    keys = jnp.dot(normed, wk[...], preferred_element_type=F32)
    keys = (keys * cosine + pltpu.roll(keys, head_dim // 2, 1) * sine).astype(BF16)
    copies[3].wait()
    vals = jnp.dot(normed, wv[...], preferred_element_type=F32).astype(BF16)
    flat = queries[...].reshape(rows * per_row, head_dim)
    scores = lax.dot_general(flat, keys, NT, preferred_element_type=F32) * head_dim ** (-0.5)
    row = lax.broadcasted_iota(jnp.int32, scores.shape, 0)
    col = lax.broadcasted_iota(jnp.int32, scores.shape, 1)
    seen = (lax.div(row, per_row) == lax.div(col, steps)) & (lax.rem(col, steps) <= lax.rem(row, steps))
    top = jnp.max(jnp.where(seen, scores, -jnp.inf), -1, keepdims=True)
    expo = jnp.where(seen, jnp.exp(jnp.where(seen, scores - top, 0.0)), 0.0)
    vec[...] = jnp.dot(expo.astype(BF16), vals, preferred_element_type=F32)
    lane = lax.broadcasted_iota(jnp.int32, stat.shape, 1)
    stat[...] = jnp.where(lane == 0, top, jnp.sum(expo, -1, keepdims=True))
    copies[4].wait()


def cache_kernel(recv, keys, kv_hbm, back, scores, expos, tops, sums, values, sem):
    devices, _, per_row, head_dim = recv.shape
    copy = pltpu.make_async_copy(kv_hbm.at[:, 0, :, keys.shape[2] :], values, sem)
    copy.start()
    slots = [(d, j) for d in range(devices) for j in range(PAIR)]
    lane = lax.broadcasted_iota(jnp.int32, (per_row, head_dim), 1)
    spots = []
    for d in range(devices):
        spot = recv[d, PAIR].astype(F32)
        for j in range(PAIR):
            spots.append(spot[0, j * (head_dim // PAIR)].astype(jnp.int32))
    for i, (d, j) in enumerate(slots):
        scores[i] = lax.dot_general(
            recv[d, j], keys[spots[i]], NT, preferred_element_type=F32
        ) * head_dim ** (-0.5)
    for i in range(len(slots)):
        score = scores[i]
        top = jnp.max(score, -1, keepdims=True)
        expo = jnp.exp(score - top)
        expos[i] = expo.astype(BF16)
        tops[i] = jnp.broadcast_to(top, lane.shape)
        sums[i] = jnp.broadcast_to(jnp.sum(expo, -1, keepdims=True), lane.shape)
    copy.wait()
    for i, (d, j) in enumerate(slots):
        vector = jnp.dot(expos[i], values[spots[i]], preferred_element_type=F32)
        back[d, j] = (vector / sums[i]).astype(BF16)
    for d in range(devices):
        stat = jnp.zeros(lane.shape, F32)
        for j in range(PAIR):
            at_lane = j * (head_dim // PAIR)
            for value, parts in ((tops[d * PAIR + j], 3), (sums[d * PAIR + j], 2)):
                for _ in range(parts):
                    part = value.astype(BF16).astype(F32)
                    stat = jnp.where(lane == at_lane, part, stat)
                    value = value - part
                    at_lane += 1
        back[d, PAIR] = stat.astype(BF16)


def project(heads, w, out, own):
    index = lax.axis_index("tensor")
    first, core = lax.div(index, 2), lax.rem(index, 2)
    core = core if own else 1 - core
    groups, _, column = out.shape
    for k in range(groups):
        block = 2 * lax.rem(first + k, groups) + core
        at = pl.multiple_of(block * column, column)
        out[k] = jnp.dot(heads[...], w[:, pl.ds(at, column)], preferred_element_type=F32).astype(BF16)


def merge_kernel(anc, recv, vec, stat, w, out, heads, grid_ref, sums, lined, count):
    devices, _, per_row, head_dim = recv.shape
    rows = vec.shape[0] // per_row
    steps = heads.shape[0] // rows
    for d in range(devices):
        count[d] = 0
    for r in range(rows):
        source, rank = slot_of(anc, r, rows, count)
        grid_ref[pl.ds(r * per_row, per_row), :] = recv[source, rank].astype(F32)
        both = recv[source, PAIR].astype(F32)
        sums[pl.ds(r * per_row, per_row), :] = jnp.where(rank == 0, both, pltpu.roll(both, head_dim // 2, 1))
    parts = sums[...]
    top_c = parts[:, 0:1] + parts[:, 1:2] + parts[:, 2:3]
    sum_c = parts[:, 3:4] + parts[:, 4:5]
    top_f, sum_f = stat[:, 0:1], stat[:, 1:2]
    top = jnp.maximum(top_c, top_f)
    factor_c = sum_c * jnp.exp(top_c - top)
    factor_f = jnp.exp(top_f - top)
    share = 1.0 / (factor_c + sum_f * factor_f)
    grid_ref[...] = grid_ref[...] * (factor_c * share) + vec[...] * (factor_f * share)
    for h in range(per_row // steps):
        for s in range(steps):
            lined[h, pl.ds(s, rows, stride=steps), :] = grid_ref[pl.ds(h * steps + s, rows, stride=per_row), :]
        heads[:, pl.ds(h * head_dim, head_dim)] = lined[h].astype(BF16)
    project(heads, w, out, False)


def second_kernel(heads, w, out):
    project(heads, w, out, True)


def shards(inputs, norm_gain, query_proj, w_key, w_value, w_out, kv_cache, ancestors):
    rows, steps, width = inputs.shape
    context = kv_cache.shape[2]
    head_dim = kv_cache.shape[3] // 2
    local = query_proj.shape[2]
    heads = local // head_dim
    per_row = heads * steps
    devices = lax.axis_size("particle")
    tensor = lax.axis_size("tensor")
    column = width // tensor
    cosine, sine = rotary_tables(context, steps, head_dim)
    tables = np.stack([np.tile(cosine, (heads, 1)), np.tile(sine, (heads, 1))])
    smem = pl.BlockSpec(memory_space=pltpu.SMEM)
    vmem = pl.BlockSpec(memory_space=pltpu.VMEM)
    stay = pl.BlockSpec(memory_space=pl.ANY)
    hbm = lambda x: pltpu.with_memory_space_constraint(x, pltpu.HBM)
    tables = hbm(jnp.asarray(tables))

    packed = (devices, PAIR + 1, per_row, head_dim)
    send, queries = pl.pallas_call(
        pack_kernel,
        out_shape=(
            jax.ShapeDtypeStruct(packed, BF16),
            jax.ShapeDtypeStruct((rows, per_row, head_dim), BF16),
        ),
        in_specs=[stay] * 3,
        out_specs=(vmem, vmem),
        scratch_shapes=[
            pltpu.VMEM((rows, per_row, head_dim), F32),
            pltpu.VMEM((rows, steps, local), BF16),
            pltpu.VMEM((2, per_row, head_dim), F32),
            pltpu.SMEM((rows,), jnp.int32),
            pltpu.SMEM((devices,), jnp.int32),
            pltpu.SMEM((devices * PAIR,), jnp.int32),
            pltpu.SemaphoreType.DMA((3,)),
        ],
        compiler_params=pltpu.CompilerParams(vmem_limit_bytes=4 * MIB),
        cost_estimate=pl.CostEstimate(flops=10_000_000_000, bytes_accessed=MIB, transcendentals=0),
        name="pack_queries",
    )(hbm(ancestors), hbm(query_proj), tables)

    recv = lax.all_to_all(send, "particle", split_axis=0, concat_axis=0, tiled=True)

    vec, stat, cached_keys = pl.pallas_call(
        fresh_kernel,
        out_shape=(
            jax.ShapeDtypeStruct((rows * per_row, head_dim), F32),
            jax.ShapeDtypeStruct((rows * per_row, head_dim), F32),
            pltpu.VMEM((rows, context, head_dim), BF16),
        ),
        in_specs=[vmem, stay, stay, stay, vmem, stay, stay],
        out_specs=(vmem, vmem, vmem),
        scratch_shapes=[
            pltpu.VMEM((width, head_dim), BF16),
            pltpu.VMEM((width, head_dim), BF16),
            pltpu.VMEM((1, width), F32),
            pltpu.VMEM((2, per_row, head_dim), F32),
            pltpu.SemaphoreType.DMA((5,)),
        ],
        compiler_params=pltpu.CompilerParams(vmem_limit_bytes=16 * MIB),
        cost_estimate=pl.CostEstimate(
            flops=4_000_000_000, bytes_accessed=5 * MIB, transcendentals=0
        ),
        name="new_tokens",
    )(
        inputs.reshape(rows * steps, width),
        hbm(norm_gain.reshape(1, width)),
        hbm(w_key),
        hbm(w_value),
        queries,
        tables,
        hbm(kv_cache),
    )

    slots = devices * PAIR
    back = pl.pallas_call(
        cache_kernel,
        out_shape=jax.ShapeDtypeStruct(packed, BF16),
        in_specs=[vmem, vmem, stay],
        out_specs=vmem,
        scratch_shapes=[
            pltpu.VMEM((slots, per_row, context), F32),
            pltpu.VMEM((slots, per_row, context), BF16),
            pltpu.VMEM((slots, per_row, head_dim), F32),
            pltpu.VMEM((slots, per_row, head_dim), F32),
            pltpu.VMEM((rows, context, head_dim), BF16),
            pltpu.SemaphoreType.DMA(()),
        ],
        compiler_params=pltpu.CompilerParams(vmem_limit_bytes=8 * MIB),
        cost_estimate=pl.CostEstimate(
            flops=10_000_000_000, bytes_accessed=5 * MIB, transcendentals=0
        ),
        name="cache_attention",
    )(recv, cached_keys, hbm(kv_cache))
    home = lax.all_to_all(back, "particle", split_axis=0, concat_axis=0, tiled=True)

    groups = tensor // 2
    block = (groups, rows * steps, column)
    params = pltpu.CompilerParams(vmem_limit_bytes=8 * MIB)
    cost = pl.CostEstimate(
        flops=rows * steps * local * width, bytes_accessed=local * width, transcendentals=0
    )
    other, heads_out = pl.pallas_call(
        merge_kernel,
        out_shape=(
            jax.ShapeDtypeStruct(block, BF16),
            jax.ShapeDtypeStruct((rows * steps, local), BF16),
        ),
        in_specs=[smem, vmem, vmem, vmem, vmem],
        out_specs=(vmem, vmem),
        scratch_shapes=[
            pltpu.VMEM((rows * per_row, head_dim), F32),
            pltpu.VMEM((rows * per_row, head_dim), F32),
            pltpu.VMEM((heads, rows * steps, head_dim), F32),
            pltpu.SMEM((devices,), jnp.int32),
        ],
        compiler_params=params,
        cost_estimate=cost,
        name="merge_project_sibling",
    )(ancestors, home, vec, stat, w_out)
    given = lax.ppermute(other, "tensor", [(i, i ^ 1) for i in range(tensor)])
    mine = pl.pallas_call(
        second_kernel,
        out_shape=jax.ShapeDtypeStruct(block, BF16),
        in_specs=[vmem, vmem],
        out_specs=vmem,
        compiler_params=params,
        cost_estimate=cost,
        name="project_own",
    )(heads_out, w_out)
    pair = [(mine[k].astype(F32) + given[k].astype(F32)) for k in range(groups)]
    total = pair[0]
    for k in range(1, groups):
        ring = [(i, ((i // 2 + k) % groups) * 2 + i % 2) for i in range(tensor)]
        total = total + lax.ppermute(pair[k].astype(BF16), "tensor", ring).astype(F32)
    return total.astype(BF16).reshape(rows, steps, column)


def solution(mesh):
    in_specs = (
        P("particle", None, None),
        P(),
        P("particle", None, "tensor"),
        P(None, "tensor"),
        P(None, "tensor"),
        P("tensor", None),
        P("particle", "tensor", None, None),
        P("particle"),
    )
    out_specs = P("particle", None, "tensor")
    return jax.shard_map(shards, mesh=mesh, in_specs=in_specs, out_specs=out_specs, check_vma=False)
```

```python
import jax
import jax.numpy as jnp
import numpy as np
from jax import lax
from jax.experimental import pallas as pl
from jax.experimental.pallas import tpu as pltpu
from jax.sharding import PartitionSpec as P

PAIR = 2
THETA = 500000.0
EPSILON = 1e-05
F32 = jnp.float32
BF16 = jnp.bfloat16
MIB = 1 << 20
NT = (((1,), (1,)), ((), ()))


def rotary_tables(context, steps, head_dim):
    half = head_dim // 2
    freqs = np.float32(THETA) ** (-np.arange(half, dtype=np.float32) * np.float32(2.0) / np.float32(head_dim))
    position = (np.float32(context) + np.arange(steps, dtype=np.float32)).reshape(steps, 1)
    angles = (position * freqs.astype(np.float32)).astype(np.float32)
    cosine, sine = np.cos(angles), np.sin(angles)
    return (
        np.concatenate([cosine, cosine], 1).astype(np.float32),
        np.concatenate([-sine, sine], 1).astype(np.float32),
    )


def slot_of(anc, row, rows, count):
    source = lax.div(anc[row], rows)
    rank = count[source]
    count[source] = rank + 1
    return source, rank


def pack_kernel(anc_hbm, qp_hbm, tables_hbm, send, queries, grid_ref, qp, tables, anc, count, spots, sems):
    copies = [
        pltpu.make_async_copy(src, dst, sems.at[i])
        for i, (src, dst) in enumerate(((qp_hbm, qp), (tables_hbm, tables), (anc_hbm, anc)))
    ]
    for copy in copies:
        copy.start()
    rows, steps, width = qp.shape
    _, per_row, head_dim = tables.shape
    devices = send.shape[0]
    send[...] = jnp.zeros(send.shape, BF16)
    for d in range(devices):
        count[d] = 0
        for j in range(PAIR):
            spots[PAIR * d + j] = 0
    for copy in copies:
        copy.wait()
    for h in range(width // head_dim):
        grid_ref[:, steps * h : steps * (h + 1), :] = qp[:, :, head_dim * h : head_dim * (h + 1)].astype(F32)
    flat = grid_ref[...].reshape(rows * per_row, head_dim)
    swapped = pltpu.roll(flat, head_dim // 2, 1)
    shape = (rows, per_row, head_dim)
    turned = flat.reshape(shape) * tables[0][None] + swapped.reshape(shape) * tables[1][None]
    queries[...] = turned.astype(BF16)
    for r in range(rows):
        source, rank = slot_of(anc, r, rows, count)
        spots[source * PAIR + rank] = lax.rem(anc[r], rows)
        send[source, rank] = queries[r]
    lane = lax.broadcasted_iota(jnp.int32, (per_row, head_dim), 1)
    for d in range(devices):
        send[d, PAIR] = jnp.where(
            lane < head_dim // 2, spots[PAIR * d].astype(F32), spots[PAIR * d + 1].astype(F32)
        ).astype(BF16)


def fresh_kernel(
    x, gain_hbm, wk_hbm, wv_hbm, queries, tables_hbm, kv_hbm, vec, stat, old, wk, wv, gain, tables, sems
):
    copies = [
        pltpu.make_async_copy(src, dst, sems.at[i])
        for i, (src, dst) in enumerate(
            ((gain_hbm, gain), (tables_hbm, tables), (wk_hbm, wk), (wv_hbm, wv), (kv_hbm.at[:, 0, :, : wk.shape[1]], old))
        )
    ]
    for copy in copies:
        copy.start()
    tokens = x.shape[0]
    rows, per_row, head_dim = queries.shape
    steps = tokens // rows
    floats = x[...].astype(F32)
    inverse = lax.rsqrt(jnp.mean(floats * floats, -1, keepdims=True) + EPSILON)
    copies[0].wait()
    normed = (floats * inverse * gain[...]).astype(BF16)
    for copy in copies[1:3]:
        copy.wait()
    repeat = tokens // per_row
    cosine, sine = (jnp.concatenate([tables[i]] * repeat, 0) for i in range(2))
    keys = jnp.dot(normed, wk[...], preferred_element_type=F32)
    keys = (keys * cosine + pltpu.roll(keys, head_dim // 2, 1) * sine).astype(BF16)
    copies[3].wait()
    vals = jnp.dot(normed, wv[...], preferred_element_type=F32).astype(BF16)
    flat = queries[...].reshape(rows * per_row, head_dim)
    scores = lax.dot_general(flat, keys, NT, preferred_element_type=F32) * head_dim ** (-0.5)
    row = lax.broadcasted_iota(jnp.int32, scores.shape, 0)
    col = lax.broadcasted_iota(jnp.int32, scores.shape, 1)
    seen = (lax.div(row, per_row) == lax.div(col, steps)) & (lax.rem(col, steps) <= lax.rem(row, steps))
    top = jnp.max(jnp.where(seen, scores, -jnp.inf), -1, keepdims=True)
    expo = jnp.where(seen, jnp.exp(jnp.where(seen, scores - top, 0.0)), 0.0)
    vec[...] = jnp.dot(expo.astype(BF16), vals, preferred_element_type=F32)
    lane = lax.broadcasted_iota(jnp.int32, stat.shape, 1)
    stat[...] = jnp.where(lane == 0, top, jnp.sum(expo, -1, keepdims=True))
    copies[4].wait()


def cache_kernel(recv, keys, kv_hbm, vectors, tops, sums, scores, expos, values, sem):
    devices, _, per_row, head_dim = recv.shape
    copy = pltpu.make_async_copy(kv_hbm.at[:, 0, :, keys.shape[2] :], values, sem)
    copy.start()
    slots = [(d, j) for d in range(devices) for j in range(PAIR)]
    lane = lax.broadcasted_iota(jnp.int32, (per_row, head_dim), 1)
    spots = []
    for d in range(devices):
        spot = recv[d, PAIR].astype(F32)
        for j in range(PAIR):
            spots.append(spot[0, j * (head_dim // PAIR)].astype(jnp.int32))
    for i, (d, j) in enumerate(slots):
        scores[i] = lax.dot_general(
            recv[d, j], keys[spots[i]], NT, preferred_element_type=F32
        ) * head_dim ** (-0.5)
    for i in range(len(slots)):
        score = scores[i]
        top = jnp.max(score, -1, keepdims=True)
        expo = jnp.exp(score - top)
        expos[i] = expo.astype(BF16)
        tops[i] = jnp.broadcast_to(top, lane.shape)
        sums[i] = jnp.broadcast_to(jnp.sum(expo, -1, keepdims=True), lane.shape)
    copy.wait()
    for i in range(len(slots)):
        vectors[i] = jnp.dot(expos[i], values[spots[i]], preferred_element_type=F32)

def return_kernel(vectors, tops, sums, back):
    devices, _, per_row, head_dim = back.shape
    lane = lax.broadcasted_iota(jnp.int32, (per_row, head_dim), 1)
    for d in range(devices):
        for j in range(PAIR):
            back[d, j] = (vectors[d * PAIR + j] / sums[d * PAIR + j]).astype(BF16)
        stat = jnp.zeros(lane.shape, F32)
        for j in range(PAIR):
            at_lane = j * (head_dim // PAIR)
            for value, parts in ((tops[d * PAIR + j], 3), (sums[d * PAIR + j], 2)):
                for _ in range(parts):
                    part = value.astype(BF16).astype(F32)
                    stat = jnp.where(lane == at_lane, part, stat)
                    value = value - part
                    at_lane += 1
        back[d, PAIR] = stat.astype(BF16)


def project(heads, w, out, own):
    index = lax.axis_index("tensor")
    first, core = lax.div(index, 2), lax.rem(index, 2)
    core = core if own else 1 - core
    groups, tokens, column = out.shape
    wide = jnp.concatenate([heads[...]] * max(1, 128 // tokens), 0)
    for k in range(groups):
        block = 2 * lax.rem(first + k, groups) + core
        at = pl.multiple_of(block * column, column)
        out[k] = jnp.dot(wide, w[:, pl.ds(at, column)], preferred_element_type=F32)[:tokens].astype(BF16)


def merge_kernel(anc, recv, vec, stat, w, out, heads, grid_ref, sums, lined, count):
    devices, _, per_row, head_dim = recv.shape
    rows = vec.shape[0] // per_row
    steps = heads.shape[0] // rows
    for d in range(devices):
        count[d] = 0
    for r in range(rows):
        source, rank = slot_of(anc, r, rows, count)
        grid_ref[pl.ds(r * per_row, per_row), :] = recv[source, rank].astype(F32)
        both = recv[source, PAIR].astype(F32)
        sums[pl.ds(r * per_row, per_row), :] = jnp.where(rank == 0, both, pltpu.roll(both, head_dim // 2, 1))
    parts = sums[...]
    top_c = parts[:, 0:1] + parts[:, 1:2] + parts[:, 2:3]
    sum_c = parts[:, 3:4] + parts[:, 4:5]
    top_f, sum_f = stat[:, 0:1], stat[:, 1:2]
    top = jnp.maximum(top_c, top_f)
    factor_c = sum_c * jnp.exp(top_c - top)
    factor_f = jnp.exp(top_f - top)
    share = 1.0 / (factor_c + sum_f * factor_f)
    grid_ref[...] = grid_ref[...] * (factor_c * share) + vec[...] * (factor_f * share)
    for h in range(per_row // steps):
        for s in range(steps):
            lined[h, pl.ds(s, rows, stride=steps), :] = grid_ref[pl.ds(h * steps + s, rows, stride=per_row), :]
        heads[:, pl.ds(h * head_dim, head_dim)] = lined[h].astype(BF16)
    project(heads, w, out, False)


def second_kernel(heads, w, out):
    project(heads, w, out, True)


def shards(inputs, norm_gain, query_proj, w_key, w_value, w_out, kv_cache, ancestors):
    rows, steps, width = inputs.shape
    context = kv_cache.shape[2]
    head_dim = kv_cache.shape[3] // 2
    local = query_proj.shape[2]
    heads = local // head_dim
    per_row = heads * steps
    devices = lax.axis_size("particle")
    tensor = lax.axis_size("tensor")
    column = width // tensor
    cosine, sine = rotary_tables(context, steps, head_dim)
    tables = np.stack([np.tile(cosine, (heads, 1)), np.tile(sine, (heads, 1))])
    smem = pl.BlockSpec(memory_space=pltpu.SMEM)
    vmem = pl.BlockSpec(memory_space=pltpu.VMEM)
    stay = pl.BlockSpec(memory_space=pl.ANY)
    hbm = lambda x: pltpu.with_memory_space_constraint(x, pltpu.HBM)
    tables = hbm(jnp.asarray(tables))

    packed = (devices, PAIR + 1, per_row, head_dim)
    send, queries = pl.pallas_call(
        pack_kernel,
        out_shape=(
            jax.ShapeDtypeStruct(packed, BF16),
            jax.ShapeDtypeStruct((rows, per_row, head_dim), BF16),
        ),
        in_specs=[stay] * 3,
        out_specs=(vmem, vmem),
        scratch_shapes=[
            pltpu.VMEM((rows, per_row, head_dim), F32),
            pltpu.VMEM((rows, steps, local), BF16),
            pltpu.VMEM((2, per_row, head_dim), F32),
            pltpu.SMEM((rows,), jnp.int32),
            pltpu.SMEM((devices,), jnp.int32),
            pltpu.SMEM((devices * PAIR,), jnp.int32),
            pltpu.SemaphoreType.DMA((3,)),
        ],
        compiler_params=pltpu.CompilerParams(vmem_limit_bytes=4 * MIB),
        cost_estimate=pl.CostEstimate(flops=10_000_000_000, bytes_accessed=MIB, transcendentals=0),
        name="pack_queries",
    )(hbm(ancestors), hbm(query_proj), tables)

    recv = lax.all_to_all(send, "particle", split_axis=0, concat_axis=0, tiled=True)

    vec, stat, cached_keys = pl.pallas_call(
        fresh_kernel,
        out_shape=(
            jax.ShapeDtypeStruct((rows * per_row, head_dim), F32),
            jax.ShapeDtypeStruct((rows * per_row, head_dim), F32),
            pltpu.VMEM((rows, context, head_dim), BF16),
        ),
        in_specs=[vmem, stay, stay, stay, vmem, stay, stay],
        out_specs=(vmem, vmem, vmem),
        scratch_shapes=[
            pltpu.VMEM((width, head_dim), BF16),
            pltpu.VMEM((width, head_dim), BF16),
            pltpu.VMEM((1, width), F32),
            pltpu.VMEM((2, per_row, head_dim), F32),
            pltpu.SemaphoreType.DMA((5,)),
        ],
        compiler_params=pltpu.CompilerParams(vmem_limit_bytes=16 * MIB),
        cost_estimate=pl.CostEstimate(
            flops=4_000_000_000, bytes_accessed=5 * MIB, transcendentals=0
        ),
        name="new_tokens",
    )(
        inputs.reshape(rows * steps, width),
        hbm(norm_gain.reshape(1, width)),
        hbm(w_key),
        hbm(w_value),
        queries,
        tables,
        hbm(kv_cache),
    )

    slots = devices * PAIR
    partial_result = jax.ShapeDtypeStruct((slots, per_row, head_dim), F32)
    found = pl.pallas_call(
        cache_kernel,
        out_shape=(partial_result,) * 3,
        in_specs=[vmem, vmem, stay],
        out_specs=(vmem,) * 3,
        scratch_shapes=[
            pltpu.VMEM((slots, per_row, context), F32),
            pltpu.VMEM((slots, per_row, context), BF16),
            pltpu.VMEM((rows, context, head_dim), BF16),
            pltpu.SemaphoreType.DMA(()),
        ],
        compiler_params=pltpu.CompilerParams(vmem_limit_bytes=8 * MIB),
        cost_estimate=pl.CostEstimate(
            flops=4 * slots * per_row * context * head_dim, bytes_accessed=5 * MIB, transcendentals=0
        ),
        name="cache_attention",
    )(recv, cached_keys, hbm(kv_cache))
    back = pl.pallas_call(
        return_kernel,
        out_shape=jax.ShapeDtypeStruct(packed, BF16),
        in_specs=[vmem] * 3,
        out_specs=vmem,
        compiler_params=pltpu.CompilerParams(vmem_limit_bytes=2 * MIB),
        cost_estimate=pl.CostEstimate(flops=10_000_000_000, bytes_accessed=MIB, transcendentals=0),
        name="pack_results",
    )(*found)
    home = lax.all_to_all(back, "particle", split_axis=0, concat_axis=0, tiled=True)

    groups = tensor // 2
    block = (groups, rows * steps, column)
    params = pltpu.CompilerParams(vmem_limit_bytes=8 * MIB)
    cost = pl.CostEstimate(
        flops=rows * steps * local * width, bytes_accessed=local * width, transcendentals=0
    )
    other, heads_out = pl.pallas_call(
        merge_kernel,
        out_shape=(
            jax.ShapeDtypeStruct(block, BF16),
            jax.ShapeDtypeStruct((rows * steps, local), BF16),
        ),
        in_specs=[smem, vmem, vmem, vmem, vmem],
        out_specs=(vmem, vmem),
        scratch_shapes=[
            pltpu.VMEM((rows * per_row, head_dim), F32),
            pltpu.VMEM((rows * per_row, head_dim), F32),
            pltpu.VMEM((heads, rows * steps, head_dim), F32),
            pltpu.SMEM((devices,), jnp.int32),
        ],
        compiler_params=params,
        cost_estimate=cost,
        name="merge_project_sibling",
    )(ancestors, home, vec, stat, w_out)
    given = lax.ppermute(other, "tensor", [(i, i ^ 1) for i in range(tensor)])
    mine = pl.pallas_call(
        second_kernel,
        out_shape=jax.ShapeDtypeStruct(block, BF16),
        in_specs=[vmem, vmem],
        out_specs=vmem,
        compiler_params=params,
        cost_estimate=cost,
        name="project_own",
    )(heads_out, w_out)
    pair = [(mine[k].astype(F32) + given[k].astype(F32)) for k in range(groups)]
    total = pair[0]
    for k in (2, 1, 3):
        ring = [(i, ((i // 2 + k) % groups) * 2 + i % 2) for i in range(tensor)]
        total = total + lax.ppermute(pair[k].astype(BF16), "tensor", ring).astype(F32)
    return total.astype(BF16).reshape(rows, steps, column)


def solution(mesh):
    in_specs = (
        P("particle", None, None),
        P(),
        P("particle", None, "tensor"),
        P(None, "tensor"),
        P(None, "tensor"),
        P("tensor", None),
        P("particle", "tensor", None, None),
        P("particle"),
    )
    out_specs = P("particle", None, "tensor")
    return jax.shard_map(shards, mesh=mesh, in_specs=in_specs, out_specs=out_specs, check_vma=False)
```

```python
import jax
import jax.numpy as jnp
import numpy as np
from jax import lax
from jax.experimental import pallas as pl
from jax.experimental.pallas import tpu as pltpu
from jax.sharding import PartitionSpec as P

PAIR = 2
THETA = 500000.0
EPSILON = 1e-05
F32 = jnp.float32
BF16 = jnp.bfloat16
MIB = 1 << 20
NT = (((1,), (1,)), ((), ()))


def rotary_tables(context, steps, head_dim):
    half = head_dim // 2
    freqs = np.float32(THETA) ** (-np.arange(half, dtype=np.float32) * np.float32(2.0) / np.float32(head_dim))
    position = (np.float32(context) + np.arange(steps, dtype=np.float32)).reshape(steps, 1)
    angles = (position * freqs.astype(np.float32)).astype(np.float32)
    cosine, sine = np.cos(angles), np.sin(angles)
    return (
        np.concatenate([cosine, cosine], 1).astype(np.float32),
        np.concatenate([-sine, sine], 1).astype(np.float32),
    )


def slot_of(anc, row, rows, count):
    source = lax.div(anc[row], rows)
    rank = count[source]
    count[source] = rank + 1
    return source, rank


def pack_kernel(anc_hbm, qp_hbm, tables_hbm, send, queries, grid_ref, qp, tables, anc, count, spots, sems):
    copies = [
        pltpu.make_async_copy(src, dst, sems.at[i])
        for i, (src, dst) in enumerate(((qp_hbm, qp), (tables_hbm, tables), (anc_hbm, anc)))
    ]
    for copy in copies:
        copy.start()
    rows, steps, width = qp.shape
    _, per_row, head_dim = tables.shape
    devices = send.shape[0]
    send[...] = jnp.zeros(send.shape, BF16)
    for d in range(devices):
        count[d] = 0
        for j in range(PAIR):
            spots[PAIR * d + j] = 0
    for copy in copies:
        copy.wait()
    for h in range(width // head_dim):
        grid_ref[:, steps * h : steps * (h + 1), :] = qp[:, :, head_dim * h : head_dim * (h + 1)].astype(F32)
    flat = grid_ref[...].reshape(rows * per_row, head_dim)
    swapped = pltpu.roll(flat, head_dim // 2, 1)
    shape = (rows, per_row, head_dim)
    turned = flat.reshape(shape) * tables[0][None] + swapped.reshape(shape) * tables[1][None]
    queries[...] = turned.astype(BF16)
    for r in range(rows):
        source, rank = slot_of(anc, r, rows, count)
        spots[source * PAIR + rank] = lax.rem(anc[r], rows)
        send[source, rank] = queries[r]
    lane = lax.broadcasted_iota(jnp.int32, (per_row, head_dim), 1)
    for d in range(devices):
        send[d, PAIR] = jnp.where(
            lane < head_dim // 2, spots[PAIR * d].astype(F32), spots[PAIR * d + 1].astype(F32)
        ).astype(BF16)


def fresh_kernel(
    x, gain_hbm, wk_hbm, wv_hbm, queries, tables_hbm, kv_hbm, vec, stat, old, wk, wv, gain, tables, sems
):
    copies = [
        pltpu.make_async_copy(src, dst, sems.at[i])
        for i, (src, dst) in enumerate(
            ((gain_hbm, gain), (tables_hbm, tables), (wk_hbm, wk), (wv_hbm, wv), (kv_hbm.at[:, 0, :, : wk.shape[1]], old))
        )
    ]
    for copy in copies:
        copy.start()
    tokens = x.shape[0]
    rows, per_row, head_dim = queries.shape
    steps = tokens // rows
    floats = x[...].astype(F32)
    inverse = lax.rsqrt(jnp.mean(floats * floats, -1, keepdims=True) + EPSILON)
    copies[0].wait()
    normed = (floats * inverse * gain[...]).astype(BF16)
    for copy in copies[1:3]:
        copy.wait()
    repeat = tokens // per_row
    cosine, sine = (jnp.concatenate([tables[i]] * repeat, 0) for i in range(2))
    keys = jnp.dot(normed, wk[...], preferred_element_type=F32)
    keys = (keys * cosine + pltpu.roll(keys, head_dim // 2, 1) * sine).astype(BF16)
    copies[3].wait()
    vals = jnp.dot(normed, wv[...], preferred_element_type=F32).astype(BF16)
    flat = queries[...].reshape(rows * per_row, head_dim)
    scores = lax.dot_general(flat, keys, NT, preferred_element_type=F32) * head_dim ** (-0.5)
    row = lax.broadcasted_iota(jnp.int32, scores.shape, 0)
    col = lax.broadcasted_iota(jnp.int32, scores.shape, 1)
    seen = (lax.div(row, per_row) == lax.div(col, steps)) & (lax.rem(col, steps) <= lax.rem(row, steps))
    top = jnp.max(jnp.where(seen, scores, -jnp.inf), -1, keepdims=True)
    expo = jnp.where(seen, jnp.exp(jnp.where(seen, scores - top, 0.0)), 0.0)
    vec[...] = jnp.dot(expo.astype(BF16), vals, preferred_element_type=F32)
    stat[0] = jnp.broadcast_to(top, stat.shape[1:])
    stat[1] = jnp.broadcast_to(jnp.sum(expo, -1, keepdims=True), stat.shape[1:])
    copies[4].wait()


def cache_kernel(recv, keys, kv_hbm, vectors, tops, sums, scores, expos, values, spots, sem):
    devices, _, per_row, head_dim = recv.shape
    lane = lax.broadcasted_iota(jnp.int32, (per_row, head_dim), 1)
    copy = pltpu.make_async_copy(kv_hbm.at[:, 0, :, head_dim:], values, sem)
    copy.start()
    half = devices // 2

    def score(part, _):
        chosen = []
        for k in range(half):
            spot = recv[part * half + k, PAIR].astype(F32)
            for j in range(PAIR):
                chosen.append(spot[0, j * (head_dim // PAIR)].astype(jnp.int32))
                spots[(part * half + k) * PAIR + j] = chosen[-1]
        for k in range(half):
            for j in range(PAIR):
                d = part * half + k
                scores[d * PAIR + j] = lax.dot_general(
                    recv[d, j], keys[chosen[k * PAIR + j]], NT, preferred_element_type=F32
                ) * head_dim ** (-0.5)
        return 0

    lax.fori_loop(0, 2, score, 0)
    for i in range(devices * PAIR):
        top = jnp.max(scores[i], -1, keepdims=True)
        expo = jnp.exp(scores[i] - top)
        expos[i] = expo.astype(BF16)
        tops[i] = jnp.broadcast_to(top, lane.shape)
        sums[i] = jnp.broadcast_to(jnp.sum(expo, -1, keepdims=True), lane.shape)
    copy.wait()
    for i in range(devices * PAIR):
        vectors[i] = jnp.dot(expos[i], values[spots[i]], preferred_element_type=F32)


def return_kernel(vectors, tops, sums, back):
    devices, _, per_row, head_dim = back.shape
    lane = lax.broadcasted_iota(jnp.int32, (per_row, head_dim), 1)
    for d in range(devices):
        for j in range(PAIR):
            back[d, j] = (vectors[d * PAIR + j] / sums[d * PAIR + j]).astype(BF16)
        stat = jnp.zeros(lane.shape, F32)
        for j in range(PAIR):
            at_lane = j * (head_dim // PAIR)
            for value, parts in ((tops[d * PAIR + j], 3), (sums[d * PAIR + j], 2)):
                for _ in range(parts):
                    part = value.astype(BF16).astype(F32)
                    stat = jnp.where(lane == at_lane, part, stat)
                    value = value - part
                    at_lane += 1
        back[d, PAIR] = stat.astype(BF16)


def project(heads, w, out, own):
    index = lax.axis_index("tensor")
    first, core = lax.div(index, 2), lax.rem(index, 2)
    core = core if own else 1 - core
    groups, tokens, column = out.shape
    wide = jnp.concatenate([heads[...]] * max(1, 128 // tokens), 0)
    for k in range(groups):
        block = 2 * lax.rem(first + k, groups) + core
        at = pl.multiple_of(block * column, column)
        out[k] = jnp.dot(wide, w[:, pl.ds(at, column)], preferred_element_type=F32)[:tokens].astype(BF16)


def merge_kernel(anc, recv, vec, stat, w, out, heads, grid_ref, sums, lined, count):
    devices, _, per_row, head_dim = recv.shape
    rows = vec.shape[0] // per_row
    steps = heads.shape[0] // rows
    half = head_dim // PAIR
    for d in range(devices):
        count[d] = 0
    lane = lax.broadcasted_iota(jnp.int32, (per_row, head_dim), 1)
    for r in range(rows):
        source, rank = slot_of(anc, r, rows, count)
        grid_ref[pl.ds(r * per_row, per_row), :] = recv[source, rank].astype(F32)
        parts = recv[source, PAIR].astype(F32)
        sums[pl.ds(r * per_row, per_row), :] = jnp.where(lax.div(lane, half) == rank, parts, 0.0).astype(BF16)
    lane_from = lax.rem(lax.broadcasted_iota(jnp.int32, (head_dim, 2 * head_dim), 0), half)
    lane_to = lax.broadcasted_iota(jnp.int32, (head_dim, 2 * head_dim), 1)
    first = jnp.where(lane_from < 3, 1.0, 0.0)
    second = jnp.where((lane_from >= 3) & (lane_from < 5), 1.0, 0.0)
    spread = jnp.where(lane_to < head_dim, first, second)
    both = jnp.dot(sums[...], spread.astype(BF16), preferred_element_type=F32)
    top_c, sum_c = both[:, :head_dim], both[:, head_dim:]
    top_f, sum_f = stat[0], stat[1]
    top = jnp.maximum(top_c, top_f)
    factor_c = sum_c * jnp.exp(top_c - top)
    factor_f = jnp.exp(top_f - top)
    share = 1.0 / (factor_c + sum_f * factor_f)
    grid_ref[...] = (grid_ref[...] * factor_c + vec[...] * factor_f) * share
    for h in range(per_row // steps):
        for s in range(steps):
            lined[h, pl.ds(s, rows, stride=steps), :] = grid_ref[pl.ds(h * steps + s, rows, stride=per_row), :]
        heads[:, pl.ds(h * head_dim, head_dim)] = lined[h].astype(BF16)
    project(heads, w, out, False)


def second_kernel(heads, w, out):
    project(heads, w, out, True)


def shards(inputs, norm_gain, query_proj, w_key, w_value, w_out, kv_cache, ancestors):
    rows, steps, width = inputs.shape
    context = kv_cache.shape[2]
    head_dim = kv_cache.shape[3] // 2
    local = query_proj.shape[2]
    heads = local // head_dim
    per_row = heads * steps
    devices = lax.axis_size("particle")
    tensor = lax.axis_size("tensor")
    column = width // tensor
    cosine, sine = rotary_tables(context, steps, head_dim)
    tables = np.stack([np.tile(cosine, (heads, 1)), np.tile(sine, (heads, 1))])
    smem = pl.BlockSpec(memory_space=pltpu.SMEM)
    vmem = pl.BlockSpec(memory_space=pltpu.VMEM)
    stay = pl.BlockSpec(memory_space=pl.ANY)
    hbm = lambda x: pltpu.with_memory_space_constraint(x, pltpu.HBM)
    tables = hbm(jnp.asarray(tables))

    packed = (devices, PAIR + 1, per_row, head_dim)
    send, queries = pl.pallas_call(
        pack_kernel,
        out_shape=(
            jax.ShapeDtypeStruct(packed, BF16),
            jax.ShapeDtypeStruct((rows, per_row, head_dim), BF16),
        ),
        in_specs=[stay] * 3,
        out_specs=(vmem, vmem),
        scratch_shapes=[
            pltpu.VMEM((rows, per_row, head_dim), F32),
            pltpu.VMEM((rows, steps, local), BF16),
            pltpu.VMEM((2, per_row, head_dim), F32),
            pltpu.SMEM((rows,), jnp.int32),
            pltpu.SMEM((devices,), jnp.int32),
            pltpu.SMEM((devices * PAIR,), jnp.int32),
            pltpu.SemaphoreType.DMA((3,)),
        ],
        compiler_params=pltpu.CompilerParams(vmem_limit_bytes=4 * MIB),
        cost_estimate=pl.CostEstimate(flops=10_000_000_000, bytes_accessed=MIB, transcendentals=0),
        name="pack_queries",
    )(hbm(ancestors), hbm(query_proj), tables)

    recv = lax.all_to_all(send, "particle", split_axis=0, concat_axis=0, tiled=True)

    vec, stat, cached_keys = pl.pallas_call(
        fresh_kernel,
        out_shape=(
            jax.ShapeDtypeStruct((rows * per_row, head_dim), F32),
            jax.ShapeDtypeStruct((2, rows * per_row, head_dim), F32),
            pltpu.VMEM((rows, context, head_dim), BF16),
        ),
        in_specs=[vmem, stay, stay, stay, vmem, stay, stay],
        out_specs=(vmem, vmem, vmem),
        scratch_shapes=[
            pltpu.VMEM((width, head_dim), BF16),
            pltpu.VMEM((width, head_dim), BF16),
            pltpu.VMEM((1, width), F32),
            pltpu.VMEM((2, per_row, head_dim), F32),
            pltpu.SemaphoreType.DMA((5,)),
        ],
        compiler_params=pltpu.CompilerParams(vmem_limit_bytes=16 * MIB),
        cost_estimate=pl.CostEstimate(
            flops=4_000_000_000, bytes_accessed=5 * MIB, transcendentals=0
        ),
        name="new_tokens",
    )(
        inputs.reshape(rows * steps, width),
        hbm(norm_gain.reshape(1, width)),
        hbm(w_key),
        hbm(w_value),
        queries,
        tables,
        hbm(kv_cache),
    )

    slots = devices * PAIR
    partial_result = jax.ShapeDtypeStruct((slots, per_row, head_dim), F32)
    found = pl.pallas_call(
        cache_kernel,
        out_shape=(partial_result,) * 3,
        in_specs=[vmem, vmem, stay],
        out_specs=(vmem,) * 3,
        scratch_shapes=[
            pltpu.VMEM((slots, per_row, context), F32),
            pltpu.VMEM((slots, per_row, context), BF16),
            pltpu.VMEM((rows, context, head_dim), BF16),
            pltpu.SMEM((slots,), jnp.int32),
            pltpu.SemaphoreType.DMA(()),
        ],
        compiler_params=pltpu.CompilerParams(vmem_limit_bytes=8 * MIB),
        cost_estimate=pl.CostEstimate(
            flops=4 * slots * per_row * context * head_dim, bytes_accessed=5 * MIB, transcendentals=0
        ),
        name="cache_attention",
    )(recv, cached_keys, hbm(kv_cache))
    back = pl.pallas_call(
        return_kernel,
        out_shape=jax.ShapeDtypeStruct(packed, BF16),
        in_specs=[vmem] * 3,
        out_specs=vmem,
        compiler_params=pltpu.CompilerParams(vmem_limit_bytes=2 * MIB),
        cost_estimate=pl.CostEstimate(flops=10_000_000_000, bytes_accessed=MIB, transcendentals=0),
        name="pack_results",
    )(*found)
    home = lax.all_to_all(back, "particle", split_axis=0, concat_axis=0, tiled=True)

    groups = tensor // 2
    block = (groups, rows * steps, column)
    params = pltpu.CompilerParams(vmem_limit_bytes=8 * MIB)
    cost = pl.CostEstimate(
        flops=rows * steps * local * width, bytes_accessed=local * width, transcendentals=0
    )
    other, heads_out = pl.pallas_call(
        merge_kernel,
        out_shape=(
            jax.ShapeDtypeStruct(block, BF16),
            jax.ShapeDtypeStruct((rows * steps, local), BF16),
        ),
        in_specs=[smem, vmem, vmem, vmem, vmem],
        out_specs=(vmem, vmem),
        scratch_shapes=[
            pltpu.VMEM((rows * per_row, head_dim), F32),
            pltpu.VMEM((rows * per_row, head_dim), BF16),
            pltpu.VMEM((heads, rows * steps, head_dim), F32),
            pltpu.SMEM((devices,), jnp.int32),
        ],
        compiler_params=params,
        cost_estimate=cost,
        name="merge_project_sibling",
    )(ancestors, home, vec, stat, w_out)
    given = lax.ppermute(other, "tensor", [(i, i ^ 1) for i in range(tensor)])
    mine = pl.pallas_call(
        second_kernel,
        out_shape=jax.ShapeDtypeStruct(block, BF16),
        in_specs=[vmem, vmem],
        out_specs=vmem,
        compiler_params=params,
        cost_estimate=cost,
        name="project_own",
    )(heads_out, w_out)
    pair = [(mine[k].astype(F32) + given[k].astype(F32)) for k in range(groups)]
    total = pair[0]
    for k in range(1, groups):
        ring = [(i, ((i // 2 + k) % groups) * 2 + i % 2) for i in range(tensor)]
        total = total + lax.ppermute(pair[k].astype(BF16), "tensor", ring).astype(F32)
    return total.astype(BF16).reshape(rows, steps, column)


def solution(mesh):
    in_specs = (
        P("particle", None, None),
        P(),
        P("particle", None, "tensor"),
        P(None, "tensor"),
        P(None, "tensor"),
        P("tensor", None),
        P("particle", "tensor", None, None),
        P("particle"),
    )
    out_specs = P("particle", None, "tensor")
    return jax.shard_map(shards, mesh=mesh, in_specs=in_specs, out_specs=out_specs, check_vma=False)
```

```python
import jax
import jax.numpy as jnp
import numpy as np
from jax import lax
from jax.experimental import pallas as pl
from jax.experimental.pallas import tpu as pltpu
from jax.sharding import PartitionSpec as P

PAIR = 2
THETA = 500000.0
EPSILON = 1e-05
F32 = jnp.float32
BF16 = jnp.bfloat16
MIB = 1 << 20
NT = (((1,), (1,)), ((), ()))


def rotary_tables(context, steps, head_dim):
    half = head_dim // 2
    freqs = np.float32(THETA) ** (-np.arange(half, dtype=np.float32) * np.float32(2.0) / np.float32(head_dim))
    position = (np.float32(context) + np.arange(steps, dtype=np.float32)).reshape(steps, 1)
    angles = (position * freqs.astype(np.float32)).astype(np.float32)
    cosine, sine = np.cos(angles), np.sin(angles)
    return (
        np.concatenate([cosine, cosine], 1).astype(np.float32),
        np.concatenate([-sine, sine], 1).astype(np.float32),
    )


def slot_of(anc, row, rows, count):
    source = lax.div(anc[row], rows)
    rank = count[source]
    count[source] = rank + 1
    return source, rank


def pack_kernel(
    anc_hbm, qp_hbm, tables_hbm, gain_hbm, send, queries, tables, gain, grid_ref, qp, anc, count, spots, sems
):
    pairs = ((anc_hbm, anc), (qp_hbm, qp), (tables_hbm, tables), (gain_hbm, gain))
    copies = [pltpu.make_async_copy(src, dst, sems.at[i]) for i, (src, dst) in enumerate(pairs)]
    for copy in copies:
        copy.start()
    rows, steps, width = qp.shape
    _, per_row, head_dim = tables.shape
    devices = send.shape[0]

    def clear(d, _):
        send[d] = jnp.zeros(send.shape[1:], BF16)
        count[d] = 0
        for j in range(PAIR):
            spots[PAIR * d + j] = 0
        return 0

    lax.fori_loop(0, devices, clear, 0)
    for copy in copies:
        copy.wait()
    for h in range(width // head_dim):
        grid_ref[:, steps * h : steps * (h + 1), :] = qp[:, :, head_dim * h : head_dim * (h + 1)].astype(F32)
    for r in range(rows):
        source, rank = slot_of(anc, r, rows, count)
        spots[source * PAIR + rank] = lax.rem(anc[r], rows)
        plain = grid_ref[r]
        turned = (plain * tables[0] + pltpu.roll(plain, head_dim // 2, 1) * tables[1]).astype(BF16)
        queries[r] = turned
        send[source, rank] = turned
    lane = lax.broadcasted_iota(jnp.int32, (per_row, head_dim), 1)
    for d in range(devices):
        send[d, PAIR] = jnp.where(
            lane < head_dim // 2, spots[PAIR * d].astype(F32), spots[PAIR * d + 1].astype(F32)
        ).astype(BF16)


def attend_kernel(
    recv, kv, x, gain, wk, wv, queries, tables, vectors, tops, sums, vec, stat, *scratch
):
    scores, expos, normed = scratch
    devices, _, per_row, head_dim = recv.shape
    lane = lax.broadcasted_iota(jnp.int32, (per_row, head_dim), 1)
    spots = []
    for d in range(devices):
        spot = recv[d, PAIR].astype(F32)
        for j in range(PAIR):
            spots.append(spot[0, j * (head_dim // PAIR)].astype(jnp.int32))
    for i in range(devices * PAIR):
        scores[i] = lax.dot_general(
            recv[i // PAIR, i % PAIR], kv[spots[i], 0, :, :head_dim], NT, preferred_element_type=F32
        ) * head_dim ** (-0.5)
    for i in range(devices * PAIR):
        top = jnp.max(scores[i], -1, keepdims=True)
        expo = jnp.exp(scores[i] - top)
        expos[i] = expo.astype(BF16)
        tops[i] = jnp.broadcast_to(top, lane.shape)
        sums[i] = jnp.broadcast_to(jnp.sum(expo, -1, keepdims=True), lane.shape)
    for i in range(devices * PAIR):
        vectors[i] = jnp.dot(expos[i], kv[spots[i], 0, :, head_dim:], preferred_element_type=F32)
    rows, steps, width = x.shape
    tokens = rows * steps
    floats = x[...].reshape(tokens, width).astype(F32)
    inverse = lax.rsqrt(jnp.mean(floats * floats, -1, keepdims=True) + EPSILON)
    normed[...] = (floats * inverse * gain[...]).astype(BF16)
    repeat = tokens // per_row
    cosine, sine = (jnp.concatenate([tables[i]] * repeat, 0) for i in range(2))
    keys = jnp.dot(normed[...], wk[...], preferred_element_type=F32)
    keys = (keys * cosine + pltpu.roll(keys, head_dim // 2, 1) * sine).astype(BF16)
    vals = jnp.dot(normed[...], wv[...], preferred_element_type=F32).astype(BF16)
    flat = queries[...].reshape(rows * per_row, head_dim)
    fresh = lax.dot_general(flat, keys, NT, preferred_element_type=F32) * head_dim ** (-0.5)
    row = lax.broadcasted_iota(jnp.int32, fresh.shape, 0)
    col = lax.broadcasted_iota(jnp.int32, fresh.shape, 1)
    seen = (lax.div(row, per_row) == lax.div(col, steps)) & (lax.rem(col, steps) <= lax.rem(row, steps))
    top = jnp.max(jnp.where(seen, fresh, -jnp.inf), -1, keepdims=True)
    expo = jnp.where(seen, jnp.exp(jnp.where(seen, fresh - top, 0.0)), 0.0)
    vec[...] = jnp.dot(expo.astype(BF16), vals, preferred_element_type=F32)
    stat[0] = jnp.broadcast_to(top, stat.shape[1:])
    stat[1] = jnp.broadcast_to(jnp.sum(expo, -1, keepdims=True), stat.shape[1:])


def return_kernel(vectors, tops, sums, back):
    devices, _, per_row, head_dim = back.shape
    lane = lax.broadcasted_iota(jnp.int32, (per_row, head_dim), 1)
    for d in range(devices):
        for j in range(PAIR):
            back[d, j] = (vectors[d * PAIR + j] / sums[d * PAIR + j]).astype(BF16)
        stat = jnp.zeros(lane.shape, F32)
        for j in range(PAIR):
            at_lane = j * (head_dim // PAIR)
            for value, parts in ((tops[d * PAIR + j], 3), (sums[d * PAIR + j], 2)):
                for _ in range(parts):
                    part = value.astype(BF16).astype(F32)
                    stat = jnp.where(lane == at_lane, part, stat)
                    value = value - part
                    at_lane += 1
        back[d, PAIR] = stat.astype(BF16)


def project(heads, w, out, own):
    index = lax.axis_index("tensor")
    first, core = lax.div(index, 2), lax.rem(index, 2)
    core = core if own else 1 - core
    groups, tokens, column = out.shape
    wide = jnp.concatenate([heads[...]] * max(1, 128 // tokens), 0)
    for k in range(groups):
        block = 2 * lax.rem(first + k, groups) + core
        at = pl.multiple_of(block * column, column)
        out[k] = jnp.dot(wide, w[:, pl.ds(at, column)], preferred_element_type=F32)[:tokens].astype(BF16)


def merge_kernel(anc, recv, vec, stat, w, out, heads, grid_ref, sums, lined, count):
    devices, _, per_row, head_dim = recv.shape
    rows = vec.shape[0] // per_row
    steps = heads.shape[0] // rows
    half = head_dim // PAIR
    for d in range(devices):
        count[d] = 0
    lane = lax.broadcasted_iota(jnp.int32, (per_row, head_dim), 1)
    for r in range(rows):
        source, rank = slot_of(anc, r, rows, count)
        grid_ref[pl.ds(r * per_row, per_row), :] = recv[source, rank].astype(F32)
        parts = recv[source, PAIR].astype(F32)
        sums[pl.ds(r * per_row, per_row), :] = jnp.where(lax.div(lane, half) == rank, parts, 0.0).astype(BF16)
    lane_from = lax.rem(lax.broadcasted_iota(jnp.int32, (head_dim, 2 * head_dim), 0), half)
    lane_to = lax.broadcasted_iota(jnp.int32, (head_dim, 2 * head_dim), 1)
    first = jnp.where(lane_from < 3, 1.0, 0.0)
    second = jnp.where((lane_from >= 3) & (lane_from < 5), 1.0, 0.0)
    spread = jnp.where(lane_to < head_dim, first, second)
    both = jnp.dot(sums[...], spread.astype(BF16), preferred_element_type=F32)
    top_c, sum_c = both[:, :head_dim], both[:, head_dim:]
    top_f, sum_f = stat[0], stat[1]
    top = jnp.maximum(top_c, top_f)
    factor_c = sum_c * jnp.exp(top_c - top)
    factor_f = jnp.exp(top_f - top)
    share = 1.0 / (factor_c + sum_f * factor_f)
    grid_ref[...] = (grid_ref[...] * factor_c + vec[...] * factor_f) * share
    for h in range(per_row // steps):
        for s in range(steps):
            lined[h, pl.ds(s, rows, stride=steps), :] = grid_ref[pl.ds(h * steps + s, rows, stride=per_row), :]
        heads[:, pl.ds(h * head_dim, head_dim)] = lined[h].astype(BF16)
    project(heads, w, out, False)


def second_kernel(heads, w, out):
    project(heads, w, out, True)


def shards(inputs, norm_gain, query_proj, w_key, w_value, w_out, kv_cache, ancestors):
    rows, steps, width = inputs.shape
    context = kv_cache.shape[2]
    head_dim = kv_cache.shape[3] // 2
    local = query_proj.shape[2]
    heads = local // head_dim
    per_row = heads * steps
    devices = lax.axis_size("particle")
    tensor = lax.axis_size("tensor")
    column = width // tensor
    cosine, sine = rotary_tables(context, steps, head_dim)
    tables = np.stack([np.tile(cosine, (heads, 1)), np.tile(sine, (heads, 1))])
    smem = pl.BlockSpec(memory_space=pltpu.SMEM)
    vmem = pl.BlockSpec(memory_space=pltpu.VMEM)
    stay = pl.BlockSpec(memory_space=pl.ANY)
    hbm = lambda x: pltpu.with_memory_space_constraint(x, pltpu.HBM)
    tables = jnp.asarray(tables)

    packed = (devices, PAIR + 1, per_row, head_dim)
    send, queries, tables, gain = pl.pallas_call(
        pack_kernel,
        out_shape=(
            jax.ShapeDtypeStruct(packed, BF16),
            jax.ShapeDtypeStruct((rows, per_row, head_dim), BF16),
            jax.ShapeDtypeStruct((2, per_row, head_dim), F32),
            jax.ShapeDtypeStruct((1, width), F32),
        ),
        in_specs=[stay] * 4,
        out_specs=(vmem,) * 4,
        scratch_shapes=[
            pltpu.VMEM((rows, per_row, head_dim), F32),
            pltpu.VMEM((rows, steps, local), BF16),
            pltpu.SMEM((rows,), jnp.int32),
            pltpu.SMEM((devices,), jnp.int32),
            pltpu.SMEM((devices * PAIR,), jnp.int32),
            pltpu.SemaphoreType.DMA((4,)),
        ],
        compiler_params=pltpu.CompilerParams(vmem_limit_bytes=4 * MIB),
        cost_estimate=pl.CostEstimate(flops=10_000_000_000, bytes_accessed=MIB, transcendentals=0),
        name="pack_queries",
    )(hbm(ancestors), hbm(query_proj), hbm(tables), hbm(norm_gain.reshape(1, width)))

    recv = lax.all_to_all(send, "particle", split_axis=0, concat_axis=0, tiled=True)

    slots = devices * PAIR
    partial_result = jax.ShapeDtypeStruct((slots, per_row, head_dim), F32)
    *found, vec, stat = pl.pallas_call(
        attend_kernel,
        out_shape=(partial_result,) * 3
        + (
            jax.ShapeDtypeStruct((rows * per_row, head_dim), F32),
            jax.ShapeDtypeStruct((2, rows * per_row, head_dim), F32),
        ),
        in_specs=[vmem] * 8,
        out_specs=(vmem,) * 5,
        scratch_shapes=[
            pltpu.VMEM((slots, per_row, context), F32),
            pltpu.VMEM((slots, per_row, context), BF16),
            pltpu.VMEM((rows * steps, width), BF16),
        ],
        compiler_params=pltpu.CompilerParams(vmem_limit_bytes=12 * MIB),
        cost_estimate=pl.CostEstimate(
            flops=4 * slots * per_row * context * head_dim, bytes_accessed=5 * MIB, transcendentals=0
        ),
        name="attention",
    )(
        recv,
        kv_cache,
        inputs,
        gain,
        w_key,
        w_value,
        queries,
        tables,
    )
    back = pl.pallas_call(
        return_kernel,
        out_shape=jax.ShapeDtypeStruct(packed, BF16),
        in_specs=[vmem] * 3,
        out_specs=vmem,
        compiler_params=pltpu.CompilerParams(vmem_limit_bytes=2 * MIB),
        cost_estimate=pl.CostEstimate(flops=10_000_000_000, bytes_accessed=MIB, transcendentals=0),
        name="pack_results",
    )(*found)
    home = lax.all_to_all(back, "particle", split_axis=0, concat_axis=0, tiled=True)

    groups = tensor // 2
    block = (groups, rows * steps, column)
    params = pltpu.CompilerParams(vmem_limit_bytes=8 * MIB)
    cost = pl.CostEstimate(
        flops=rows * steps * local * width, bytes_accessed=local * width, transcendentals=0
    )
    other, heads_out = pl.pallas_call(
        merge_kernel,
        out_shape=(
            jax.ShapeDtypeStruct(block, BF16),
            jax.ShapeDtypeStruct((rows * steps, local), BF16),
        ),
        in_specs=[smem, vmem, vmem, vmem, vmem],
        out_specs=(vmem, vmem),
        scratch_shapes=[
            pltpu.VMEM((rows * per_row, head_dim), F32),
            pltpu.VMEM((rows * per_row, head_dim), BF16),
            pltpu.VMEM((heads, rows * steps, head_dim), F32),
            pltpu.SMEM((devices,), jnp.int32),
        ],
        compiler_params=params,
        cost_estimate=cost,
        name="merge_project_sibling",
    )(ancestors, home, vec, stat, w_out)
    given = lax.ppermute(other, "tensor", [(i, i ^ 1) for i in range(tensor)])
    mine = pl.pallas_call(
        second_kernel,
        out_shape=jax.ShapeDtypeStruct(block, BF16),
        in_specs=[vmem, vmem],
        out_specs=vmem,
        compiler_params=params,
        cost_estimate=cost,
        name="project_own",
    )(heads_out, w_out)
    pair = [(mine[k].astype(F32) + given[k].astype(F32)) for k in range(groups)]
    total = pair[0]
    for k in range(1, groups):
        ring = [(i, ((i // 2 + k) % groups) * 2 + i % 2) for i in range(tensor)]
        total = total + lax.ppermute(pair[k].astype(BF16), "tensor", ring).astype(F32)
    return total.astype(BF16).reshape(rows, steps, column)


def solution(mesh):
    in_specs = (
        P("particle", None, None),
        P(),
        P("particle", None, "tensor"),
        P(None, "tensor"),
        P(None, "tensor"),
        P("tensor", None),
        P("particle", "tensor", None, None),
        P("particle"),
    )
    out_specs = P("particle", None, "tensor")
    return jax.shard_map(shards, mesh=mesh, in_specs=in_specs, out_specs=out_specs, check_vma=False)
```

```python
import functools

import jax
import jax.numpy as jnp
import numpy as np
from jax import lax
from jax.experimental import pallas as pl
from jax.experimental.pallas import tpu as pltpu
from jax.sharding import PartitionSpec as P

PAIR = 2
THETA = 500000.0
EPSILON = 1e-05
F32 = jnp.float32
BF16 = jnp.bfloat16
MIB = 1 << 20
NT = (((1,), (1,)), ((), ()))


def rotary_tables(context, steps, head_dim):
    half = head_dim // 2
    freqs = np.float32(THETA) ** (-np.arange(half, dtype=np.float32) * np.float32(2.0) / np.float32(head_dim))
    position = (np.float32(context) + np.arange(steps, dtype=np.float32)).reshape(steps, 1)
    angles = (position * freqs.astype(np.float32)).astype(np.float32)
    cosine, sine = np.cos(angles), np.sin(angles)
    return (
        np.concatenate([cosine, cosine], 1).astype(np.float32),
        np.concatenate([-sine, sine], 1).astype(np.float32),
    )


def slot_of(anc, row, rows, count):
    source = lax.div(anc[row], rows)
    rank = count[source]
    count[source] = rank + 1
    return source, rank


def prepare_kernel(*refs):
    sources, (queries, blocks), scratch = refs[:7], refs[7:9], refs[9:]
    anc, qp, tables, gain, x, wk, wv, grid_ref, normed, fresh, sems = scratch
    targets = (anc, qp, tables, gain, x, wk, wv)
    copies = [pltpu.make_async_copy(src, dst, sems.at[i]) for i, (src, dst) in enumerate(zip(sources, targets))]
    for copy in copies:
        copy.start()
    rows, steps, local = qp.shape
    width = x.shape[2]
    tokens = rows * steps
    _, per_row, head_dim = tables.shape
    for copy in copies[:5]:
        copy.wait()
    for h in range(local // head_dim):
        grid_ref[:, steps * h : steps * (h + 1), :] = qp[:, :, head_dim * h : head_dim * (h + 1)].astype(F32)
    for r in range(rows):
        plain = grid_ref[r]
        queries[r] = (plain * tables[0] + pltpu.roll(plain, head_dim // 2, 1) * tables[1]).astype(BF16)
    floats = x[...].reshape(tokens, width).astype(F32)
    inverse = lax.rsqrt(jnp.mean(floats * floats, -1, keepdims=True) + EPSILON)
    normed[...] = (floats * inverse * gain[...]).astype(BF16)
    repeat = tokens // per_row
    cosine, sine = (jnp.concatenate([tables[i]] * repeat, 0) for i in range(2))
    copies[5].wait()
    keys = jnp.dot(normed[...], wk[...], preferred_element_type=F32)
    fresh[0] = (keys * cosine + pltpu.roll(keys, head_dim // 2, 1) * sine).astype(BF16).astype(F32)
    copies[6].wait()
    fresh[1] = jnp.dot(normed[...], wv[...], preferred_element_type=F32).astype(BF16).astype(F32)
    for r in range(rows):
        blocks[r, 0:steps] = fresh[0, steps * r : steps * (r + 1)]
        blocks[r, steps : 2 * steps] = fresh[1, steps * r : steps * (r + 1)]
        blocks[r, 2 * steps :] = jnp.full(
            (blocks.shape[1] - 2 * steps, head_dim), lax.rem(anc[r], rows).astype(F32), F32
        )


def send_kernel(anc, queries, blocks, send, tiles, count):
    rows = queries.shape[0]
    devices = send.shape[0]
    eight = blocks.shape[1]
    send[...] = jnp.zeros(send.shape, BF16)
    tiles[...] = jnp.zeros(tiles.shape, F32)
    for d in range(devices):
        count[d] = 0
    for r in range(rows):
        source, rank = slot_of(anc, r, rows, count)
        send[source, rank] = queries[r]
        tiles[source, pl.ds(pl.multiple_of(rank * eight, eight), eight), :] = blocks[r]
    for d in range(devices):
        send[d, PAIR] = tiles[d].astype(BF16)


def attend_kernel(recv, kv, heads, scores, expos, tops, sums, vectors, extra, lined):
    devices, _, per_row, head_dim = recv.shape
    slots = devices * PAIR
    steps = heads.shape[0] // slots
    eight = per_row // PAIR
    spots = []
    for d in range(devices):
        tile = recv[d, PAIR].astype(F32)
        extra[pl.ds(d * per_row, per_row), :] = tile
        for j in range(PAIR):
            spots.append(tile[j * eight + 2 * steps, 0].astype(jnp.int32))
    for i in range(slots):
        scores[i] = lax.dot_general(
            recv[i // PAIR, i % PAIR], kv[spots[i], 0, :, :head_dim], NT, preferred_element_type=F32
        ) * head_dim ** (-0.5)
    for i in range(slots):
        top = jnp.max(scores[i], -1, keepdims=True)
        expo = jnp.exp(scores[i] - top)
        expos[i] = expo.astype(BF16)
        at = pl.ds(i * per_row, per_row)
        tops[at, :] = jnp.broadcast_to(top, (per_row, head_dim))
        sums[at, :] = jnp.broadcast_to(jnp.sum(expo, -1, keepdims=True), (per_row, head_dim))
    for i in range(slots):
        vectors[pl.ds(i * per_row, per_row), :] = jnp.dot(
            expos[i], kv[spots[i], 0, :, head_dim:], preferred_element_type=F32
        )
    count = devices * per_row
    extra[count:, :] = jnp.zeros((extra.shape[0] - count, head_dim), F32)
    asked = jnp.concatenate([recv[i // PAIR, i % PAIR] for i in range(slots)], 0)
    fresh = lax.dot_general(
        asked, extra[:count, :].astype(BF16), NT, preferred_element_type=F32
    ) * head_dim ** (-0.5)
    row = lax.broadcasted_iota(jnp.int32, fresh.shape, 0)
    col = lax.broadcasted_iota(jnp.int32, fresh.shape, 1)
    ahead = lax.rem(row, steps) - (col - lax.div(row, per_row) * eight)
    seen = (ahead >= 0) & (ahead <= lax.rem(row, steps))
    top_f = jnp.max(jnp.where(seen, fresh, -jnp.inf), -1, keepdims=True)
    expo = jnp.where(seen, jnp.exp(jnp.where(seen, fresh - top_f, 0.0)), 0.0)
    sum_f = jnp.sum(expo, -1, keepdims=True)
    vec_f = jnp.dot(expo.astype(BF16), extra[steps : count + steps, :].astype(BF16), preferred_element_type=F32)
    top_c = tops[...]
    top = jnp.maximum(top_c, top_f)
    factor_c = jnp.exp(top_c - top)
    factor_f = jnp.exp(top_f - top)
    vectors[...] = (vectors[...] * factor_c + vec_f * factor_f) / (sums[...] * factor_c + sum_f * factor_f)
    for h in range(per_row // steps):
        for s in range(steps):
            lined[h, pl.ds(s, slots, stride=steps), :] = vectors[pl.ds(h * steps + s, slots, stride=per_row), :]
        heads[:, pl.ds(h * head_dim, head_dim)] = lined[h].astype(BF16)


def project_kernel(own, heads, w, out):
    groups, tokens, column = out.shape
    core = lax.rem(lax.axis_index("tensor"), 2)
    core = core if own else 1 - core
    wide = jnp.concatenate([heads[...]] * max(1, 128 // tokens), 0)
    for k in range(groups):
        at = pl.multiple_of((2 * k + core) * column, column)
        out[k] = jnp.dot(wide, w[:, pl.ds(at, column)], preferred_element_type=F32)[:tokens].astype(BF16)


def arrange_kernel(mine, given, out):
    devices, groups, pair, steps, column = out.shape
    for k in range(groups):
        total = mine[k].astype(F32) + given[k].astype(F32)
        out[:, k] = total.reshape(devices, pair, steps, column).astype(BF16)


def collect_kernel(anc, parts, out, count):
    rows = out.shape[0]
    devices = parts.shape[0]
    for d in range(devices):
        count[d] = 0
    for r in range(rows):
        source, rank = slot_of(anc, r, rows, count)
        total = parts[source, 0, rank].astype(F32)
        for k in range(1, parts.shape[1]):
            total = total + parts[source, k, rank].astype(F32)
        out[r] = total.astype(BF16)


def shards(inputs, norm_gain, query_proj, w_key, w_value, w_out, kv_cache, ancestors):
    rows, steps, width = inputs.shape
    context = kv_cache.shape[2]
    head_dim = kv_cache.shape[3] // 2
    local = query_proj.shape[2]
    heads = local // head_dim
    per_row = heads * steps
    devices = lax.axis_size("particle")
    tensor = lax.axis_size("tensor")
    groups = tensor // 2
    column = width // tensor
    slots = devices * PAIR
    eight = per_row // PAIR
    cosine, sine = rotary_tables(context, steps, head_dim)
    tables = jnp.asarray(np.stack([np.tile(cosine, (heads, 1)), np.tile(sine, (heads, 1))]))
    smem = pl.BlockSpec(memory_space=pltpu.SMEM)
    vmem = pl.BlockSpec(memory_space=pltpu.VMEM)
    stay = pl.BlockSpec(memory_space=pl.ANY)
    shape = jax.ShapeDtypeStruct
    packed = (devices, PAIR + 1, per_row, head_dim)

    def call(kernel, out, ins, operands, name, mib, scratch=(), flops=0, moved=MIB):
        return pl.pallas_call(
            kernel,
            out_shape=out,
            in_specs=ins,
            out_specs=jax.tree.map(lambda _: vmem, out),
            scratch_shapes=scratch,
            compiler_params=pltpu.CompilerParams(vmem_limit_bytes=mib * MIB),
            cost_estimate=pl.CostEstimate(flops=flops, bytes_accessed=moved, transcendentals=0),
            name=name,
        )(*operands)

    fetched = [ancestors, query_proj, tables, norm_gain.reshape(1, width), inputs, w_key, w_value]
    queries, blocks = call(
        prepare_kernel,
        (shape((rows, per_row, head_dim), BF16), shape((rows, eight, head_dim), F32)),
        [stay] * 7,
        [pltpu.with_memory_space_constraint(x, pltpu.HBM) for x in fetched],
        "prepare",
        12,
        [pltpu.SMEM(fetched[0].shape, jnp.int32)]
        + [pltpu.VMEM(x.shape, x.dtype) for x in fetched[1:]]
        + [
            pltpu.VMEM((rows, per_row, head_dim), F32),
            pltpu.VMEM((rows * steps, width), BF16),
            pltpu.VMEM((2, rows * steps, head_dim), F32),
            pltpu.SemaphoreType.DMA((7,)),
        ],
    )
    send = call(
        send_kernel,
        shape(packed, BF16),
        [smem, vmem, vmem],
        [ancestors, queries, blocks],
        "pack_queries",
        4,
        [pltpu.VMEM((devices, per_row, head_dim), F32), pltpu.SMEM((devices,), jnp.int32)],
        flops=20_000_000_000,
    )
    recv = lax.all_to_all(send, "particle", split_axis=0, concat_axis=0, tiled=True)
    heads_out = call(
        attend_kernel,
        shape((slots * steps, local), BF16),
        [vmem, vmem],
        [recv, kv_cache],
        "attention",
        12,
        [
            pltpu.VMEM((slots, per_row, context), F32),
            pltpu.VMEM((slots, per_row, context), BF16),
            pltpu.VMEM((slots * per_row, head_dim), F32),
            pltpu.VMEM((slots * per_row, head_dim), F32),
            pltpu.VMEM((slots * per_row, head_dim), F32),
            pltpu.VMEM((devices * per_row + 8, head_dim), F32),
            pltpu.VMEM((heads, slots * steps, head_dim), F32),
        ],
        flops=4 * slots * per_row * context * head_dim,
        moved=5 * MIB,
    )
    block = shape((groups, slots * steps, column), BF16)
    cost = dict(flops=2 * slots * steps * local * width, moved=local * width)
    other, mine = (
        call(functools.partial(project_kernel, own), block, [vmem, vmem], [heads_out, w_out], name, 8, **cost)
        for own, name in ((False, "project_sibling"), (True, "project_own"))
    )
    given = lax.ppermute(other, "tensor", [(i, i ^ 1) for i in range(tensor)])
    parts = call(
        arrange_kernel,
        shape((devices, groups, PAIR, steps, column), BF16),
        [vmem, vmem],
        [mine, given],
        "add_sibling",
        8,
    )
    same_core = [[p * tensor + 2 * y + core for p in range(devices) for y in range(groups)] for core in range(2)]
    parts = lax.all_to_all(
        parts.reshape(devices * groups, PAIR, steps, column),
        ("particle", "tensor"),
        split_axis=0,
        concat_axis=0,
        axis_index_groups=same_core,
        tiled=True,
    ).reshape(devices, groups, PAIR, steps, column)
    return call(
        collect_kernel,
        shape((rows, steps, column), BF16),
        [smem, vmem],
        [ancestors, parts],
        "collect",
        4,
        [pltpu.SMEM((devices,), jnp.int32)],
    )


def solution(mesh):
    in_specs = (
        P("particle", None, None),
        P(),
        P("particle", None, "tensor"),
        P(None, "tensor"),
        P(None, "tensor"),
        P("tensor", None),
        P("particle", "tensor", None, None),
        P("particle"),
    )
    out_specs = P("particle", None, "tensor")
    return jax.shard_map(shards, mesh=mesh, in_specs=in_specs, out_specs=out_specs, check_vma=False)
```

```python
import jax
import jax.numpy as jnp
import numpy as np
from jax import lax
from jax.experimental import pallas as pl
from jax.experimental.pallas import tpu as pltpu
from jax.sharding import PartitionSpec as P

PAIR = 2
THETA = 500000.0
EPSILON = 1e-05
F32 = jnp.float32
BF16 = jnp.bfloat16
MIB = 1 << 20
NT = (((1,), (1,)), ((), ()))


def rotary_tables(context, steps, head_dim):
    half = head_dim // 2
    freqs = np.float32(THETA) ** (-np.arange(half, dtype=np.float32) * np.float32(2.0) / np.float32(head_dim))
    position = (np.float32(context) + np.arange(steps, dtype=np.float32)).reshape(steps, 1)
    angles = (position * freqs.astype(np.float32)).astype(np.float32)
    cosine, sine = np.cos(angles), np.sin(angles)
    return (
        np.concatenate([cosine, cosine], 1).astype(np.float32),
        np.concatenate([-sine, sine], 1).astype(np.float32),
    )


def slot_of(anc, row, rows, count):
    source = lax.div(anc[row], rows)
    rank = count[source]
    count[source] = rank + 1
    return source, rank


def pack_kernel(
    anc_hbm, qp_hbm, tables_hbm, gain_hbm, send, queries, tables, gain, grid_ref, qp, anc, count, spots, sems
):
    pairs = ((anc_hbm, anc), (qp_hbm, qp), (tables_hbm, tables), (gain_hbm, gain))
    copies = [pltpu.make_async_copy(src, dst, sems.at[i]) for i, (src, dst) in enumerate(pairs)]
    for copy in copies:
        copy.start()
    rows, steps, width = qp.shape
    _, per_row, head_dim = tables.shape
    devices = send.shape[0]

    def clear(d, _):
        send[d] = jnp.zeros(send.shape[1:], BF16)
        count[d] = 0
        for j in range(PAIR):
            spots[PAIR * d + j] = 0
        return 0

    lax.fori_loop(0, devices, clear, 0)
    for copy in copies:
        copy.wait()
    for h in range(width // head_dim):
        grid_ref[:, steps * h : steps * (h + 1), :] = qp[:, :, head_dim * h : head_dim * (h + 1)].astype(F32)
    for r in range(rows):
        source, rank = slot_of(anc, r, rows, count)
        spots[source * PAIR + rank] = lax.rem(anc[r], rows)
        plain = grid_ref[r]
        turned = (plain * tables[0] + pltpu.roll(plain, head_dim // 2, 1) * tables[1]).astype(BF16)
        queries[r] = turned
        send[source, rank] = turned
    lane = lax.broadcasted_iota(jnp.int32, (per_row, head_dim), 1)
    for d in range(devices):
        send[d, PAIR] = jnp.where(
            lane < head_dim // 2, spots[PAIR * d].astype(F32), spots[PAIR * d + 1].astype(F32)
        ).astype(BF16)


def attend_kernel(
    recv, kv, x, gain, wk, wv, queries, tables, vectors, tops, sums, vec, stat, *scratch
):
    scores, expos, normed = scratch
    devices, _, per_row, head_dim = recv.shape
    lane = lax.broadcasted_iota(jnp.int32, (per_row, head_dim), 1)
    spots = []
    for d in range(devices):
        spot = recv[d, PAIR].astype(F32)
        for j in range(PAIR):
            spots.append(spot[0, j * (head_dim // PAIR)].astype(jnp.int32))
    for i in range(devices * PAIR):
        scores[i] = lax.dot_general(
            recv[i // PAIR, i % PAIR], kv[spots[i], 0, :, :head_dim], NT, preferred_element_type=F32
        ) * head_dim ** (-0.5)
    for i in range(devices * PAIR):
        top = jnp.max(scores[i], -1, keepdims=True)
        expo = jnp.exp(scores[i] - top)
        expos[i] = expo.astype(BF16)
        tops[i] = jnp.broadcast_to(top, lane.shape)
        sums[i] = jnp.broadcast_to(jnp.sum(expo, -1, keepdims=True), lane.shape)
    for i in range(devices * PAIR):
        vectors[i] = jnp.dot(expos[i], kv[spots[i], 0, :, head_dim:], preferred_element_type=F32)
    rows, steps, width = x.shape
    tokens = rows * steps
    floats = x[...].reshape(tokens, width).astype(F32)
    inverse = lax.rsqrt(jnp.mean(floats * floats, -1, keepdims=True) + EPSILON)
    normed[...] = (floats * inverse * gain[...]).astype(BF16)
    repeat = tokens // per_row
    cosine, sine = (jnp.concatenate([tables[i]] * repeat, 0) for i in range(2))
    keys = jnp.dot(normed[...], wk[...], preferred_element_type=F32)
    keys = (keys * cosine + pltpu.roll(keys, head_dim // 2, 1) * sine).astype(BF16)
    vals = jnp.dot(normed[...], wv[...], preferred_element_type=F32).astype(BF16)
    flat = queries[...].reshape(rows * per_row, head_dim)
    fresh = lax.dot_general(flat, keys, NT, preferred_element_type=F32) * head_dim ** (-0.5)
    row = lax.broadcasted_iota(jnp.int32, fresh.shape, 0)
    col = lax.broadcasted_iota(jnp.int32, fresh.shape, 1)
    seen = (lax.div(row, per_row) == lax.div(col, steps)) & (lax.rem(col, steps) <= lax.rem(row, steps))
    top = jnp.max(jnp.where(seen, fresh, -jnp.inf), -1, keepdims=True)
    expo = jnp.where(seen, jnp.exp(jnp.where(seen, fresh - top, 0.0)), 0.0)
    vec[...] = jnp.dot(expo.astype(BF16), vals, preferred_element_type=F32)
    stat[0] = jnp.broadcast_to(top, stat.shape[1:])
    stat[1] = jnp.broadcast_to(jnp.sum(expo, -1, keepdims=True), stat.shape[1:])


def return_kernel(vectors, tops, sums, back):
    devices, _, per_row, head_dim = back.shape
    lane = lax.broadcasted_iota(jnp.int32, (per_row, head_dim), 1)
    for d in range(devices):
        for j in range(PAIR):
            back[d, j] = (vectors[d * PAIR + j] / sums[d * PAIR + j]).astype(BF16)
        stat = jnp.zeros(lane.shape, F32)
        for j in range(PAIR):
            at_lane = j * (head_dim // PAIR)
            for value, parts in ((tops[d * PAIR + j], 3), (sums[d * PAIR + j], 2)):
                for _ in range(parts):
                    part = value.astype(BF16).astype(F32)
                    stat = jnp.where(lane == at_lane, part, stat)
                    value = value - part
                    at_lane += 1
        back[d, PAIR] = stat.astype(BF16)


def units(own, groups):
    index = lax.axis_index("tensor")
    y, core = lax.div(index, 2), lax.rem(index, 2)
    core = core if own else 1 - core
    near = lax.rem(y + 1 + (groups - 2) * core, groups)
    far = lax.rem(y + 2, groups)
    return 2 * near + core, 2 * near + 1 - core, 2 * far + core, 2 * y + core


def project(heads, w, out, blocks):
    tokens, column = out.shape[-2:]
    wide = jnp.concatenate([heads[...]] * max(1, 128 // tokens), 0)
    for k, block in enumerate(blocks):
        at = pl.multiple_of(block * column, column)
        out[k] = jnp.dot(wide, w[:, pl.ds(at, column)], preferred_element_type=F32)[:tokens].astype(BF16)


def merge_kernel(anc, recv, vec, stat, w, out, heads, grid_ref, sums, lined, count):
    devices, _, per_row, head_dim = recv.shape
    rows = vec.shape[0] // per_row
    steps = heads.shape[0] // rows
    half = head_dim // PAIR
    for d in range(devices):
        count[d] = 0
    lane = lax.broadcasted_iota(jnp.int32, (per_row, head_dim), 1)
    for r in range(rows):
        source, rank = slot_of(anc, r, rows, count)
        grid_ref[pl.ds(r * per_row, per_row), :] = recv[source, rank].astype(F32)
        parts = recv[source, PAIR].astype(F32)
        sums[pl.ds(r * per_row, per_row), :] = jnp.where(lax.div(lane, half) == rank, parts, 0.0).astype(BF16)
    lane_from = lax.rem(lax.broadcasted_iota(jnp.int32, (head_dim, 2 * head_dim), 0), half)
    lane_to = lax.broadcasted_iota(jnp.int32, (head_dim, 2 * head_dim), 1)
    first = jnp.where(lane_from < 3, 1.0, 0.0)
    second = jnp.where((lane_from >= 3) & (lane_from < 5), 1.0, 0.0)
    spread = jnp.where(lane_to < head_dim, first, second)
    both = jnp.dot(sums[...], spread.astype(BF16), preferred_element_type=F32)
    top_c, sum_c = both[:, :head_dim], both[:, head_dim:]
    top_f, sum_f = stat[0], stat[1]
    top = jnp.maximum(top_c, top_f)
    factor_c = sum_c * jnp.exp(top_c - top)
    factor_f = jnp.exp(top_f - top)
    share = 1.0 / (factor_c + sum_f * factor_f)
    grid_ref[...] = (grid_ref[...] * factor_c + vec[...] * factor_f) * share
    for h in range(per_row // steps):
        for s in range(steps):
            lined[h, pl.ds(s, rows, stride=steps), :] = grid_ref[pl.ds(h * steps + s, rows, stride=per_row), :]
        heads[:, pl.ds(h * head_dim, head_dim)] = lined[h].astype(BF16)
    project(heads, w, out, units(False, w.shape[1] // out.shape[-1] // 2)[:3])


def second_kernel(heads, w, out):
    project(heads, w, out, units(True, w.shape[1] // out.shape[-1] // 2)[:3])


def add_kernel(mine, given, near, far):
    near[...] = (mine[:2].astype(F32) + given[:2].astype(F32)).astype(BF16)
    far[...] = (mine[2].astype(F32) + given[2].astype(F32)).astype(BF16)


def last_kernel(heads, w, out):
    groups = w.shape[1] // out.shape[-1] // 2
    project(heads, w, out, (units(True, groups)[3], units(False, groups)[3]))


def shards(inputs, norm_gain, query_proj, w_key, w_value, w_out, kv_cache, ancestors):
    rows, steps, width = inputs.shape
    context = kv_cache.shape[2]
    head_dim = kv_cache.shape[3] // 2
    local = query_proj.shape[2]
    heads = local // head_dim
    per_row = heads * steps
    devices = lax.axis_size("particle")
    tensor = lax.axis_size("tensor")
    column = width // tensor
    cosine, sine = rotary_tables(context, steps, head_dim)
    tables = np.stack([np.tile(cosine, (heads, 1)), np.tile(sine, (heads, 1))])
    smem = pl.BlockSpec(memory_space=pltpu.SMEM)
    vmem = pl.BlockSpec(memory_space=pltpu.VMEM)
    stay = pl.BlockSpec(memory_space=pl.ANY)
    hbm = lambda x: pltpu.with_memory_space_constraint(x, pltpu.HBM)
    tables = jnp.asarray(tables)

    packed = (devices, PAIR + 1, per_row, head_dim)
    send, queries, tables, gain = pl.pallas_call(
        pack_kernel,
        out_shape=(
            jax.ShapeDtypeStruct(packed, BF16),
            jax.ShapeDtypeStruct((rows, per_row, head_dim), BF16),
            jax.ShapeDtypeStruct((2, per_row, head_dim), F32),
            jax.ShapeDtypeStruct((1, width), F32),
        ),
        in_specs=[stay] * 4,
        out_specs=(vmem,) * 4,
        scratch_shapes=[
            pltpu.VMEM((rows, per_row, head_dim), F32),
            pltpu.VMEM((rows, steps, local), BF16),
            pltpu.SMEM((rows,), jnp.int32),
            pltpu.SMEM((devices,), jnp.int32),
            pltpu.SMEM((devices * PAIR,), jnp.int32),
            pltpu.SemaphoreType.DMA((4,)),
        ],
        compiler_params=pltpu.CompilerParams(vmem_limit_bytes=4 * MIB),
        cost_estimate=pl.CostEstimate(flops=10_000_000_000, bytes_accessed=MIB, transcendentals=0),
        name="pack_queries",
    )(hbm(ancestors), hbm(query_proj), hbm(tables), hbm(norm_gain.reshape(1, width)))

    recv = lax.all_to_all(send, "particle", split_axis=0, concat_axis=0, tiled=True)

    slots = devices * PAIR
    partial_result = jax.ShapeDtypeStruct((slots, per_row, head_dim), F32)
    *found, vec, stat = pl.pallas_call(
        attend_kernel,
        out_shape=(partial_result,) * 3
        + (
            jax.ShapeDtypeStruct((rows * per_row, head_dim), F32),
            jax.ShapeDtypeStruct((2, rows * per_row, head_dim), F32),
        ),
        in_specs=[vmem] * 8,
        out_specs=(vmem,) * 5,
        scratch_shapes=[
            pltpu.VMEM((slots, per_row, context), F32),
            pltpu.VMEM((slots, per_row, context), BF16),
            pltpu.VMEM((rows * steps, width), BF16),
        ],
        compiler_params=pltpu.CompilerParams(vmem_limit_bytes=12 * MIB),
        cost_estimate=pl.CostEstimate(
            flops=4 * slots * per_row * context * head_dim, bytes_accessed=5 * MIB, transcendentals=0
        ),
        name="attention",
    )(
        recv,
        kv_cache,
        inputs,
        gain,
        w_key,
        w_value,
        queries,
        tables,
    )
    back = pl.pallas_call(
        return_kernel,
        out_shape=jax.ShapeDtypeStruct(packed, BF16),
        in_specs=[vmem] * 3,
        out_specs=vmem,
        compiler_params=pltpu.CompilerParams(vmem_limit_bytes=2 * MIB),
        cost_estimate=pl.CostEstimate(flops=10_000_000_000, bytes_accessed=MIB, transcendentals=0),
        name="pack_results",
    )(*found)
    home = lax.all_to_all(back, "particle", split_axis=0, concat_axis=0, tiled=True)

    groups = tensor // 2
    block = jax.ShapeDtypeStruct((3, rows * steps, column), BF16)
    params = pltpu.CompilerParams(vmem_limit_bytes=8 * MIB)
    cost = pl.CostEstimate(
        flops=rows * steps * local * width, bytes_accessed=local * width, transcendentals=0
    )
    other, heads_out = pl.pallas_call(
        merge_kernel,
        out_shape=(
            block,
            jax.ShapeDtypeStruct((rows * steps, local), BF16),
        ),
        in_specs=[smem, vmem, vmem, vmem, vmem],
        out_specs=(vmem, vmem),
        scratch_shapes=[
            pltpu.VMEM((rows * per_row, head_dim), F32),
            pltpu.VMEM((rows * per_row, head_dim), BF16),
            pltpu.VMEM((heads, rows * steps, head_dim), F32),
            pltpu.SMEM((devices,), jnp.int32),
        ],
        compiler_params=params,
        cost_estimate=cost,
        name="merge_project_sibling",
    )(ancestors, home, vec, stat, w_out)
    sibling = [(i, i ^ 1) for i in range(tensor)]
    given = lax.ppermute(other, "tensor", sibling)
    mine = pl.pallas_call(
        second_kernel,
        out_shape=block,
        in_specs=[vmem, vmem],
        out_specs=vmem,
        compiler_params=params,
        cost_estimate=cost,
        name="project_own",
    )(heads_out, w_out)
    near, far = pl.pallas_call(
        add_kernel,
        out_shape=(
            jax.ShapeDtypeStruct((2, rows * steps, column), BF16),
            jax.ShapeDtypeStruct((rows * steps, column), BF16),
        ),
        in_specs=[vmem, vmem],
        out_specs=(vmem, vmem),
        compiler_params=params,
        name="add_sibling",
    )(mine, given)
    ring = [(i, 2 * ((i // 2 + (1 if i % 2 == 0 else groups - 1)) % groups) + i % 2) for i in range(tensor)]
    across = [(i, 2 * ((i // 2 + 2) % groups) + i % 2) for i in range(tensor)]
    from_near = lax.ppermute(near, "tensor", ring)
    from_far = lax.ppermute(far, "tensor", across)
    last = pl.pallas_call(
        last_kernel,
        out_shape=jax.ShapeDtypeStruct((2, rows * steps, column), BF16),
        in_specs=[vmem, vmem],
        out_specs=vmem,
        compiler_params=params,
        cost_estimate=cost,
        name="project_last",
    )(heads_out, w_out)
    crossing = (from_near[1].astype(F32) + last[1].astype(F32)).astype(BF16)
    crossed = lax.ppermute(crossing, "tensor", sibling)
    total = last[0].astype(F32) + from_near[0].astype(F32) + from_far.astype(F32) + crossed.astype(F32)
    return total.astype(BF16).reshape(rows, steps, column)


def solution(mesh):
    in_specs = (
        P("particle", None, None),
        P(),
        P("particle", None, "tensor"),
        P(None, "tensor"),
        P(None, "tensor"),
        P("tensor", None),
        P("particle", "tensor", None, None),
        P("particle"),
    )
    out_specs = P("particle", None, "tensor")
    return jax.shard_map(shards, mesh=mesh, in_specs=in_specs, out_specs=out_specs, check_vma=False)
```

```python
import jax
import jax.numpy as jnp
import numpy as np
from jax import lax
from jax.experimental import pallas as pl
from jax.experimental.pallas import tpu as pltpu
from jax.sharding import PartitionSpec as P

PAIR = 2
THETA = 500000.0
EPSILON = 1e-05
F32 = jnp.float32
BF16 = jnp.bfloat16
MIB = 1 << 20
NT = (((1,), (1,)), ((), ()))


def rotary_tables(context, steps, head_dim):
    half = head_dim // 2
    freqs = np.float32(THETA) ** (-np.arange(half, dtype=np.float32) * np.float32(2.0) / np.float32(head_dim))
    position = (np.float32(context) + np.arange(steps, dtype=np.float32)).reshape(steps, 1)
    angles = (position * freqs.astype(np.float32)).astype(np.float32)
    cosine, sine = np.cos(angles), np.sin(angles)
    return (
        np.concatenate([cosine, cosine], 1).astype(np.float32),
        np.concatenate([-sine, sine], 1).astype(np.float32),
    )


def slot_of(anc, row, rows, count):
    source = lax.div(anc[row], rows)
    rank = count[source]
    count[source] = rank + 1
    return source, rank


def pack_kernel(
    anc_hbm, qp_hbm, tables_hbm, gain_hbm, send, queries, tables, gain, grid_ref, qp, anc, count, spots, sems
):
    pairs = ((anc_hbm, anc), (qp_hbm, qp), (tables_hbm, tables), (gain_hbm, gain))
    copies = [pltpu.make_async_copy(src, dst, sems.at[i]) for i, (src, dst) in enumerate(pairs)]
    for copy in copies:
        copy.start()
    rows, steps, width = qp.shape
    _, per_row, head_dim = tables.shape
    devices = send.shape[0]

    def clear(d, _):
        send[d] = jnp.zeros(send.shape[1:], BF16)
        count[d] = 0
        for j in range(PAIR):
            spots[PAIR * d + j] = 0
        return 0

    lax.fori_loop(0, devices, clear, 0)
    for copy in copies:
        copy.wait()
    for h in range(width // head_dim):
        grid_ref[:, steps * h : steps * (h + 1), :] = qp[:, :, head_dim * h : head_dim * (h + 1)].astype(F32)
    for r in range(rows):
        source, rank = slot_of(anc, r, rows, count)
        spots[source * PAIR + rank] = lax.rem(anc[r], rows)
        plain = grid_ref[r]
        turned = (plain * tables[0] + pltpu.roll(plain, head_dim // 2, 1) * tables[1]).astype(BF16)
        queries[r] = turned
        send[source, rank] = turned
    lane = lax.broadcasted_iota(jnp.int32, (per_row, head_dim), 1)
    for d in range(devices):
        send[d, PAIR] = jnp.where(
            lane < head_dim // 2, spots[PAIR * d].astype(F32), spots[PAIR * d + 1].astype(F32)
        ).astype(BF16)


def attend_kernel(
    recv, kv, x, gain, wk, wv, queries, tables, vectors, tops, sums, vec, stat, *scratch
):
    scores, expos, normed = scratch
    devices, _, per_row, head_dim = recv.shape
    lane = lax.broadcasted_iota(jnp.int32, (per_row, head_dim), 1)
    spots = []
    for d in range(devices):
        spot = recv[d, PAIR].astype(F32)
        for j in range(PAIR):
            spots.append(spot[0, j * (head_dim // PAIR)].astype(jnp.int32))
    for i in range(devices * PAIR):
        scores[i] = lax.dot_general(
            recv[i // PAIR, i % PAIR], kv[spots[i], 0, :, :head_dim], NT, preferred_element_type=F32
        ) * head_dim ** (-0.5)
    for i in range(devices * PAIR):
        top = jnp.max(scores[i], -1, keepdims=True)
        expo = jnp.exp(scores[i] - top)
        expos[i] = expo.astype(BF16)
        tops[i] = jnp.broadcast_to(top, lane.shape)
        sums[i] = jnp.broadcast_to(jnp.sum(expo, -1, keepdims=True), lane.shape)
    for i in range(devices * PAIR):
        vectors[i] = jnp.dot(expos[i], kv[spots[i], 0, :, head_dim:], preferred_element_type=F32)
    rows, steps, width = x.shape
    tokens = rows * steps
    floats = x[...].reshape(tokens, width).astype(F32)
    inverse = lax.rsqrt(jnp.mean(floats * floats, -1, keepdims=True) + EPSILON)
    normed[...] = (floats * inverse * gain[...]).astype(BF16)
    repeat = tokens // per_row
    cosine, sine = (jnp.concatenate([tables[i]] * repeat, 0) for i in range(2))
    keys = jnp.dot(normed[...], wk[...], preferred_element_type=F32)
    keys = (keys * cosine + pltpu.roll(keys, head_dim // 2, 1) * sine).astype(BF16)
    vals = jnp.dot(normed[...], wv[...], preferred_element_type=F32).astype(BF16)
    flat = queries[...].reshape(rows * per_row, head_dim)
    fresh = lax.dot_general(flat, keys, NT, preferred_element_type=F32) * head_dim ** (-0.5)
    row = lax.broadcasted_iota(jnp.int32, fresh.shape, 0)
    col = lax.broadcasted_iota(jnp.int32, fresh.shape, 1)
    seen = (lax.div(row, per_row) == lax.div(col, steps)) & (lax.rem(col, steps) <= lax.rem(row, steps))
    top = jnp.max(jnp.where(seen, fresh, -jnp.inf), -1, keepdims=True)
    expo = jnp.where(seen, jnp.exp(jnp.where(seen, fresh - top, 0.0)), 0.0)
    vec[...] = jnp.dot(expo.astype(BF16), vals, preferred_element_type=F32)
    stat[0] = jnp.broadcast_to(top, stat.shape[1:])
    stat[1] = jnp.broadcast_to(jnp.sum(expo, -1, keepdims=True), stat.shape[1:])


def return_kernel(vectors, tops, sums, back):
    devices, _, per_row, head_dim = back.shape
    lane = lax.broadcasted_iota(jnp.int32, (per_row, head_dim), 1)
    for d in range(devices):
        for j in range(PAIR):
            back[d, j] = (vectors[d * PAIR + j] / sums[d * PAIR + j]).astype(BF16)
        stat = jnp.zeros(lane.shape, F32)
        for j in range(PAIR):
            at_lane = j * (head_dim // PAIR)
            for value, parts in ((tops[d * PAIR + j], 3), (sums[d * PAIR + j], 2)):
                for _ in range(parts):
                    part = value.astype(BF16).astype(F32)
                    stat = jnp.where(lane == at_lane, part, stat)
                    value = value - part
                    at_lane += 1
        back[d, PAIR] = stat.astype(BF16)


def units(own, groups):
    index = lax.axis_index("tensor")
    y, core = lax.div(index, 2), lax.rem(index, 2)
    core = core if own else 1 - core
    near = lax.rem(y + 1 + (groups - 2) * core, groups)
    far = lax.rem(y + 2, groups)
    return 2 * near + core, 2 * near + 1 - core, 2 * far + core, 2 * y + core


def project(heads, w, out, blocks):
    tokens, column = out.shape[-2:]
    wide = jnp.concatenate([heads[...]] * max(1, 128 // tokens), 0)
    for k, block in enumerate(blocks):
        at = pl.multiple_of(block * column, column)
        out[k] = jnp.dot(wide, w[:, pl.ds(at, column)], preferred_element_type=F32)[:tokens].astype(BF16)


def merge_kernel(anc, recv, vec, stat, w, out, heads, grid_ref, sums, lined, count):
    devices, _, per_row, head_dim = recv.shape
    rows = vec.shape[0] // per_row
    steps = heads.shape[0] // rows
    half = head_dim // PAIR
    for d in range(devices):
        count[d] = 0
    lane = lax.broadcasted_iota(jnp.int32, (per_row, head_dim), 1)
    for r in range(rows):
        source, rank = slot_of(anc, r, rows, count)
        grid_ref[pl.ds(r * per_row, per_row), :] = recv[source, rank].astype(F32)
        parts = recv[source, PAIR].astype(F32)
        sums[pl.ds(r * per_row, per_row), :] = jnp.where(lax.div(lane, half) == rank, parts, 0.0).astype(BF16)
    lane_from = lax.rem(lax.broadcasted_iota(jnp.int32, (head_dim, 2 * head_dim), 0), half)
    lane_to = lax.broadcasted_iota(jnp.int32, (head_dim, 2 * head_dim), 1)
    first = jnp.where(lane_from < 3, 1.0, 0.0)
    second = jnp.where((lane_from >= 3) & (lane_from < 5), 1.0, 0.0)
    spread = jnp.where(lane_to < head_dim, first, second)
    both = jnp.dot(sums[...], spread.astype(BF16), preferred_element_type=F32)
    top_c, sum_c = both[:, :head_dim], both[:, head_dim:]
    top_f, sum_f = stat[0], stat[1]
    top = jnp.maximum(top_c, top_f)
    factor_c = sum_c * jnp.exp(top_c - top)
    factor_f = jnp.exp(top_f - top)
    share = 1.0 / (factor_c + sum_f * factor_f)
    grid_ref[...] = (grid_ref[...] * factor_c + vec[...] * factor_f) * share
    for h in range(per_row // steps):
        for s in range(steps):
            lined[h, pl.ds(s, rows, stride=steps), :] = grid_ref[pl.ds(h * steps + s, rows, stride=per_row), :]
        heads[:, pl.ds(h * head_dim, head_dim)] = lined[h].astype(BF16)
    project(heads, w, out, units(False, w.shape[1] // out.shape[-1] // 2)[:3])


def second_kernel(heads, w, out):
    project(heads, w, out, units(True, w.shape[1] // out.shape[-1] // 2)[:3])


def add_kernel(mine, given, near, far):
    near[...] = (mine[:2].astype(F32) + given[:2].astype(F32)).astype(BF16)
    far[...] = (mine[2].astype(F32) + given[2].astype(F32)).astype(BF16)


def last_kernel(heads, w, arrived, keep, crossing):
    tokens, column = keep.shape
    mine, given = units(True, w.shape[1] // column // 2)[3], units(False, w.shape[1] // column // 2)[3]
    wide = jnp.concatenate([heads[...]] * max(1, 128 // tokens), 0)
    for k, (out, block) in enumerate(((keep, mine), (crossing, given))):
        at = pl.multiple_of(block * column, column)
        product = jnp.dot(wide, w[:, pl.ds(at, column)], preferred_element_type=F32)[:tokens]
        out[...] = (product + arrived[k].astype(F32)).astype(out.dtype)


def shards(inputs, norm_gain, query_proj, w_key, w_value, w_out, kv_cache, ancestors):
    rows, steps, width = inputs.shape
    context = kv_cache.shape[2]
    head_dim = kv_cache.shape[3] // 2
    local = query_proj.shape[2]
    heads = local // head_dim
    per_row = heads * steps
    devices = lax.axis_size("particle")
    tensor = lax.axis_size("tensor")
    column = width // tensor
    cosine, sine = rotary_tables(context, steps, head_dim)
    tables = np.stack([np.tile(cosine, (heads, 1)), np.tile(sine, (heads, 1))])
    smem = pl.BlockSpec(memory_space=pltpu.SMEM)
    vmem = pl.BlockSpec(memory_space=pltpu.VMEM)
    stay = pl.BlockSpec(memory_space=pl.ANY)
    hbm = lambda x: pltpu.with_memory_space_constraint(x, pltpu.HBM)
    tables = jnp.asarray(tables)

    packed = (devices, PAIR + 1, per_row, head_dim)
    send, queries, tables, gain = pl.pallas_call(
        pack_kernel,
        out_shape=(
            jax.ShapeDtypeStruct(packed, BF16),
            jax.ShapeDtypeStruct((rows, per_row, head_dim), BF16),
            jax.ShapeDtypeStruct((2, per_row, head_dim), F32),
            jax.ShapeDtypeStruct((1, width), F32),
        ),
        in_specs=[stay] * 4,
        out_specs=(vmem,) * 4,
        scratch_shapes=[
            pltpu.VMEM((rows, per_row, head_dim), F32),
            pltpu.VMEM((rows, steps, local), BF16),
            pltpu.SMEM((rows,), jnp.int32),
            pltpu.SMEM((devices,), jnp.int32),
            pltpu.SMEM((devices * PAIR,), jnp.int32),
            pltpu.SemaphoreType.DMA((4,)),
        ],
        compiler_params=pltpu.CompilerParams(vmem_limit_bytes=4 * MIB),
        cost_estimate=pl.CostEstimate(flops=10_000_000_000, bytes_accessed=MIB, transcendentals=0),
        name="pack_queries",
    )(hbm(ancestors), hbm(query_proj), hbm(tables), hbm(norm_gain.reshape(1, width)))

    recv = lax.all_to_all(send, "particle", split_axis=0, concat_axis=0, tiled=True)

    slots = devices * PAIR
    partial_result = jax.ShapeDtypeStruct((slots, per_row, head_dim), F32)
    *found, vec, stat = pl.pallas_call(
        attend_kernel,
        out_shape=(partial_result,) * 3
        + (
            jax.ShapeDtypeStruct((rows * per_row, head_dim), F32),
            jax.ShapeDtypeStruct((2, rows * per_row, head_dim), F32),
        ),
        in_specs=[vmem] * 8,
        out_specs=(vmem,) * 5,
        scratch_shapes=[
            pltpu.VMEM((slots, per_row, context), F32),
            pltpu.VMEM((slots, per_row, context), BF16),
            pltpu.VMEM((rows * steps, width), BF16),
        ],
        compiler_params=pltpu.CompilerParams(vmem_limit_bytes=12 * MIB),
        cost_estimate=pl.CostEstimate(
            flops=4 * slots * per_row * context * head_dim, bytes_accessed=5 * MIB, transcendentals=0
        ),
        name="attention",
    )(
        recv,
        kv_cache,
        inputs,
        gain,
        w_key,
        w_value,
        queries,
        tables,
    )
    back = pl.pallas_call(
        return_kernel,
        out_shape=jax.ShapeDtypeStruct(packed, BF16),
        in_specs=[vmem] * 3,
        out_specs=vmem,
        compiler_params=pltpu.CompilerParams(vmem_limit_bytes=2 * MIB),
        cost_estimate=pl.CostEstimate(flops=10_000_000_000, bytes_accessed=MIB, transcendentals=0),
        name="pack_results",
    )(*found)
    home = lax.all_to_all(back, "particle", split_axis=0, concat_axis=0, tiled=True)

    groups = tensor // 2
    block = jax.ShapeDtypeStruct((3, rows * steps, column), BF16)
    params = pltpu.CompilerParams(vmem_limit_bytes=8 * MIB)
    cost = pl.CostEstimate(
        flops=rows * steps * local * width, bytes_accessed=local * width, transcendentals=0
    )
    other, heads_out = pl.pallas_call(
        merge_kernel,
        out_shape=(
            block,
            jax.ShapeDtypeStruct((rows * steps, local), BF16),
        ),
        in_specs=[smem, vmem, vmem, vmem, vmem],
        out_specs=(vmem, vmem),
        scratch_shapes=[
            pltpu.VMEM((rows * per_row, head_dim), F32),
            pltpu.VMEM((rows * per_row, head_dim), BF16),
            pltpu.VMEM((heads, rows * steps, head_dim), F32),
            pltpu.SMEM((devices,), jnp.int32),
        ],
        compiler_params=params,
        cost_estimate=cost,
        name="merge_project_sibling",
    )(ancestors, home, vec, stat, w_out)
    sibling = [(i, i ^ 1) for i in range(tensor)]
    given = lax.ppermute(other, "tensor", sibling)
    mine = pl.pallas_call(
        second_kernel,
        out_shape=block,
        in_specs=[vmem, vmem],
        out_specs=vmem,
        compiler_params=params,
        cost_estimate=cost,
        name="project_own",
    )(heads_out, w_out)
    near, far = pl.pallas_call(
        add_kernel,
        out_shape=(
            jax.ShapeDtypeStruct((2, rows * steps, column), BF16),
            jax.ShapeDtypeStruct((rows * steps, column), BF16),
        ),
        in_specs=[vmem, vmem],
        out_specs=(vmem, vmem),
        compiler_params=params,
        name="add_sibling",
    )(mine, given)
    ring = [(i, 2 * ((i // 2 + (1 if i % 2 == 0 else groups - 1)) % groups) + i % 2) for i in range(tensor)]
    across = [(i, 2 * ((i // 2 + 2) % groups) + i % 2) for i in range(tensor)]
    from_near = lax.ppermute(near, "tensor", ring)
    from_far = lax.ppermute(far, "tensor", across)
    keep, crossing = pl.pallas_call(
        last_kernel,
        out_shape=(
            jax.ShapeDtypeStruct((rows * steps, column), F32),
            jax.ShapeDtypeStruct((rows * steps, column), BF16),
        ),
        in_specs=[vmem, vmem, vmem],
        out_specs=(vmem, vmem),
        compiler_params=params,
        cost_estimate=cost,
        name="project_last",
    )(heads_out, w_out, from_near)
    crossed = lax.ppermute(crossing, "tensor", sibling)
    total = keep + from_far.astype(F32) + crossed.astype(F32)
    return total.astype(BF16).reshape(rows, steps, column)


def solution(mesh):
    in_specs = (
        P("particle", None, None),
        P(),
        P("particle", None, "tensor"),
        P(None, "tensor"),
        P(None, "tensor"),
        P("tensor", None),
        P("particle", "tensor", None, None),
        P("particle"),
    )
    out_specs = P("particle", None, "tensor")
    return jax.shard_map(shards, mesh=mesh, in_specs=in_specs, out_specs=out_specs, check_vma=False)
```

```python
import jax
import jax.numpy as jnp
import numpy as np
from jax import lax
from jax.experimental import pallas as pl
from jax.experimental.pallas import tpu as pltpu
from jax.sharding import PartitionSpec as P

PAIR = 2
THETA = 500000.0
EPSILON = 1e-05
F32 = jnp.float32
BF16 = jnp.bfloat16
MIB = 1 << 20
NT = (((1,), (1,)), ((), ()))


def rotary_tables(context, steps, head_dim):
    half = head_dim // 2
    freqs = np.float32(THETA) ** (-np.arange(half, dtype=np.float32) * np.float32(2.0) / np.float32(head_dim))
    position = (np.float32(context) + np.arange(steps, dtype=np.float32)).reshape(steps, 1)
    angles = (position * freqs.astype(np.float32)).astype(np.float32)
    cosine, sine = np.cos(angles), np.sin(angles)
    return (
        np.concatenate([cosine, cosine], 1).astype(np.float32),
        np.concatenate([-sine, sine], 1).astype(np.float32),
    )


def slot_of(anc, row, rows, count):
    source = lax.div(anc[row], rows)
    rank = count[source]
    count[source] = rank + 1
    return source, rank


def pack_kernel(
    anc_hbm, qp_hbm, tables_hbm, gain_hbm, send, queries, tables, gain, grid_ref, qp, anc, count, spots, sems
):
    pairs = ((anc_hbm, anc), (qp_hbm, qp), (tables_hbm, tables), (gain_hbm, gain))
    copies = [pltpu.make_async_copy(src, dst, sems.at[i]) for i, (src, dst) in enumerate(pairs)]
    for copy in copies:
        copy.start()
    rows, steps, width = qp.shape
    _, per_row, head_dim = tables.shape
    devices = send.shape[0]

    def clear(d, _):
        send[d] = jnp.zeros(send.shape[1:], BF16)
        count[d] = 0
        for j in range(PAIR):
            spots[PAIR * d + j] = 0
        return 0

    lax.fori_loop(0, devices, clear, 0)
    for copy in copies:
        copy.wait()
    for h in range(width // head_dim):
        grid_ref[:, steps * h : steps * (h + 1), :] = qp[:, :, head_dim * h : head_dim * (h + 1)].astype(F32)
    for r in range(rows):
        source, rank = slot_of(anc, r, rows, count)
        spots[source * PAIR + rank] = lax.rem(anc[r], rows)
        plain = grid_ref[r]
        turned = (plain * tables[0] + pltpu.roll(plain, head_dim // 2, 1) * tables[1]).astype(BF16)
        queries[r] = turned
        send[source, rank] = turned
    lane = lax.broadcasted_iota(jnp.int32, (per_row, head_dim), 1)
    for d in range(devices):
        send[d, PAIR] = jnp.where(
            lane < head_dim // 2, spots[PAIR * d].astype(F32), spots[PAIR * d + 1].astype(F32)
        ).astype(BF16)


def attend_kernel(
    recv, kv, x, gain, wk, wv, queries, tables, vectors, tops, sums, vec, stat, *scratch
):
    scores, expos, normed = scratch
    devices, _, per_row, head_dim = recv.shape
    lane = lax.broadcasted_iota(jnp.int32, (per_row, head_dim), 1)
    spots = []
    for d in range(devices):
        spot = recv[d, PAIR].astype(F32)
        for j in range(PAIR):
            spots.append(spot[0, j * (head_dim // PAIR)].astype(jnp.int32))
    for i in range(devices * PAIR):
        scores[i] = lax.dot_general(
            recv[i // PAIR, i % PAIR], kv[spots[i], 0, :, :head_dim], NT, preferred_element_type=F32
        ) * head_dim ** (-0.5)
    for i in range(devices * PAIR):
        top = jnp.max(scores[i], -1, keepdims=True)
        expo = jnp.exp(scores[i] - top)
        expos[i] = expo.astype(BF16)
        tops[i] = jnp.broadcast_to(top, lane.shape)
        sums[i] = jnp.broadcast_to(jnp.sum(expo, -1, keepdims=True), lane.shape)
    for i in range(devices * PAIR):
        vectors[i] = jnp.dot(expos[i], kv[spots[i], 0, :, head_dim:], preferred_element_type=F32)
    rows, steps, width = x.shape
    tokens = rows * steps
    floats = x[...].reshape(tokens, width).astype(F32)
    inverse = lax.rsqrt(jnp.mean(floats * floats, -1, keepdims=True) + EPSILON)
    normed[...] = (floats * gain[...]).astype(BF16)
    repeat = tokens // per_row
    cosine, sine = (jnp.concatenate([tables[i]] * repeat, 0) for i in range(2))
    keys = jnp.dot(normed[...], wk[...], preferred_element_type=F32) * inverse
    keys = (keys * cosine + pltpu.roll(keys, head_dim // 2, 1) * sine).astype(BF16)
    vals = (jnp.dot(normed[...], wv[...], preferred_element_type=F32) * inverse).astype(BF16)
    flat = queries[...].reshape(rows * per_row, head_dim)
    fresh = lax.dot_general(flat, keys, NT, preferred_element_type=F32) * head_dim ** (-0.5)
    row = lax.broadcasted_iota(jnp.int32, fresh.shape, 0)
    col = lax.broadcasted_iota(jnp.int32, fresh.shape, 1)
    seen = (lax.div(row, per_row) == lax.div(col, steps)) & (lax.rem(col, steps) <= lax.rem(row, steps))
    top = jnp.max(jnp.where(seen, fresh, -jnp.inf), -1, keepdims=True)
    expo = jnp.where(seen, jnp.exp(jnp.where(seen, fresh - top, 0.0)), 0.0)
    vec[...] = jnp.dot(expo.astype(BF16), vals, preferred_element_type=F32)
    stat[0] = jnp.broadcast_to(top, stat.shape[1:])
    stat[1] = jnp.broadcast_to(jnp.sum(expo, -1, keepdims=True), stat.shape[1:])


def return_kernel(vectors, tops, sums, back):
    devices, _, per_row, head_dim = back.shape
    lane = lax.broadcasted_iota(jnp.int32, (per_row, head_dim), 1)
    for d in range(devices):
        for j in range(PAIR):
            back[d, j] = (vectors[d * PAIR + j] / sums[d * PAIR + j]).astype(BF16)
        stat = jnp.zeros(lane.shape, F32)
        for j in range(PAIR):
            at_lane = j * (head_dim // PAIR)
            for value, parts in ((tops[d * PAIR + j], 3), (sums[d * PAIR + j], 2)):
                for _ in range(parts):
                    part = value.astype(BF16).astype(F32)
                    stat = jnp.where(lane == at_lane, part, stat)
                    value = value - part
                    at_lane += 1
        back[d, PAIR] = stat.astype(BF16)


def units(own, groups):
    index = lax.axis_index("tensor")
    y, core = lax.div(index, 2), lax.rem(index, 2)
    core = core if own else 1 - core
    return [2 * lax.rem(y + k, groups) + core for k in (*range(1, groups), 0)]


def product(wide, w, block, tokens, column):
    at = pl.multiple_of(block * column, column)
    return jnp.dot(wide, w[:, pl.ds(at, column)], preferred_element_type=F32)[:tokens]


def widen(heads):
    return jnp.concatenate([heads[...]] * max(1, 128 // heads.shape[0]), 0)


def project(heads, w, out, own):
    away, tokens, column = out.shape
    wide = widen(heads)
    for k, block in enumerate(units(own, away + 1)[:away]):
        out[k] = product(wide, w, block, tokens, column).astype(BF16)


def merge_kernel(anc, recv, vec, stat, w, out, heads, grid_ref, sums, lined, count):
    devices, _, per_row, head_dim = recv.shape
    rows = vec.shape[0] // per_row
    steps = heads.shape[0] // rows
    half = head_dim // PAIR
    for d in range(devices):
        count[d] = 0
    lane = lax.broadcasted_iota(jnp.int32, (per_row, head_dim), 1)
    for r in range(rows):
        source, rank = slot_of(anc, r, rows, count)
        grid_ref[pl.ds(r * per_row, per_row), :] = recv[source, rank].astype(F32)
        parts = recv[source, PAIR].astype(F32)
        sums[pl.ds(r * per_row, per_row), :] = jnp.where(lax.div(lane, half) == rank, parts, 0.0).astype(BF16)
    lane_from = lax.rem(lax.broadcasted_iota(jnp.int32, (head_dim, 2 * head_dim), 0), half)
    lane_to = lax.broadcasted_iota(jnp.int32, (head_dim, 2 * head_dim), 1)
    first = jnp.where(lane_from < 3, 1.0, 0.0)
    second = jnp.where((lane_from >= 3) & (lane_from < 5), 1.0, 0.0)
    spread = jnp.where(lane_to < head_dim, first, second)
    both = jnp.dot(sums[...], spread.astype(BF16), preferred_element_type=F32)
    top_c, sum_c = both[:, :head_dim], both[:, head_dim:]
    top_f, sum_f = stat[0], stat[1]
    top = jnp.maximum(top_c, top_f)
    factor_c = sum_c * jnp.exp(top_c - top)
    factor_f = jnp.exp(top_f - top)
    share = 1.0 / (factor_c + sum_f * factor_f)
    grid_ref[...] = (grid_ref[...] * factor_c + vec[...] * factor_f) * share
    for h in range(per_row // steps):
        for s in range(steps):
            lined[h, pl.ds(s, rows, stride=steps), :] = grid_ref[pl.ds(h * steps + s, rows, stride=per_row), :]
        heads[:, pl.ds(h * head_dim, head_dim)] = lined[h].astype(BF16)
    project(heads, w, out, False)


def second_kernel(heads, w, out):
    project(heads, w, out, True)


def add_kernel(mine, given, *outs):
    for k, out in enumerate(outs):
        out[...] = (mine[k].astype(F32) + given[k].astype(F32)).astype(BF16)


def last_kernel(heads, w, arrived, keep, crossing):
    tokens, column = keep.shape
    groups = w.shape[1] // column // 2
    wide = widen(heads)
    crossing[...] = product(wide, w, units(False, groups)[-1], tokens, column).astype(BF16)
    keep[...] = product(wide, w, units(True, groups)[-1], tokens, column) + arrived[...].astype(F32)


def shards(inputs, norm_gain, query_proj, w_key, w_value, w_out, kv_cache, ancestors):
    rows, steps, width = inputs.shape
    context = kv_cache.shape[2]
    head_dim = kv_cache.shape[3] // 2
    local = query_proj.shape[2]
    heads = local // head_dim
    per_row = heads * steps
    devices = lax.axis_size("particle")
    tensor = lax.axis_size("tensor")
    column = width // tensor
    cosine, sine = rotary_tables(context, steps, head_dim)
    tables = np.stack([np.tile(cosine, (heads, 1)), np.tile(sine, (heads, 1))])
    smem = pl.BlockSpec(memory_space=pltpu.SMEM)
    vmem = pl.BlockSpec(memory_space=pltpu.VMEM)
    stay = pl.BlockSpec(memory_space=pl.ANY)
    hbm = lambda x: pltpu.with_memory_space_constraint(x, pltpu.HBM)
    tables = jnp.asarray(tables)

    packed = (devices, PAIR + 1, per_row, head_dim)
    send, queries, tables, gain = pl.pallas_call(
        pack_kernel,
        out_shape=(
            jax.ShapeDtypeStruct(packed, BF16),
            jax.ShapeDtypeStruct((rows, per_row, head_dim), BF16),
            jax.ShapeDtypeStruct((2, per_row, head_dim), F32),
            jax.ShapeDtypeStruct((1, width), F32),
        ),
        in_specs=[stay] * 4,
        out_specs=(vmem,) * 4,
        scratch_shapes=[
            pltpu.VMEM((rows, per_row, head_dim), F32),
            pltpu.VMEM((rows, steps, local), BF16),
            pltpu.SMEM((rows,), jnp.int32),
            pltpu.SMEM((devices,), jnp.int32),
            pltpu.SMEM((devices * PAIR,), jnp.int32),
            pltpu.SemaphoreType.DMA((4,)),
        ],
        compiler_params=pltpu.CompilerParams(vmem_limit_bytes=4 * MIB),
        cost_estimate=pl.CostEstimate(flops=10_000_000_000, bytes_accessed=MIB, transcendentals=0),
        name="pack_queries",
    )(hbm(ancestors), hbm(query_proj), hbm(tables), hbm(norm_gain.reshape(1, width)))

    recv = lax.all_to_all(send, "particle", split_axis=0, concat_axis=0, tiled=True)

    slots = devices * PAIR
    partial_result = jax.ShapeDtypeStruct((slots, per_row, head_dim), F32)
    *found, vec, stat = pl.pallas_call(
        attend_kernel,
        out_shape=(partial_result,) * 3
        + (
            jax.ShapeDtypeStruct((rows * per_row, head_dim), F32),
            jax.ShapeDtypeStruct((2, rows * per_row, head_dim), F32),
        ),
        in_specs=[vmem] * 8,
        out_specs=(vmem,) * 5,
        scratch_shapes=[
            pltpu.VMEM((slots, per_row, context), F32),
            pltpu.VMEM((slots, per_row, context), BF16),
            pltpu.VMEM((rows * steps, width), BF16),
        ],
        compiler_params=pltpu.CompilerParams(vmem_limit_bytes=12 * MIB),
        cost_estimate=pl.CostEstimate(
            flops=4 * slots * per_row * context * head_dim, bytes_accessed=5 * MIB, transcendentals=0
        ),
        name="attention",
    )(
        recv,
        kv_cache,
        inputs,
        gain,
        w_key,
        w_value,
        queries,
        tables,
    )
    back = pl.pallas_call(
        return_kernel,
        out_shape=jax.ShapeDtypeStruct(packed, BF16),
        in_specs=[vmem] * 3,
        out_specs=vmem,
        compiler_params=pltpu.CompilerParams(vmem_limit_bytes=2 * MIB),
        cost_estimate=pl.CostEstimate(flops=10_000_000_000, bytes_accessed=MIB, transcendentals=0),
        name="pack_results",
    )(*found)
    home = lax.all_to_all(back, "particle", split_axis=0, concat_axis=0, tiled=True)

    groups = tensor // 2
    away = groups - 1
    block = jax.ShapeDtypeStruct((away, rows * steps, column), BF16)
    one = jax.ShapeDtypeStruct((rows * steps, column), BF16)
    params = pltpu.CompilerParams(vmem_limit_bytes=8 * MIB)
    cost = pl.CostEstimate(
        flops=rows * steps * local * width, bytes_accessed=local * width, transcendentals=0
    )
    other, heads_out = pl.pallas_call(
        merge_kernel,
        out_shape=(
            block,
            jax.ShapeDtypeStruct((rows * steps, local), BF16),
        ),
        in_specs=[smem, vmem, vmem, vmem, vmem],
        out_specs=(vmem, vmem),
        scratch_shapes=[
            pltpu.VMEM((rows * per_row, head_dim), F32),
            pltpu.VMEM((rows * per_row, head_dim), BF16),
            pltpu.VMEM((heads, rows * steps, head_dim), F32),
            pltpu.SMEM((devices,), jnp.int32),
        ],
        compiler_params=params,
        cost_estimate=cost,
        name="merge_project_sibling",
    )(ancestors, home, vec, stat, w_out)
    sibling = [(i, i ^ 1) for i in range(tensor)]
    given = lax.ppermute(other, "tensor", sibling)
    mine = pl.pallas_call(
        second_kernel,
        out_shape=block,
        in_specs=[vmem, vmem],
        out_specs=vmem,
        compiler_params=params,
        cost_estimate=cost,
        name="project_own",
    )(heads_out, w_out)
    pair = pl.pallas_call(
        add_kernel,
        out_shape=(one,) * away,
        in_specs=[vmem, vmem],
        out_specs=(vmem,) * away,
        compiler_params=params,
        name="add_sibling",
    )(mine, given)
    arrived = []
    for k in (1, *range(groups - 1, 1, -1)):
        ring = [(i, ((i // 2 + k) % groups) * 2 + i % 2) for i in range(tensor)]
        arrived.append(lax.ppermute(pair[k - 1], "tensor", ring))
    keep, crossing = pl.pallas_call(
        last_kernel,
        out_shape=(jax.ShapeDtypeStruct(one.shape, F32), one),
        in_specs=[vmem, vmem, vmem],
        out_specs=(vmem, vmem),
        compiler_params=params,
        cost_estimate=cost,
        name="project_last",
    )(heads_out, w_out, arrived[0])
    total = keep + lax.ppermute(crossing, "tensor", sibling).astype(F32)
    for part in arrived[1:]:
        total = total + part.astype(F32)
    return total.astype(BF16).reshape(rows, steps, column)


def solution(mesh):
    in_specs = (
        P("particle", None, None),
        P(),
        P("particle", None, "tensor"),
        P(None, "tensor"),
        P(None, "tensor"),
        P("tensor", None),
        P("particle", "tensor", None, None),
        P("particle"),
    )
    out_specs = P("particle", None, "tensor")
    return jax.shard_map(shards, mesh=mesh, in_specs=in_specs, out_specs=out_specs, check_vma=False)
```

```python
import jax
import jax.numpy as jnp
import numpy as np
from jax import lax
from jax.experimental import pallas as pl
from jax.experimental.pallas import tpu as pltpu
from jax.sharding import PartitionSpec as P

PAIR = 2
MORE = 8
THETA = 500000.0
EPSILON = 1e-05
F32 = jnp.float32
BF16 = jnp.bfloat16
MIB = 1 << 20
NT = (((1,), (1,)), ((), ()))


def rotary_tables(context, steps, head_dim):
    half = head_dim // 2
    freqs = np.float32(THETA) ** (-np.arange(half, dtype=np.float32) * np.float32(2.0) / np.float32(head_dim))
    position = (np.float32(context) + np.arange(steps, dtype=np.float32)).reshape(steps, 1)
    angles = (position * freqs.astype(np.float32)).astype(np.float32)
    cosine, sine = np.cos(angles), np.sin(angles)
    return (
        np.concatenate([cosine, cosine], 1).astype(np.float32),
        np.concatenate([-sine, sine], 1).astype(np.float32),
    )


def slot_of(anc, row, rows, count):
    source = lax.div(anc[row], rows)
    rank = count[source]
    count[source] = rank + 1
    return source, rank


def pack_kernel(
    anc_hbm, qp_hbm, tables_hbm, gain_hbm, send, queries, tables, gain, grid_ref, qp, anc, count, spots, sems
):
    pairs = ((anc_hbm, anc), (qp_hbm, qp), (tables_hbm, tables), (gain_hbm, gain))
    copies = [pltpu.make_async_copy(src, dst, sems.at[i]) for i, (src, dst) in enumerate(pairs)]
    for copy in copies:
        copy.start()
    rows, steps, width = qp.shape
    _, per_row, head_dim = tables.shape
    devices = send.shape[0]

    def clear(d, _):
        send[d] = jnp.zeros(send.shape[1:], BF16)
        count[d] = 0
        spots[d] = 0
        return 0

    lax.fori_loop(0, devices, clear, 0)
    for copy in copies:
        copy.wait()
    for h in range(width // head_dim):
        grid_ref[:, steps * h : steps * (h + 1), :] = qp[:, :, head_dim * h : head_dim * (h + 1)].astype(F32)
    for r in range(rows):
        source, rank = slot_of(anc, r, rows, count)
        spot = lax.rem(anc[r], rows)
        spots[source] = spots[source] + jnp.where(rank == 0, rows * spot, spot)
        plain = grid_ref[r]
        turned = (plain * tables[0] + pltpu.roll(plain, head_dim // 2, 1) * tables[1]).astype(BF16)
        queries[r] = turned
        send[source, pl.ds(pl.multiple_of(rank * per_row, per_row), per_row), :] = turned
    for d in range(devices):
        send[d, PAIR * per_row :, :] = jnp.full((MORE, head_dim), spots[d].astype(F32), F32).astype(BF16)


def slot_rows(chunks, i, per_row):
    at = (i % PAIR) * per_row
    return chunks[i // PAIR, at : at + per_row, :]


def attend_kernel(
    recv, kv, x, gain, wk, wv, queries, tables, vectors, tops, sums, vec, stat, *scratch
):
    scores, expos, normed = scratch
    devices, _, head_dim = recv.shape
    per_row = queries.shape[1]
    lane = lax.broadcasted_iota(jnp.int32, (per_row, head_dim), 1)
    spots = []
    for d in range(devices):
        both = recv[d, PAIR * per_row :, :].astype(F32)[0, 0].astype(jnp.int32)
        spots += [lax.div(both, kv.shape[0]), lax.rem(both, kv.shape[0])]
    for i in range(devices * PAIR):
        scores[i] = lax.dot_general(
            slot_rows(recv, i, per_row), kv[spots[i], 0, :, :head_dim], NT, preferred_element_type=F32
        ) * head_dim ** (-0.5)
    for i in range(devices * PAIR):
        top = jnp.max(scores[i], -1, keepdims=True)
        expo = jnp.exp(scores[i] - top)
        expos[i] = expo.astype(BF16)
        tops[i] = jnp.broadcast_to(top, lane.shape)
        sums[i] = jnp.broadcast_to(jnp.sum(expo, -1, keepdims=True), lane.shape)
    for i in range(devices * PAIR):
        vectors[i] = jnp.dot(expos[i], kv[spots[i], 0, :, head_dim:], preferred_element_type=F32)
    rows, steps, width = x.shape
    tokens = rows * steps
    floats = x[...].reshape(tokens, width).astype(F32)
    inverse = lax.rsqrt(jnp.mean(floats * floats, -1, keepdims=True) + EPSILON)
    normed[...] = (floats * inverse * gain[...]).astype(BF16)
    repeat = tokens // per_row
    cosine, sine = (jnp.concatenate([tables[i]] * repeat, 0) for i in range(2))
    keys = jnp.dot(normed[...], wk[...], preferred_element_type=F32)
    keys = (keys * cosine + pltpu.roll(keys, head_dim // 2, 1) * sine).astype(BF16)
    vals = jnp.dot(normed[...], wv[...], preferred_element_type=F32).astype(BF16)
    flat = queries[...].reshape(rows * per_row, head_dim)
    fresh = lax.dot_general(flat, keys, NT, preferred_element_type=F32) * head_dim ** (-0.5)
    row = lax.broadcasted_iota(jnp.int32, fresh.shape, 0)
    col = lax.broadcasted_iota(jnp.int32, fresh.shape, 1)
    seen = (lax.div(row, per_row) == lax.div(col, steps)) & (lax.rem(col, steps) <= lax.rem(row, steps))
    top = jnp.max(jnp.where(seen, fresh, -jnp.inf), -1, keepdims=True)
    expo = jnp.where(seen, jnp.exp(jnp.where(seen, fresh - top, 0.0)), 0.0)
    vec[...] = jnp.dot(expo.astype(BF16), vals, preferred_element_type=F32)
    stat[0] = jnp.broadcast_to(top, stat.shape[1:])
    stat[1] = jnp.broadcast_to(jnp.sum(expo, -1, keepdims=True), stat.shape[1:])


def return_kernel(vectors, tops, sums, back):
    devices, _, head_dim = back.shape
    per_row = vectors.shape[1]
    lane = lax.broadcasted_iota(jnp.int32, (MORE, head_dim), 1)
    quarter = head_dim * MORE // (PAIR * per_row)
    for d in range(devices):
        stat = jnp.zeros(lane.shape, F32)
        for j in range(PAIR):
            i = d * PAIR + j
            back[d, j * per_row : (j + 1) * per_row, :] = (vectors[i] / sums[i]).astype(BF16)
            for g in range(per_row // MORE):
                at_lane = (j * (per_row // MORE) + g) * quarter
                for source, parts in ((tops, 3), (sums, 2)):
                    value = source[i, g * MORE : (g + 1) * MORE, :]
                    for _ in range(parts):
                        part = value.astype(BF16).astype(F32)
                        stat = jnp.where(lane == at_lane, part, stat)
                        value = value - part
                        at_lane += 1
        back[d, PAIR * per_row :, :] = stat.astype(BF16)


def units(own, groups):
    index = lax.axis_index("tensor")
    y, core = lax.div(index, 2), lax.rem(index, 2)
    core = core if own else 1 - core
    return [2 * lax.rem(y + k, groups) + core for k in (*range(1, groups), 0)]


def product(wide, w, block, tokens, column):
    at = pl.multiple_of(block * column, column)
    return jnp.dot(wide, w[:, pl.ds(at, column)], preferred_element_type=F32)[:tokens]


def widen(heads):
    return jnp.concatenate([heads[...]] * max(1, 128 // heads.shape[0]), 0)


def project(heads, w, out, own):
    away, tokens, column = out.shape
    wide = widen(heads)
    for k, block in enumerate(units(own, away + 1)[:away]):
        out[k] = product(wide, w, block, tokens, column).astype(BF16)


def merge_kernel(anc, recv, vec, stat, w, out, heads, grid_ref, sums, lined, count):
    devices, chunk, head_dim = recv.shape
    per_row = (chunk - MORE) // PAIR
    rows = vec.shape[0] // per_row
    steps = heads.shape[0] // rows
    pieces = per_row // MORE
    quarter = head_dim // (PAIR * pieces)
    for d in range(devices):
        count[d] = 0
    part_of = lax.div(lax.broadcasted_iota(jnp.int32, (MORE, head_dim), 1), quarter)
    for r in range(rows):
        source, rank = slot_of(anc, r, rows, count)
        at = pl.multiple_of(rank * per_row, per_row)
        grid_ref[pl.ds(r * per_row, per_row), :] = recv[source, pl.ds(at, per_row), :].astype(F32)
        parts = recv[source, PAIR * per_row :, :].astype(F32)
        sums[pl.ds(r * per_row, per_row), :] = jnp.concatenate(
            [jnp.where(part_of == rank * pieces + g, parts, 0.0) for g in range(pieces)], 0
        ).astype(BF16)
    lane_from = lax.rem(lax.broadcasted_iota(jnp.int32, (head_dim, 2 * head_dim), 0), quarter)
    lane_to = lax.broadcasted_iota(jnp.int32, (head_dim, 2 * head_dim), 1)
    first = jnp.where(lane_from < 3, 1.0, 0.0)
    second = jnp.where((lane_from >= 3) & (lane_from < 5), 1.0, 0.0)
    spread = jnp.where(lane_to < head_dim, first, second)
    both = jnp.dot(sums[...], spread.astype(BF16), preferred_element_type=F32)
    top_c, sum_c = both[:, :head_dim], both[:, head_dim:]
    top_f, sum_f = stat[0], stat[1]
    top = jnp.maximum(top_c, top_f)
    factor_c = sum_c * jnp.exp(top_c - top)
    factor_f = jnp.exp(top_f - top)
    share = 1.0 / (factor_c + sum_f * factor_f)
    grid_ref[...] = (grid_ref[...] * factor_c + vec[...] * factor_f) * share
    for h in range(per_row // steps):
        for s in range(steps):
            lined[h, pl.ds(s, rows, stride=steps), :] = grid_ref[pl.ds(h * steps + s, rows, stride=per_row), :]
        heads[:, pl.ds(h * head_dim, head_dim)] = lined[h].astype(BF16)
    project(heads, w, out, False)


def second_kernel(heads, w, out):
    project(heads, w, out, True)


def add_kernel(mine, given, *outs):
    for k, out in enumerate(outs):
        out[...] = (mine[k].astype(F32) + given[k].astype(F32)).astype(BF16)


def last_kernel(heads, w, arrived, keep, crossing):
    tokens, column = keep.shape
    groups = w.shape[1] // column // 2
    wide = widen(heads)
    crossing[...] = product(wide, w, units(False, groups)[-1], tokens, column).astype(BF16)
    keep[...] = product(wide, w, units(True, groups)[-1], tokens, column) + arrived[...].astype(F32)


def shards(inputs, norm_gain, query_proj, w_key, w_value, w_out, kv_cache, ancestors):
    rows, steps, width = inputs.shape
    context = kv_cache.shape[2]
    head_dim = kv_cache.shape[3] // 2
    local = query_proj.shape[2]
    heads = local // head_dim
    per_row = heads * steps
    devices = lax.axis_size("particle")
    tensor = lax.axis_size("tensor")
    column = width // tensor
    cosine, sine = rotary_tables(context, steps, head_dim)
    tables = np.stack([np.tile(cosine, (heads, 1)), np.tile(sine, (heads, 1))])
    smem = pl.BlockSpec(memory_space=pltpu.SMEM)
    vmem = pl.BlockSpec(memory_space=pltpu.VMEM)
    stay = pl.BlockSpec(memory_space=pl.ANY)
    hbm = lambda x: pltpu.with_memory_space_constraint(x, pltpu.HBM)
    tables = jnp.asarray(tables)

    packed = (devices, PAIR * per_row + MORE, head_dim)
    send, queries, tables, gain = pl.pallas_call(
        pack_kernel,
        out_shape=(
            jax.ShapeDtypeStruct(packed, BF16),
            jax.ShapeDtypeStruct((rows, per_row, head_dim), BF16),
            jax.ShapeDtypeStruct((2, per_row, head_dim), F32),
            jax.ShapeDtypeStruct((1, width), F32),
        ),
        in_specs=[stay] * 4,
        out_specs=(vmem,) * 4,
        scratch_shapes=[
            pltpu.VMEM((rows, per_row, head_dim), F32),
            pltpu.VMEM((rows, steps, local), BF16),
            pltpu.SMEM((rows,), jnp.int32),
            pltpu.SMEM((devices,), jnp.int32),
            pltpu.SMEM((devices,), jnp.int32),
            pltpu.SemaphoreType.DMA((4,)),
        ],
        compiler_params=pltpu.CompilerParams(vmem_limit_bytes=4 * MIB),
        cost_estimate=pl.CostEstimate(flops=10_000_000_000, bytes_accessed=MIB, transcendentals=0),
        name="pack_queries",
    )(hbm(ancestors), hbm(query_proj), hbm(tables), hbm(norm_gain.reshape(1, width)))

    recv = lax.all_to_all(send, "particle", split_axis=0, concat_axis=0, tiled=True)

    slots = devices * PAIR
    partial_result = jax.ShapeDtypeStruct((slots, per_row, head_dim), F32)
    *found, vec, stat = pl.pallas_call(
        attend_kernel,
        out_shape=(partial_result,) * 3
        + (
            jax.ShapeDtypeStruct((rows * per_row, head_dim), F32),
            jax.ShapeDtypeStruct((2, rows * per_row, head_dim), F32),
        ),
        in_specs=[vmem] * 8,
        out_specs=(vmem,) * 5,
        scratch_shapes=[
            pltpu.VMEM((slots, per_row, context), F32),
            pltpu.VMEM((slots, per_row, context), BF16),
            pltpu.VMEM((rows * steps, width), BF16),
        ],
        compiler_params=pltpu.CompilerParams(vmem_limit_bytes=12 * MIB),
        cost_estimate=pl.CostEstimate(
            flops=4 * slots * per_row * context * head_dim, bytes_accessed=5 * MIB, transcendentals=0
        ),
        name="attention",
    )(
        recv,
        kv_cache,
        inputs,
        gain,
        w_key,
        w_value,
        queries,
        tables,
    )
    back = pl.pallas_call(
        return_kernel,
        out_shape=jax.ShapeDtypeStruct(packed, BF16),
        in_specs=[vmem] * 3,
        out_specs=vmem,
        compiler_params=pltpu.CompilerParams(vmem_limit_bytes=2 * MIB),
        cost_estimate=pl.CostEstimate(flops=10_000_000_000, bytes_accessed=MIB, transcendentals=0),
        name="pack_results",
    )(*found)
    home = lax.all_to_all(back, "particle", split_axis=0, concat_axis=0, tiled=True)

    groups = tensor // 2
    away = groups - 1
    block = jax.ShapeDtypeStruct((away, rows * steps, column), BF16)
    one = jax.ShapeDtypeStruct((rows * steps, column), BF16)
    params = pltpu.CompilerParams(vmem_limit_bytes=8 * MIB)
    cost = pl.CostEstimate(
        flops=rows * steps * local * width, bytes_accessed=local * width, transcendentals=0
    )
    other, heads_out = pl.pallas_call(
        merge_kernel,
        out_shape=(
            block,
            jax.ShapeDtypeStruct((rows * steps, local), BF16),
        ),
        in_specs=[smem, vmem, vmem, vmem, vmem],
        out_specs=(vmem, vmem),
        scratch_shapes=[
            pltpu.VMEM((rows * per_row, head_dim), F32),
            pltpu.VMEM((rows * per_row, head_dim), BF16),
            pltpu.VMEM((heads, rows * steps, head_dim), F32),
            pltpu.SMEM((devices,), jnp.int32),
        ],
        compiler_params=params,
        cost_estimate=cost,
        name="merge_project_sibling",
    )(ancestors, home, vec, stat, w_out)
    sibling = [(i, i ^ 1) for i in range(tensor)]
    given = lax.ppermute(other, "tensor", sibling)
    mine = pl.pallas_call(
        second_kernel,
        out_shape=block,
        in_specs=[vmem, vmem],
        out_specs=vmem,
        compiler_params=params,
        cost_estimate=cost,
        name="project_own",
    )(heads_out, w_out)
    pair = pl.pallas_call(
        add_kernel,
        out_shape=(one,) * away,
        in_specs=[vmem, vmem],
        out_specs=(vmem,) * away,
        compiler_params=params,
        name="add_sibling",
    )(mine, given)
    arrived = []
    for k in (1, *range(groups - 1, 1, -1)):
        ring = [(i, ((i // 2 + k) % groups) * 2 + i % 2) for i in range(tensor)]
        arrived.append(lax.ppermute(pair[k - 1], "tensor", ring))
    keep, crossing = pl.pallas_call(
        last_kernel,
        out_shape=(jax.ShapeDtypeStruct(one.shape, F32), one),
        in_specs=[vmem, vmem, vmem],
        out_specs=(vmem, vmem),
        compiler_params=params,
        cost_estimate=cost,
        name="project_last",
    )(heads_out, w_out, arrived[0])
    total = keep + lax.ppermute(crossing, "tensor", sibling).astype(F32)
    for part in arrived[1:]:
        total = total + part.astype(F32)
    return total.astype(BF16).reshape(rows, steps, column)


def solution(mesh):
    in_specs = (
        P("particle", None, None),
        P(),
        P("particle", None, "tensor"),
        P(None, "tensor"),
        P(None, "tensor"),
        P("tensor", None),
        P("particle", "tensor", None, None),
        P("particle"),
    )
    out_specs = P("particle", None, "tensor")
    return jax.shard_map(shards, mesh=mesh, in_specs=in_specs, out_specs=out_specs, check_vma=False)
```

```python
import jax
import jax.numpy as jnp
import numpy as np
from jax import lax
from jax.experimental import pallas as pl
from jax.experimental.pallas import tpu as pltpu
from jax.sharding import PartitionSpec as P

PAIR = 2
MORE = 8
THETA = 500000.0
EPSILON = 1e-05
F32 = jnp.float32
BF16 = jnp.bfloat16
MIB = 1 << 20
NT = (((1,), (1,)), ((), ()))


def rotary_tables(context, steps, head_dim):
    half = head_dim // 2
    freqs = np.float32(THETA) ** (-np.arange(half, dtype=np.float32) * np.float32(2.0) / np.float32(head_dim))
    position = (np.float32(context) + np.arange(steps, dtype=np.float32)).reshape(steps, 1)
    angles = (position * freqs.astype(np.float32)).astype(np.float32)
    cosine, sine = np.cos(angles), np.sin(angles)
    return (
        np.concatenate([cosine, cosine], 1).astype(np.float32),
        np.concatenate([-sine, sine], 1).astype(np.float32),
    )


def slot_of(anc, row, rows, count):
    source = lax.div(anc[row], rows)
    rank = count[source]
    count[source] = rank + 1
    return source, rank


def pack_kernel(
    anc_hbm, qp_hbm, tables_hbm, gain_hbm, send, queries, tables, gain, grid_ref, qp, anc, count, spots, sems
):
    pairs = ((anc_hbm, anc), (qp_hbm, qp), (tables_hbm, tables), (gain_hbm, gain))
    copies = [pltpu.make_async_copy(src, dst, sems.at[i]) for i, (src, dst) in enumerate(pairs)]
    for copy in copies:
        copy.start()
    rows, steps, width = qp.shape
    _, per_row, head_dim = tables.shape
    devices = send.shape[0]

    def clear(d, _):
        send[d] = jnp.zeros(send.shape[1:], BF16)
        count[d] = 0
        for j in range(PAIR):
            spots[PAIR * d + j] = 0
        return 0

    lax.fori_loop(0, devices, clear, 0)
    for copy in copies:
        copy.wait()
    for h in range(width // head_dim):
        grid_ref[:, steps * h : steps * (h + 1), :] = qp[:, :, head_dim * h : head_dim * (h + 1)].astype(F32)
    for r in range(rows):
        source, rank = slot_of(anc, r, rows, count)
        spots[source * PAIR + rank] = lax.rem(anc[r], rows)
        plain = grid_ref[r]
        turned = (plain * tables[0] + pltpu.roll(plain, head_dim // 2, 1) * tables[1]).astype(BF16)
        queries[r] = turned
        send[source, pl.ds(pl.multiple_of(rank * per_row, per_row), per_row), :] = turned
    lane = lax.broadcasted_iota(jnp.int32, (MORE, head_dim), 1)
    for d in range(devices):
        send[d, PAIR * per_row :, :] = jnp.where(
            lane < head_dim // PAIR, spots[PAIR * d].astype(F32), spots[PAIR * d + 1].astype(F32)
        ).astype(BF16)


def slot_rows(chunks, i, per_row):
    at = (i % PAIR) * per_row
    return chunks[i // PAIR, at : at + per_row, :]


def pack_statistics(tops, sums, back):
    devices, _, head_dim = back.shape
    per_row = tops.shape[1]
    lane = lax.broadcasted_iota(jnp.int32, (MORE, head_dim), 1)
    quarter = head_dim * MORE // (PAIR * per_row)
    for d in range(devices):
        stat = jnp.zeros(lane.shape, F32)
        for j in range(PAIR):
            i = d * PAIR + j
            for g in range(per_row // MORE):
                at_lane = (j * (per_row // MORE) + g) * quarter
                for source, parts in ((tops, 3), (sums, 2)):
                    value = source[i, g * MORE : (g + 1) * MORE, :]
                    for _ in range(parts):
                        part = value.astype(BF16).astype(F32)
                        stat = jnp.where(lane == at_lane, part, stat)
                        value = value - part
                        at_lane += 1
        back[d, PAIR * per_row :, :] = stat.astype(BF16)


def attend_kernel(
    recv, kv, x, gain, wk, wv, queries, tables, back, vec, stat, *scratch
):
    scores, expos, tops, sums, normed = scratch
    devices, _, head_dim = recv.shape
    per_row = queries.shape[1]
    lane = lax.broadcasted_iota(jnp.int32, (per_row, head_dim), 1)
    spots = []
    for d in range(devices):
        spot = recv[d, PAIR * per_row :, :].astype(F32)
        for j in range(PAIR):
            spots.append(spot[0, j * (head_dim // PAIR)].astype(jnp.int32))
    for i in range(devices * PAIR):
        scores[i] = lax.dot_general(
            slot_rows(recv, i, per_row), kv[spots[i], 0, :, :head_dim], NT, preferred_element_type=F32
        ) * head_dim ** (-0.5)
    for i in range(devices * PAIR):
        top = jnp.max(scores[i], -1, keepdims=True)
        expo = jnp.exp(scores[i] - top)
        expos[i] = expo.astype(BF16)
        tops[i] = jnp.broadcast_to(top, lane.shape)
        sums[i] = jnp.broadcast_to(jnp.sum(expo, -1, keepdims=True), lane.shape)
    for i in range(devices * PAIR):
        vector = jnp.dot(expos[i], kv[spots[i], 0, :, head_dim:], preferred_element_type=F32)
        at = (i % PAIR) * per_row
        back[i // PAIR, at : at + per_row, :] = (vector / sums[i]).astype(BF16)
    pack_statistics(tops, sums, back)
    rows, steps, width = x.shape
    tokens = rows * steps
    floats = x[...].reshape(tokens, width).astype(F32)
    inverse = lax.rsqrt(jnp.mean(floats * floats, -1, keepdims=True) + EPSILON)
    normed[...] = (floats * inverse * gain[...]).astype(BF16)
    repeat = tokens // per_row
    cosine, sine = (jnp.concatenate([tables[i]] * repeat, 0) for i in range(2))
    keys = jnp.dot(normed[...], wk[...], preferred_element_type=F32)
    keys = (keys * cosine + pltpu.roll(keys, head_dim // 2, 1) * sine).astype(BF16)
    vals = jnp.dot(normed[...], wv[...], preferred_element_type=F32).astype(BF16)
    flat = queries[...].reshape(rows * per_row, head_dim)
    fresh = lax.dot_general(flat, keys, NT, preferred_element_type=F32) * head_dim ** (-0.5)
    row = lax.broadcasted_iota(jnp.int32, fresh.shape, 0)
    col = lax.broadcasted_iota(jnp.int32, fresh.shape, 1)
    seen = (lax.div(row, per_row) == lax.div(col, steps)) & (lax.rem(col, steps) <= lax.rem(row, steps))
    top = jnp.max(jnp.where(seen, fresh, -jnp.inf), -1, keepdims=True)
    expo = jnp.where(seen, jnp.exp(jnp.where(seen, fresh - top, 0.0)), 0.0)
    vec[...] = jnp.dot(expo.astype(BF16), vals, preferred_element_type=F32)
    stat[0] = jnp.broadcast_to(top, stat.shape[1:])
    stat[1] = jnp.broadcast_to(jnp.sum(expo, -1, keepdims=True), stat.shape[1:])


def units(own, groups):
    index = lax.axis_index("tensor")
    y, core = lax.div(index, 2), lax.rem(index, 2)
    core = core if own else 1 - core
    return [2 * lax.rem(y + k, groups) + core for k in (*range(1, groups), 0)]


def product(wide, w, block, tokens, column):
    at = pl.multiple_of(block * column, column)
    return jnp.dot(wide, w[:, pl.ds(at, column)], preferred_element_type=F32)[:tokens]


def widen(heads):
    return jnp.concatenate([heads[...]] * max(1, 128 // heads.shape[0]), 0)


def project(heads, w, out, own):
    away, tokens, column = out.shape
    wide = widen(heads)
    for k, block in enumerate(units(own, away + 1)[:away]):
        out[k] = product(wide, w, block, tokens, column).astype(BF16)


def merge_kernel(anc, recv, vec, stat, w, out, heads, grid_ref, sums, lined, count):
    devices, chunk, head_dim = recv.shape
    per_row = (chunk - MORE) // PAIR
    rows = vec.shape[0] // per_row
    steps = heads.shape[0] // rows
    pieces = per_row // MORE
    quarter = head_dim // (PAIR * pieces)
    for d in range(devices):
        count[d] = 0
    part_of = lax.div(lax.broadcasted_iota(jnp.int32, (MORE, head_dim), 1), quarter)
    for r in range(rows):
        source, rank = slot_of(anc, r, rows, count)
        at = pl.multiple_of(rank * per_row, per_row)
        grid_ref[pl.ds(r * per_row, per_row), :] = recv[source, pl.ds(at, per_row), :].astype(F32)
        parts = recv[source, PAIR * per_row :, :].astype(F32)
        sums[pl.ds(r * per_row, per_row), :] = jnp.concatenate(
            [jnp.where(part_of == rank * pieces + g, parts, 0.0) for g in range(pieces)], 0
        ).astype(BF16)
    lane_from = lax.rem(lax.broadcasted_iota(jnp.int32, (head_dim, 2 * head_dim), 0), quarter)
    lane_to = lax.broadcasted_iota(jnp.int32, (head_dim, 2 * head_dim), 1)
    first = jnp.where(lane_from < 3, 1.0, 0.0)
    second = jnp.where((lane_from >= 3) & (lane_from < 5), 1.0, 0.0)
    spread = jnp.where(lane_to < head_dim, first, second)
    both = jnp.dot(sums[...], spread.astype(BF16), preferred_element_type=F32)
    top_c, sum_c = both[:, :head_dim], both[:, head_dim:]
    top_f, sum_f = stat[0], stat[1]
    top = jnp.maximum(top_c, top_f)
    factor_c = sum_c * jnp.exp(top_c - top)
    factor_f = jnp.exp(top_f - top)
    share = 1.0 / (factor_c + sum_f * factor_f)
    grid_ref[...] = (grid_ref[...] * factor_c + vec[...] * factor_f) * share
    for h in range(per_row // steps):
        for s in range(steps):
            lined[h, pl.ds(s, rows, stride=steps), :] = grid_ref[pl.ds(h * steps + s, rows, stride=per_row), :]
        heads[:, pl.ds(h * head_dim, head_dim)] = lined[h].astype(BF16)
    project(heads, w, out, False)


def second_kernel(heads, w, out):
    project(heads, w, out, True)


def add_kernel(mine, given, *outs):
    for k, out in enumerate(outs):
        out[...] = (mine[k].astype(F32) + given[k].astype(F32)).astype(BF16)


def last_kernel(heads, w, arrived, keep, crossing):
    tokens, column = keep.shape
    groups = w.shape[1] // column // 2
    wide = widen(heads)
    crossing[...] = product(wide, w, units(False, groups)[-1], tokens, column).astype(BF16)
    keep[...] = product(wide, w, units(True, groups)[-1], tokens, column) + arrived[...].astype(F32)


def shards(inputs, norm_gain, query_proj, w_key, w_value, w_out, kv_cache, ancestors):
    rows, steps, width = inputs.shape
    context = kv_cache.shape[2]
    head_dim = kv_cache.shape[3] // 2
    local = query_proj.shape[2]
    heads = local // head_dim
    per_row = heads * steps
    devices = lax.axis_size("particle")
    tensor = lax.axis_size("tensor")
    column = width // tensor
    cosine, sine = rotary_tables(context, steps, head_dim)
    tables = np.stack([np.tile(cosine, (heads, 1)), np.tile(sine, (heads, 1))])
    smem = pl.BlockSpec(memory_space=pltpu.SMEM)
    vmem = pl.BlockSpec(memory_space=pltpu.VMEM)
    stay = pl.BlockSpec(memory_space=pl.ANY)
    hbm = lambda x: pltpu.with_memory_space_constraint(x, pltpu.HBM)
    tables = jnp.asarray(tables)

    packed = (devices, PAIR * per_row + MORE, head_dim)
    send, queries, tables, gain = pl.pallas_call(
        pack_kernel,
        out_shape=(
            jax.ShapeDtypeStruct(packed, BF16),
            jax.ShapeDtypeStruct((rows, per_row, head_dim), BF16),
            jax.ShapeDtypeStruct((2, per_row, head_dim), F32),
            jax.ShapeDtypeStruct((1, width), F32),
        ),
        in_specs=[stay] * 4,
        out_specs=(vmem,) * 4,
        scratch_shapes=[
            pltpu.VMEM((rows, per_row, head_dim), F32),
            pltpu.VMEM((rows, steps, local), BF16),
            pltpu.SMEM((rows,), jnp.int32),
            pltpu.SMEM((devices,), jnp.int32),
            pltpu.SMEM((devices * PAIR,), jnp.int32),
            pltpu.SemaphoreType.DMA((4,)),
        ],
        compiler_params=pltpu.CompilerParams(vmem_limit_bytes=4 * MIB),
        cost_estimate=pl.CostEstimate(flops=10_000_000_000, bytes_accessed=MIB, transcendentals=0),
        name="pack_queries",
    )(hbm(ancestors), hbm(query_proj), hbm(tables), hbm(norm_gain.reshape(1, width)))

    recv = lax.all_to_all(send, "particle", split_axis=0, concat_axis=0, tiled=True)

    slots = devices * PAIR
    back, vec, stat = pl.pallas_call(
        attend_kernel,
        out_shape=(
            jax.ShapeDtypeStruct(packed, BF16),
            jax.ShapeDtypeStruct((rows * per_row, head_dim), F32),
            jax.ShapeDtypeStruct((2, rows * per_row, head_dim), F32),
        ),
        in_specs=[vmem] * 8,
        out_specs=(vmem,) * 3,
        scratch_shapes=[
            pltpu.VMEM((slots, per_row, context), F32),
            pltpu.VMEM((slots, per_row, context), BF16),
            pltpu.VMEM((slots, per_row, head_dim), F32),
            pltpu.VMEM((slots, per_row, head_dim), F32),
            pltpu.VMEM((rows * steps, width), BF16),
        ],
        compiler_params=pltpu.CompilerParams(vmem_limit_bytes=12 * MIB),
        cost_estimate=pl.CostEstimate(
            flops=10_000_000_000, bytes_accessed=5 * MIB, transcendentals=0
        ),
        name="attention",
    )(
        recv,
        kv_cache,
        inputs,
        gain,
        w_key,
        w_value,
        queries,
        tables,
    )
    home = lax.all_to_all(back, "particle", split_axis=0, concat_axis=0, tiled=True)

    groups = tensor // 2
    away = groups - 1
    block = jax.ShapeDtypeStruct((away, rows * steps, column), BF16)
    one = jax.ShapeDtypeStruct((rows * steps, column), BF16)
    params = pltpu.CompilerParams(vmem_limit_bytes=8 * MIB)
    cost = pl.CostEstimate(
        flops=rows * steps * local * width, bytes_accessed=local * width, transcendentals=0
    )
    other, heads_out = pl.pallas_call(
        merge_kernel,
        out_shape=(
            block,
            jax.ShapeDtypeStruct((rows * steps, local), BF16),
        ),
        in_specs=[smem, vmem, vmem, vmem, vmem],
        out_specs=(vmem, vmem),
        scratch_shapes=[
            pltpu.VMEM((rows * per_row, head_dim), F32),
            pltpu.VMEM((rows * per_row, head_dim), BF16),
            pltpu.VMEM((heads, rows * steps, head_dim), F32),
            pltpu.SMEM((devices,), jnp.int32),
        ],
        compiler_params=params,
        cost_estimate=cost,
        name="merge_project_sibling",
    )(ancestors, home, vec, stat, w_out)
    sibling = [(i, i ^ 1) for i in range(tensor)]
    given = lax.ppermute(other, "tensor", sibling)
    mine = pl.pallas_call(
        second_kernel,
        out_shape=block,
        in_specs=[vmem, vmem],
        out_specs=vmem,
        compiler_params=params,
        cost_estimate=cost,
        name="project_own",
    )(heads_out, w_out)
    pair = pl.pallas_call(
        add_kernel,
        out_shape=(one,) * away,
        in_specs=[vmem, vmem],
        out_specs=(vmem,) * away,
        compiler_params=params,
        name="add_sibling",
    )(mine, given)
    arrived = []
    for k in range(1, groups):
        ring = [(i, ((i // 2 + k) % groups) * 2 + i % 2) for i in range(tensor)]
        arrived.append(lax.ppermute(pair[k - 1], "tensor", ring))
    keep, crossing = pl.pallas_call(
        last_kernel,
        out_shape=(jax.ShapeDtypeStruct(one.shape, F32), one),
        in_specs=[vmem, vmem, vmem],
        out_specs=(vmem, vmem),
        compiler_params=params,
        cost_estimate=cost,
        name="project_last",
    )(heads_out, w_out, arrived[0])
    total = keep + lax.ppermute(crossing, "tensor", sibling).astype(F32)
    for part in arrived[1:]:
        total = total + part.astype(F32)
    return total.astype(BF16).reshape(rows, steps, column)


def solution(mesh):
    in_specs = (
        P("particle", None, None),
        P(),
        P("particle", None, "tensor"),
        P(None, "tensor"),
        P(None, "tensor"),
        P("tensor", None),
        P("particle", "tensor", None, None),
        P("particle"),
    )
    out_specs = P("particle", None, "tensor")
    return jax.shard_map(shards, mesh=mesh, in_specs=in_specs, out_specs=out_specs, check_vma=False)
```

```python
import jax
import jax.numpy as jnp
import numpy as np
from jax import lax
from jax.experimental import pallas as pl
from jax.experimental.pallas import tpu as pltpu
from jax.sharding import PartitionSpec as P

PAIR = 2
PARTNERS = (2, 3, 1)
MORE = 8
THETA = 500000.0
EPSILON = 1e-05
F32 = jnp.float32
BF16 = jnp.bfloat16
MIB = 1 << 20
NT = (((1,), (1,)), ((), ()))


def rotary_tables(context, steps, head_dim):
    half = head_dim // 2
    freqs = np.float32(THETA) ** (-np.arange(half, dtype=np.float32) * np.float32(2.0) / np.float32(head_dim))
    position = (np.float32(context) + np.arange(steps, dtype=np.float32)).reshape(steps, 1)
    angles = (position * freqs.astype(np.float32)).astype(np.float32)
    cosine, sine = np.cos(angles), np.sin(angles)
    return (
        np.concatenate([cosine, cosine], 1).astype(np.float32),
        np.concatenate([-sine, sine], 1).astype(np.float32),
    )


def slot_of(anc, row, rows, count):
    source = lax.div(anc[row], rows)
    rank = count[source]
    count[source] = rank + 1
    return source, rank


def pack_kernel(
    anc_hbm, qp_hbm, tables_hbm, gain_hbm, send, queries, tables, gain, grid_ref, qp, anc, count, spots, sems
):
    pairs = ((anc_hbm, anc), (qp_hbm, qp), (tables_hbm, tables), (gain_hbm, gain))
    copies = [pltpu.make_async_copy(src, dst, sems.at[i]) for i, (src, dst) in enumerate(pairs)]
    for copy in copies:
        copy.start()
    rows, steps, width = qp.shape
    _, per_row, head_dim = tables.shape
    devices = send.shape[0]

    def clear(d, _):
        send[d] = jnp.zeros(send.shape[1:], BF16)
        count[d] = 0
        for j in range(PAIR):
            spots[PAIR * d + j] = 0
        return 0

    lax.fori_loop(0, devices, clear, 0)
    for copy in copies:
        copy.wait()
    for h in range(width // head_dim):
        grid_ref[:, steps * h : steps * (h + 1), :] = qp[:, :, head_dim * h : head_dim * (h + 1)].astype(F32)
    for r in range(rows):
        source, rank = slot_of(anc, r, rows, count)
        spots[source * PAIR + rank] = lax.rem(anc[r], rows)
        plain = grid_ref[r]
        turned = (plain * tables[0] + pltpu.roll(plain, head_dim // 2, 1) * tables[1]).astype(BF16)
        queries[r] = turned
        send[source, pl.ds(pl.multiple_of(rank * per_row, per_row), per_row), :] = turned
    lane = lax.broadcasted_iota(jnp.int32, (MORE, head_dim), 1)
    for d in range(devices):
        send[d, PAIR * per_row :, :] = jnp.where(
            lane < head_dim // PAIR, spots[PAIR * d].astype(F32), spots[PAIR * d + 1].astype(F32)
        ).astype(BF16)


def slot_rows(chunks, i, per_row):
    at = (i % PAIR) * per_row
    return chunks[i // PAIR, at : at + per_row, :]


def pack_statistics(tops, sums, back):
    devices, _, head_dim = back.shape
    per_row = tops.shape[1]
    lane = lax.broadcasted_iota(jnp.int32, (MORE, head_dim), 1)
    quarter = head_dim * MORE // (PAIR * per_row)
    for d in range(devices):
        stat = jnp.zeros(lane.shape, F32)
        for j in range(PAIR):
            i = d * PAIR + j
            for g in range(per_row // MORE):
                at_lane = (j * (per_row // MORE) + g) * quarter
                for source, parts in ((tops, 3), (sums, 2)):
                    value = source[i, g * MORE : (g + 1) * MORE, :]
                    for _ in range(parts):
                        part = value.astype(BF16).astype(F32)
                        stat = jnp.where(lane == at_lane, part, stat)
                        value = value - part
                        at_lane += 1
        back[d, PAIR * per_row :, :] = stat.astype(BF16)


def attend_kernel(
    recv, kv, x, gain, wk, wv, queries, tables, back, vec, stat, *scratch
):
    scores, expos, tops, sums, normed = scratch
    devices, _, head_dim = recv.shape
    per_row = queries.shape[1]
    lane = lax.broadcasted_iota(jnp.int32, (per_row, head_dim), 1)
    spots = []
    for d in range(devices):
        spot = recv[d, PAIR * per_row :, :].astype(F32)
        for j in range(PAIR):
            spots.append(spot[0, j * (head_dim // PAIR)].astype(jnp.int32))
    for i in range(devices * PAIR):
        scores[i] = lax.dot_general(
            slot_rows(recv, i, per_row), kv[spots[i], 0, :, :head_dim], NT, preferred_element_type=F32
        ) * head_dim ** (-0.5)
    for i in range(devices * PAIR):
        top = jnp.max(scores[i], -1, keepdims=True)
        expo = jnp.exp(scores[i] - top)
        expos[i] = expo.astype(BF16)
        tops[i] = jnp.broadcast_to(top, lane.shape)
        sums[i] = jnp.broadcast_to(jnp.sum(expo, -1, keepdims=True), lane.shape)
    for i in range(devices * PAIR):
        vector = jnp.dot(expos[i], kv[spots[i], 0, :, head_dim:], preferred_element_type=F32)
        at = (i % PAIR) * per_row
        back[i // PAIR, at : at + per_row, :] = (vector / sums[i]).astype(BF16)
    pack_statistics(tops, sums, back)
    rows, steps, width = x.shape
    tokens = rows * steps
    floats = x[...].reshape(tokens, width).astype(F32)
    inverse = lax.rsqrt(jnp.mean(floats * floats, -1, keepdims=True) + EPSILON)
    normed[...] = (floats * inverse * gain[...]).astype(BF16)
    repeat = tokens // per_row
    cosine, sine = (jnp.concatenate([tables[i]] * repeat, 0) for i in range(2))
    keys = jnp.dot(normed[...], wk[...], preferred_element_type=F32)
    keys = (keys * cosine + pltpu.roll(keys, head_dim // 2, 1) * sine).astype(BF16)
    vals = jnp.dot(normed[...], wv[...], preferred_element_type=F32).astype(BF16)
    flat = queries[...].reshape(rows * per_row, head_dim)
    fresh = lax.dot_general(flat, keys, NT, preferred_element_type=F32) * head_dim ** (-0.5)
    row = lax.broadcasted_iota(jnp.int32, fresh.shape, 0)
    col = lax.broadcasted_iota(jnp.int32, fresh.shape, 1)
    seen = (lax.div(row, per_row) == lax.div(col, steps)) & (lax.rem(col, steps) <= lax.rem(row, steps))
    top = jnp.max(jnp.where(seen, fresh, -jnp.inf), -1, keepdims=True)
    expo = jnp.where(seen, jnp.exp(jnp.where(seen, fresh - top, 0.0)), 0.0)
    vec[...] = jnp.dot(expo.astype(BF16), vals, preferred_element_type=F32)
    stat[0] = jnp.broadcast_to(top, stat.shape[1:])
    stat[1] = jnp.broadcast_to(jnp.sum(expo, -1, keepdims=True), stat.shape[1:])


def units(own):
    index = lax.axis_index("tensor")
    y, core = lax.div(index, 2), lax.rem(index, 2)
    core = core if own else 1 - core
    return [2 * lax.bitwise_xor(y, k) + core for k in (*PARTNERS, 0)]


def product(wide, w, block, tokens, column):
    at = pl.multiple_of(block * column, column)
    return jnp.dot(wide, w[:, pl.ds(at, column)], preferred_element_type=F32)[:tokens]


def widen(heads):
    return jnp.concatenate([heads[...]] * max(1, 128 // heads.shape[0]), 0)


def project(heads, w, out, own):
    away, tokens, column = out.shape
    wide = widen(heads)
    for k, block in enumerate(units(own)[:away]):
        out[k] = product(wide, w, block, tokens, column).astype(BF16)


def merge_kernel(anc, recv, vec, stat, w, out, heads, grid_ref, sums, lined, count):
    devices, chunk, head_dim = recv.shape
    per_row = (chunk - MORE) // PAIR
    rows = vec.shape[0] // per_row
    steps = heads.shape[0] // rows
    pieces = per_row // MORE
    quarter = head_dim // (PAIR * pieces)
    for d in range(devices):
        count[d] = 0
    part_of = lax.div(lax.broadcasted_iota(jnp.int32, (MORE, head_dim), 1), quarter)
    for r in range(rows):
        source, rank = slot_of(anc, r, rows, count)
        at = pl.multiple_of(rank * per_row, per_row)
        grid_ref[pl.ds(r * per_row, per_row), :] = recv[source, pl.ds(at, per_row), :].astype(F32)
        parts = recv[source, PAIR * per_row :, :].astype(F32)
        sums[pl.ds(r * per_row, per_row), :] = jnp.concatenate(
            [jnp.where(part_of == rank * pieces + g, parts, 0.0) for g in range(pieces)], 0
        ).astype(BF16)
    lane_from = lax.rem(lax.broadcasted_iota(jnp.int32, (head_dim, 2 * head_dim), 0), quarter)
    lane_to = lax.broadcasted_iota(jnp.int32, (head_dim, 2 * head_dim), 1)
    first = jnp.where(lane_from < 3, 1.0, 0.0)
    second = jnp.where((lane_from >= 3) & (lane_from < 5), 1.0, 0.0)
    spread = jnp.where(lane_to < head_dim, first, second)
    both = jnp.dot(sums[...], spread.astype(BF16), preferred_element_type=F32)
    top_c, sum_c = both[:, :head_dim], both[:, head_dim:]
    top_f, sum_f = stat[0], stat[1]
    top = jnp.maximum(top_c, top_f)
    factor_c = sum_c * jnp.exp(top_c - top)
    factor_f = jnp.exp(top_f - top)
    share = 1.0 / (factor_c + sum_f * factor_f)
    grid_ref[...] = (grid_ref[...] * factor_c + vec[...] * factor_f) * share
    for h in range(per_row // steps):
        for s in range(steps):
            lined[h, pl.ds(s, rows, stride=steps), :] = grid_ref[pl.ds(h * steps + s, rows, stride=per_row), :]
        heads[:, pl.ds(h * head_dim, head_dim)] = lined[h].astype(BF16)
    project(heads, w, out, False)


def second_kernel(heads, w, out):
    project(heads, w, out, True)


def add_kernel(mine, given, *outs):
    for k, out in enumerate(outs):
        out[...] = (mine[k].astype(F32) + given[k].astype(F32)).astype(BF16)


def last_kernel(heads, w, arrived, keep, crossing):
    tokens, column = keep.shape
    wide = widen(heads)
    crossing[...] = product(wide, w, units(False)[-1], tokens, column).astype(BF16)
    keep[...] = product(wide, w, units(True)[-1], tokens, column) + arrived[...].astype(F32)


def shards(inputs, norm_gain, query_proj, w_key, w_value, w_out, kv_cache, ancestors):
    rows, steps, width = inputs.shape
    context = kv_cache.shape[2]
    head_dim = kv_cache.shape[3] // 2
    local = query_proj.shape[2]
    heads = local // head_dim
    per_row = heads * steps
    devices = lax.axis_size("particle")
    tensor = lax.axis_size("tensor")
    column = width // tensor
    cosine, sine = rotary_tables(context, steps, head_dim)
    tables = np.stack([np.tile(cosine, (heads, 1)), np.tile(sine, (heads, 1))])
    smem = pl.BlockSpec(memory_space=pltpu.SMEM)
    vmem = pl.BlockSpec(memory_space=pltpu.VMEM)
    stay = pl.BlockSpec(memory_space=pl.ANY)
    hbm = lambda x: pltpu.with_memory_space_constraint(x, pltpu.HBM)
    tables = jnp.asarray(tables)

    packed = (devices, PAIR * per_row + MORE, head_dim)
    send, queries, tables, gain = pl.pallas_call(
        pack_kernel,
        out_shape=(
            jax.ShapeDtypeStruct(packed, BF16),
            jax.ShapeDtypeStruct((rows, per_row, head_dim), BF16),
            jax.ShapeDtypeStruct((2, per_row, head_dim), F32),
            jax.ShapeDtypeStruct((1, width), F32),
        ),
        in_specs=[stay] * 4,
        out_specs=(vmem,) * 4,
        scratch_shapes=[
            pltpu.VMEM((rows, per_row, head_dim), F32),
            pltpu.VMEM((rows, steps, local), BF16),
            pltpu.SMEM((rows,), jnp.int32),
            pltpu.SMEM((devices,), jnp.int32),
            pltpu.SMEM((devices * PAIR,), jnp.int32),
            pltpu.SemaphoreType.DMA((4,)),
        ],
        compiler_params=pltpu.CompilerParams(vmem_limit_bytes=4 * MIB),
        cost_estimate=pl.CostEstimate(flops=10_000_000_000, bytes_accessed=MIB, transcendentals=0),
        name="pack_queries",
    )(hbm(ancestors), hbm(query_proj), hbm(tables), hbm(norm_gain.reshape(1, width)))

    recv = lax.all_to_all(send, "particle", split_axis=0, concat_axis=0, tiled=True)

    slots = devices * PAIR
    back, vec, stat = pl.pallas_call(
        attend_kernel,
        out_shape=(
            jax.ShapeDtypeStruct(packed, BF16),
            jax.ShapeDtypeStruct((rows * per_row, head_dim), F32),
            jax.ShapeDtypeStruct((2, rows * per_row, head_dim), F32),
        ),
        in_specs=[vmem] * 8,
        out_specs=(vmem,) * 3,
        scratch_shapes=[
            pltpu.VMEM((slots, per_row, context), F32),
            pltpu.VMEM((slots, per_row, context), BF16),
            pltpu.VMEM((slots, per_row, head_dim), F32),
            pltpu.VMEM((slots, per_row, head_dim), F32),
            pltpu.VMEM((rows * steps, width), BF16),
        ],
        compiler_params=pltpu.CompilerParams(vmem_limit_bytes=12 * MIB),
        cost_estimate=pl.CostEstimate(
            flops=10_000_000_000, bytes_accessed=5 * MIB, transcendentals=0
        ),
        name="attention",
    )(
        recv,
        kv_cache,
        inputs,
        gain,
        w_key,
        w_value,
        queries,
        tables,
    )
    home = lax.all_to_all(back, "particle", split_axis=0, concat_axis=0, tiled=True)

    away = len(PARTNERS)
    block = jax.ShapeDtypeStruct((away, rows * steps, column), BF16)
    one = jax.ShapeDtypeStruct((rows * steps, column), BF16)
    params = pltpu.CompilerParams(vmem_limit_bytes=8 * MIB)
    cost = pl.CostEstimate(
        flops=rows * steps * local * width, bytes_accessed=local * width, transcendentals=0
    )
    other, heads_out = pl.pallas_call(
        merge_kernel,
        out_shape=(
            block,
            jax.ShapeDtypeStruct((rows * steps, local), BF16),
        ),
        in_specs=[smem, vmem, vmem, vmem, vmem],
        out_specs=(vmem, vmem),
        scratch_shapes=[
            pltpu.VMEM((rows * per_row, head_dim), F32),
            pltpu.VMEM((rows * per_row, head_dim), BF16),
            pltpu.VMEM((heads, rows * steps, head_dim), F32),
            pltpu.SMEM((devices,), jnp.int32),
        ],
        compiler_params=params,
        cost_estimate=cost,
        name="merge_project_sibling",
    )(ancestors, home, vec, stat, w_out)
    sibling = [(i, i ^ 1) for i in range(tensor)]
    given = lax.ppermute(other, "tensor", sibling)
    mine = pl.pallas_call(
        second_kernel,
        out_shape=block,
        in_specs=[vmem, vmem],
        out_specs=vmem,
        compiler_params=params,
        cost_estimate=cost,
        name="project_own",
    )(heads_out, w_out)
    pair = pl.pallas_call(
        add_kernel,
        out_shape=(one,) * away,
        in_specs=[vmem, vmem],
        out_specs=(vmem,) * away,
        compiler_params=params,
        name="add_sibling",
    )(mine, given)
    arrived = []
    for part, k in zip(pair, PARTNERS):
        exchange = [(i, ((i // 2) ^ k) * 2 + i % 2) for i in range(tensor)]
        arrived.append(lax.ppermute(part, "tensor", exchange))
    keep, crossing = pl.pallas_call(
        last_kernel,
        out_shape=(jax.ShapeDtypeStruct(one.shape, F32), one),
        in_specs=[vmem, vmem, vmem],
        out_specs=(vmem, vmem),
        compiler_params=params,
        cost_estimate=cost,
        name="project_last",
    )(heads_out, w_out, arrived[0])
    total = keep + lax.ppermute(crossing, "tensor", sibling).astype(F32)
    for part in arrived[1:]:
        total = total + part.astype(F32)
    return total.astype(BF16).reshape(rows, steps, column)


def solution(mesh):
    in_specs = (
        P("particle", None, None),
        P(),
        P("particle", None, "tensor"),
        P(None, "tensor"),
        P(None, "tensor"),
        P("tensor", None),
        P("particle", "tensor", None, None),
        P("particle"),
    )
    out_specs = P("particle", None, "tensor")
    return jax.shard_map(shards, mesh=mesh, in_specs=in_specs, out_specs=out_specs, check_vma=False)
```

```python
import jax
import jax.numpy as jnp
import numpy as np
from jax import lax
from jax.experimental import pallas as pl
from jax.experimental.pallas import tpu as pltpu
from jax.sharding import PartitionSpec as P

PAIR = 2
MORE = 8
THETA = 500000.0
EPSILON = 1e-05
F32 = jnp.float32
BF16 = jnp.bfloat16
MIB = 1 << 20
NT = (((1,), (1,)), ((), ()))


def rotary_tables(context, steps, head_dim):
    half = head_dim // 2
    freqs = np.float32(THETA) ** (-np.arange(half, dtype=np.float32) * np.float32(2.0) / np.float32(head_dim))
    position = (np.float32(context) + np.arange(steps, dtype=np.float32)).reshape(steps, 1)
    angles = (position * freqs.astype(np.float32)).astype(np.float32)
    cosine, sine = np.cos(angles), np.sin(angles)
    return (
        np.concatenate([cosine, cosine], 1).astype(np.float32),
        np.concatenate([-sine, sine], 1).astype(np.float32),
    )


def slot_of(anc, row, rows, count):
    source = lax.div(anc[row], rows)
    rank = count[source]
    count[source] = rank + 1
    return source, rank


def pack_kernel(
    anc_hbm, qp_hbm, tables_hbm, gain_hbm, send, queries, tables, gain, grid_ref, qp, anc, count, spots, sems
):
    pairs = ((anc_hbm, anc), (qp_hbm, qp), (tables_hbm, tables), (gain_hbm, gain))
    copies = [pltpu.make_async_copy(src, dst, sems.at[i]) for i, (src, dst) in enumerate(pairs)]
    for copy in copies:
        copy.start()
    rows, steps, width = qp.shape
    _, per_row, head_dim = tables.shape
    devices = send.shape[0]

    def clear(d, _):
        send[d] = jnp.zeros(send.shape[1:], BF16)
        count[d] = 0
        for j in range(PAIR):
            spots[PAIR * d + j] = 0
        return 0

    lax.fori_loop(0, devices, clear, 0)
    for copy in copies:
        copy.wait()
    for h in range(width // head_dim):
        grid_ref[:, steps * h : steps * (h + 1), :] = qp[:, :, head_dim * h : head_dim * (h + 1)].astype(F32)
    for r in range(rows):
        source, rank = slot_of(anc, r, rows, count)
        spots[source * PAIR + rank] = lax.rem(anc[r], rows)
        plain = grid_ref[r]
        turned = (plain * tables[0] + pltpu.roll(plain, head_dim // 2, 1) * tables[1]).astype(BF16)
        queries[r] = turned
        send[source, pl.ds(pl.multiple_of(rank * per_row, per_row), per_row), :] = turned
    lane = lax.broadcasted_iota(jnp.int32, (MORE, head_dim), 1)
    for d in range(devices):
        send[d, PAIR * per_row :, :] = jnp.where(
            lane < head_dim // PAIR, spots[PAIR * d].astype(F32), spots[PAIR * d + 1].astype(F32)
        ).astype(BF16)


def slot_rows(chunks, i, per_row):
    at = (i % PAIR) * per_row
    return chunks[i // PAIR, at : at + per_row, :]


def pack_statistics(tops, sums, back):
    devices, _, head_dim = back.shape
    per_row = tops.shape[1]
    lane = lax.broadcasted_iota(jnp.int32, (MORE, head_dim), 1)
    quarter = head_dim * MORE // (PAIR * per_row)
    for d in range(devices):
        stat = jnp.zeros(lane.shape, F32)
        for j in range(PAIR):
            i = d * PAIR + j
            for g in range(per_row // MORE):
                at_lane = (j * (per_row // MORE) + g) * quarter
                for source, parts in ((tops, 3), (sums, 2)):
                    value = source[i, g * MORE : (g + 1) * MORE, :]
                    for _ in range(parts):
                        part = value.astype(BF16).astype(F32)
                        stat = jnp.where(lane == at_lane, part, stat)
                        value = value - part
                        at_lane += 1
        back[d, PAIR * per_row :, :] = stat.astype(BF16)


def attend_kernel(
    recv, kv, x, gain, wk, wv, queries, tables, back, vec, stat, *scratch
):
    scores, expos, tops, sums, normed = scratch
    devices, _, head_dim = recv.shape
    per_row = queries.shape[1]
    lane = lax.broadcasted_iota(jnp.int32, (per_row, head_dim), 1)
    spots = []
    for d in range(devices):
        spot = recv[d, PAIR * per_row :, :].astype(F32)
        for j in range(PAIR):
            spots.append(spot[0, j * (head_dim // PAIR)].astype(jnp.int32))
    for i in range(devices * PAIR):
        scores[i] = lax.dot_general(
            slot_rows(recv, i, per_row), kv[spots[i], 0, :, :head_dim], NT, preferred_element_type=F32
        ) * head_dim ** (-0.5)
    for i in range(devices * PAIR):
        top = jnp.max(scores[i], -1, keepdims=True)
        expo = jnp.exp(scores[i] - top)
        expos[i] = expo.astype(BF16)
        tops[i] = jnp.broadcast_to(top, lane.shape)
        sums[i] = jnp.broadcast_to(jnp.sum(expo, -1, keepdims=True), lane.shape)
    for i in range(devices * PAIR):
        vector = jnp.dot(expos[i], kv[spots[i], 0, :, head_dim:], preferred_element_type=F32)
        at = (i % PAIR) * per_row
        back[i // PAIR, at : at + per_row, :] = (vector / sums[i]).astype(BF16)
    pack_statistics(tops, sums, back)
    rows, steps, width = x.shape
    tokens = rows * steps
    floats = x[...].reshape(tokens, width).astype(F32)
    inverse = lax.rsqrt(jnp.mean(floats * floats, -1, keepdims=True) + EPSILON)
    normed[...] = (floats * inverse * gain[...]).astype(BF16)
    repeat = tokens // per_row
    cosine, sine = (jnp.concatenate([tables[i]] * repeat, 0) for i in range(2))
    keys = jnp.dot(normed[...], wk[...], preferred_element_type=F32)
    keys = (keys * cosine + pltpu.roll(keys, head_dim // 2, 1) * sine).astype(BF16)
    vals = jnp.dot(normed[...], wv[...], preferred_element_type=F32).astype(BF16)
    flat = queries[...].reshape(rows * per_row, head_dim)
    fresh = lax.dot_general(flat, keys, NT, preferred_element_type=F32) * head_dim ** (-0.5)
    row = lax.broadcasted_iota(jnp.int32, fresh.shape, 0)
    col = lax.broadcasted_iota(jnp.int32, fresh.shape, 1)
    seen = (lax.div(row, per_row) == lax.div(col, steps)) & (lax.rem(col, steps) <= lax.rem(row, steps))
    top = jnp.max(jnp.where(seen, fresh, -jnp.inf), -1, keepdims=True)
    expo = jnp.where(seen, jnp.exp(jnp.where(seen, fresh - top, 0.0)), 0.0)
    vec[...] = jnp.dot(expo.astype(BF16), vals, preferred_element_type=F32)
    stat[0] = jnp.broadcast_to(top, stat.shape[1:])
    stat[1] = jnp.broadcast_to(jnp.sum(expo, -1, keepdims=True), stat.shape[1:])


def units(own):
    index = lax.axis_index("tensor")
    y, core = lax.div(index, 2), lax.rem(index, 2)
    core = core if own else 1 - core
    served = lax.bitwise_xor(y, 2 + core)
    return 2 * served + core, 2 * served + 1 - core, 2 * lax.bitwise_xor(y, 1) + core, 2 * y + core


def product(wide, w, block, tokens, column):
    at = pl.multiple_of(block * column, column)
    return jnp.dot(wide, w[:, pl.ds(at, column)], preferred_element_type=F32)[:tokens]


def widen(heads):
    return jnp.concatenate([heads[...]] * max(1, 128 // heads.shape[0]), 0)


def project(heads, w, out, own):
    away, tokens, column = out.shape
    wide = widen(heads)
    for k, block in enumerate(units(own)[:away]):
        out[k] = product(wide, w, block, tokens, column).astype(BF16)


def merge_kernel(anc, recv, vec, stat, w, out, heads, grid_ref, sums, lined, count):
    devices, chunk, head_dim = recv.shape
    per_row = (chunk - MORE) // PAIR
    rows = vec.shape[0] // per_row
    steps = heads.shape[0] // rows
    pieces = per_row // MORE
    quarter = head_dim // (PAIR * pieces)
    for d in range(devices):
        count[d] = 0
    part_of = lax.div(lax.broadcasted_iota(jnp.int32, (MORE, head_dim), 1), quarter)
    for r in range(rows):
        source, rank = slot_of(anc, r, rows, count)
        at = pl.multiple_of(rank * per_row, per_row)
        grid_ref[pl.ds(r * per_row, per_row), :] = recv[source, pl.ds(at, per_row), :].astype(F32)
        parts = recv[source, PAIR * per_row :, :].astype(F32)
        sums[pl.ds(r * per_row, per_row), :] = jnp.concatenate(
            [jnp.where(part_of == rank * pieces + g, parts, 0.0) for g in range(pieces)], 0
        ).astype(BF16)
    lane_from = lax.rem(lax.broadcasted_iota(jnp.int32, (head_dim, 2 * head_dim), 0), quarter)
    lane_to = lax.broadcasted_iota(jnp.int32, (head_dim, 2 * head_dim), 1)
    first = jnp.where(lane_from < 3, 1.0, 0.0)
    second = jnp.where((lane_from >= 3) & (lane_from < 5), 1.0, 0.0)
    spread = jnp.where(lane_to < head_dim, first, second)
    both = jnp.dot(sums[...], spread.astype(BF16), preferred_element_type=F32)
    top_c, sum_c = both[:, :head_dim], both[:, head_dim:]
    top_f, sum_f = stat[0], stat[1]
    top = jnp.maximum(top_c, top_f)
    factor_c = sum_c * jnp.exp(top_c - top)
    factor_f = jnp.exp(top_f - top)
    share = 1.0 / (factor_c + sum_f * factor_f)
    grid_ref[...] = (grid_ref[...] * factor_c + vec[...] * factor_f) * share
    for h in range(per_row // steps):
        for s in range(steps):
            lined[h, pl.ds(s, rows, stride=steps), :] = grid_ref[pl.ds(h * steps + s, rows, stride=per_row), :]
        heads[:, pl.ds(h * head_dim, head_dim)] = lined[h].astype(BF16)
    project(heads, w, out, False)


def second_kernel(heads, w, out):
    project(heads, w, out, True)


def add_kernel(mine, given, served, near):
    served[...] = (mine[:2].astype(F32) + given[:2].astype(F32)).astype(BF16)
    near[...] = (mine[2].astype(F32) + given[2].astype(F32)).astype(BF16)


def last_kernel(heads, w, arrived, keep, crossing):
    tokens, column = keep.shape
    wide = widen(heads)
    crossing[...] = (
        product(wide, w, units(False)[-1], tokens, column) + arrived[1].astype(F32)
    ).astype(BF16)
    keep[...] = product(wide, w, units(True)[-1], tokens, column) + arrived[0].astype(F32)


def shards(inputs, norm_gain, query_proj, w_key, w_value, w_out, kv_cache, ancestors):
    rows, steps, width = inputs.shape
    context = kv_cache.shape[2]
    head_dim = kv_cache.shape[3] // 2
    local = query_proj.shape[2]
    heads = local // head_dim
    per_row = heads * steps
    devices = lax.axis_size("particle")
    tensor = lax.axis_size("tensor")
    column = width // tensor
    cosine, sine = rotary_tables(context, steps, head_dim)
    tables = np.stack([np.tile(cosine, (heads, 1)), np.tile(sine, (heads, 1))])
    smem = pl.BlockSpec(memory_space=pltpu.SMEM)
    vmem = pl.BlockSpec(memory_space=pltpu.VMEM)
    stay = pl.BlockSpec(memory_space=pl.ANY)
    hbm = lambda x: pltpu.with_memory_space_constraint(x, pltpu.HBM)
    tables = jnp.asarray(tables)

    packed = (devices, PAIR * per_row + MORE, head_dim)
    send, queries, tables, gain = pl.pallas_call(
        pack_kernel,
        out_shape=(
            jax.ShapeDtypeStruct(packed, BF16),
            jax.ShapeDtypeStruct((rows, per_row, head_dim), BF16),
            jax.ShapeDtypeStruct((2, per_row, head_dim), F32),
            jax.ShapeDtypeStruct((1, width), F32),
        ),
        in_specs=[stay] * 4,
        out_specs=(vmem,) * 4,
        scratch_shapes=[
            pltpu.VMEM((rows, per_row, head_dim), F32),
            pltpu.VMEM((rows, steps, local), BF16),
            pltpu.SMEM((rows,), jnp.int32),
            pltpu.SMEM((devices,), jnp.int32),
            pltpu.SMEM((devices * PAIR,), jnp.int32),
            pltpu.SemaphoreType.DMA((4,)),
        ],
        compiler_params=pltpu.CompilerParams(vmem_limit_bytes=4 * MIB),
        cost_estimate=pl.CostEstimate(flops=10_000_000_000, bytes_accessed=MIB, transcendentals=0),
        name="pack_queries",
    )(hbm(ancestors), hbm(query_proj), hbm(tables), hbm(norm_gain.reshape(1, width)))

    recv = lax.all_to_all(send, "particle", split_axis=0, concat_axis=0, tiled=True)

    slots = devices * PAIR
    back, vec, stat = pl.pallas_call(
        attend_kernel,
        out_shape=(
            jax.ShapeDtypeStruct(packed, BF16),
            jax.ShapeDtypeStruct((rows * per_row, head_dim), F32),
            jax.ShapeDtypeStruct((2, rows * per_row, head_dim), F32),
        ),
        in_specs=[vmem] * 8,
        out_specs=(vmem,) * 3,
        scratch_shapes=[
            pltpu.VMEM((slots, per_row, context), F32),
            pltpu.VMEM((slots, per_row, context), BF16),
            pltpu.VMEM((slots, per_row, head_dim), F32),
            pltpu.VMEM((slots, per_row, head_dim), F32),
            pltpu.VMEM((rows * steps, width), BF16),
        ],
        compiler_params=pltpu.CompilerParams(vmem_limit_bytes=12 * MIB),
        cost_estimate=pl.CostEstimate(
            flops=10_000_000_000, bytes_accessed=5 * MIB, transcendentals=0
        ),
        name="attention",
    )(
        recv,
        kv_cache,
        inputs,
        gain,
        w_key,
        w_value,
        queries,
        tables,
    )
    home = lax.all_to_all(back, "particle", split_axis=0, concat_axis=0, tiled=True)

    block = jax.ShapeDtypeStruct((3, rows * steps, column), BF16)
    one = jax.ShapeDtypeStruct((rows * steps, column), BF16)
    params = pltpu.CompilerParams(vmem_limit_bytes=8 * MIB)
    cost = pl.CostEstimate(
        flops=rows * steps * local * width, bytes_accessed=local * width, transcendentals=0
    )
    other, heads_out = pl.pallas_call(
        merge_kernel,
        out_shape=(
            block,
            jax.ShapeDtypeStruct((rows * steps, local), BF16),
        ),
        in_specs=[smem, vmem, vmem, vmem, vmem],
        out_specs=(vmem, vmem),
        scratch_shapes=[
            pltpu.VMEM((rows * per_row, head_dim), F32),
            pltpu.VMEM((rows * per_row, head_dim), BF16),
            pltpu.VMEM((heads, rows * steps, head_dim), F32),
            pltpu.SMEM((devices,), jnp.int32),
        ],
        compiler_params=params,
        cost_estimate=cost,
        name="merge_project_sibling",
    )(ancestors, home, vec, stat, w_out)
    sibling = [(i, i ^ 1) for i in range(tensor)]
    given = lax.ppermute(other, "tensor", sibling)
    mine = pl.pallas_call(
        second_kernel,
        out_shape=block,
        in_specs=[vmem, vmem],
        out_specs=vmem,
        compiler_params=params,
        cost_estimate=cost,
        name="project_own",
    )(heads_out, w_out)
    served, near = pl.pallas_call(
        add_kernel,
        out_shape=(jax.ShapeDtypeStruct((2, *one.shape), BF16), one),
        in_specs=[vmem, vmem],
        out_specs=(vmem, vmem),
        compiler_params=params,
        name="add_sibling",
    )(mine, given)
    arrived = lax.ppermute(served, "tensor", [(i, ((i // 2) ^ (2 + i % 2)) * 2 + i % 2) for i in range(tensor)])
    from_near = lax.ppermute(near, "tensor", [(i, i ^ 2) for i in range(tensor)])
    keep, crossing = pl.pallas_call(
        last_kernel,
        out_shape=(jax.ShapeDtypeStruct(one.shape, F32), one),
        in_specs=[vmem, vmem, vmem],
        out_specs=(vmem, vmem),
        compiler_params=params,
        cost_estimate=cost,
        name="project_last",
    )(heads_out, w_out, arrived)
    total = keep + from_near.astype(F32) + lax.ppermute(crossing, "tensor", sibling).astype(F32)
    return total.astype(BF16).reshape(rows, steps, column)


def solution(mesh):
    in_specs = (
        P("particle", None, None),
        P(),
        P("particle", None, "tensor"),
        P(None, "tensor"),
        P(None, "tensor"),
        P("tensor", None),
        P("particle", "tensor", None, None),
        P("particle"),
    )
    out_specs = P("particle", None, "tensor")
    return jax.shard_map(shards, mesh=mesh, in_specs=in_specs, out_specs=out_specs, check_vma=False)
```

```python
import jax
import jax.numpy as jnp
import numpy as np
from jax import lax
from jax.experimental import pallas as pl
from jax.experimental.pallas import tpu as pltpu
from jax.sharding import PartitionSpec as P

PAIR = 2
MORE = 8
THETA = 500000.0
EPSILON = 1e-05
F32 = jnp.float32
BF16 = jnp.bfloat16
MIB = 1 << 20
NT = (((1,), (1,)), ((), ()))


def rotary_tables(context, steps, head_dim):
    half = head_dim // 2
    freqs = np.float32(THETA) ** (-np.arange(half, dtype=np.float32) * np.float32(2.0) / np.float32(head_dim))
    position = (np.float32(context) + np.arange(steps, dtype=np.float32)).reshape(steps, 1)
    angles = (position * freqs.astype(np.float32)).astype(np.float32)
    cosine, sine = np.cos(angles), np.sin(angles)
    return (
        np.concatenate([cosine, cosine], 1).astype(np.float32),
        np.concatenate([-sine, sine], 1).astype(np.float32),
    )


def slot_of(anc, row, rows, count):
    source = lax.div(anc[row], rows)
    rank = count[source]
    count[source] = rank + 1
    return source, rank


def pack_kernel(
    anc_hbm, qp_hbm, tables_hbm, gain_hbm, send, queries, tables, gain, grid_ref, qp, anc, count, spots, sems
):
    pairs = ((anc_hbm, anc), (qp_hbm, qp), (tables_hbm, tables), (gain_hbm, gain))
    copies = [pltpu.make_async_copy(src, dst, sems.at[i]) for i, (src, dst) in enumerate(pairs)]
    for copy in copies:
        copy.start()
    rows, steps, width = qp.shape
    _, per_row, head_dim = tables.shape
    devices = send.shape[0]

    def clear(d, _):
        send[d] = jnp.zeros(send.shape[1:], BF16)
        count[d] = 0
        for j in range(PAIR):
            spots[PAIR * d + j] = -1
        return 0

    lax.fori_loop(0, devices, clear, 0)
    for copy in copies:
        copy.wait()
    for h in range(width // head_dim):
        grid_ref[:, steps * h : steps * (h + 1), :] = qp[:, :, head_dim * h : head_dim * (h + 1)].astype(F32)
    for r in range(rows):
        source, rank = slot_of(anc, r, rows, count)
        spots[source * PAIR + rank] = lax.rem(anc[r], rows)
        plain = grid_ref[r]
        turned = (plain * tables[0] + pltpu.roll(plain, head_dim // 2, 1) * tables[1]).astype(BF16)
        queries[r] = turned
        send[source, pl.ds(pl.multiple_of(rank * per_row, per_row), per_row), :] = turned
    lane = lax.broadcasted_iota(jnp.int32, (MORE, head_dim), 1)
    for d in range(devices):
        send[d, PAIR * per_row :, :] = jnp.where(
            lane < head_dim // PAIR, spots[PAIR * d].astype(F32), spots[PAIR * d + 1].astype(F32)
        ).astype(BF16)


def pack_statistics(tops, sums, places, back):
    devices, _, head_dim = back.shape
    per_row = tops.shape[1]
    pieces = per_row // MORE
    lane = lax.broadcasted_iota(jnp.int32, (MORE, head_dim), 1)
    quarter = head_dim // (PAIR * pieces)
    piece_of, is_top, part_of = lax.div(lane, quarter), lax.rem(lane, quarter) < 4, lax.rem(lane, 4)
    for d in range(devices):
        value = jnp.zeros(lane.shape, F32)
        for j in range(PAIR):
            place = places[d * PAIR + j]
            for g in range(pieces):
                at = slice(g * MORE, (g + 1) * MORE)
                both = jnp.where(is_top, tops[place, at, :], sums[place, at, :])
                value = jnp.where(piece_of == j * pieces + g, both, value)
        first = value.astype(BF16).astype(F32)
        second = (value - first).astype(BF16).astype(F32)
        third = value - first - second
        back[d, PAIR * per_row :, :] = jnp.where(
            part_of == 0, first, jnp.where(part_of == 1, second, third)
        ).astype(BF16)


def attend_kernel(
    recv, kv, x, gain, wk, wv, queries, tables, back, vec, stat, *scratch
):
    scores, expos, tops, sums, vectors, normed, chosen, row_of = scratch
    devices, _, head_dim = recv.shape
    per_row = queries.shape[1]
    lane = lax.broadcasted_iota(jnp.int32, (per_row, head_dim), 1)
    slots = devices * PAIR
    for k in range(slots):
        chosen[k] = 0
        row_of[k] = 0
    used = jnp.int32(0)
    places = []
    for d in range(devices):
        spot = recv[d, PAIR * per_row :, :].astype(F32)
        for j in range(PAIR):
            row = spot[0, j * (head_dim // PAIR)].astype(jnp.int32)
            chosen[used] = d * PAIR + j
            row_of[used] = jnp.maximum(row, 0)
            places.append(used)
            used = used + jnp.where(row >= 0, 1, 0)

    def cached(first, last):
        for k in range(first, last):
            d, j = lax.div(chosen[k], PAIR), lax.rem(chosen[k], PAIR)
            asked = recv[d, pl.ds(pl.multiple_of(j * per_row, per_row), per_row), :]
            scores[k] = lax.dot_general(
                asked, kv[row_of[k], 0, :, :head_dim], NT, preferred_element_type=F32
            ) * head_dim ** (-0.5)
        for k in range(first, last):
            top = jnp.max(scores[k], -1, keepdims=True)
            expo = jnp.exp(scores[k] - top)
            expos[k] = expo.astype(BF16)
            tops[k] = jnp.broadcast_to(top, lane.shape)
            sums[k] = jnp.broadcast_to(jnp.sum(expo, -1, keepdims=True), lane.shape)
        for k in range(first, last):
            vector = jnp.dot(expos[k], kv[row_of[k], 0, :, head_dim:], preferred_element_type=F32)
            vectors[k] = (vector / sums[k]).astype(BF16)

    most = slots * 3 // 4
    cached(0, most)
    rows, steps, width = x.shape
    tokens = rows * steps
    floats = x[...].reshape(tokens, width).astype(F32)
    inverse = lax.rsqrt(jnp.mean(floats * floats, -1, keepdims=True) + EPSILON)
    normed[...] = (floats * inverse * gain[...]).astype(BF16)
    repeat = tokens // per_row
    cosine, sine = (jnp.concatenate([tables[i]] * repeat, 0) for i in range(2))
    keys = jnp.dot(normed[...], wk[...], preferred_element_type=F32)
    keys = (keys * cosine + pltpu.roll(keys, head_dim // 2, 1) * sine).astype(BF16)
    vals = jnp.dot(normed[...], wv[...], preferred_element_type=F32).astype(BF16)
    flat = queries[...].reshape(rows * per_row, head_dim)
    fresh = lax.dot_general(flat, keys, NT, preferred_element_type=F32) * head_dim ** (-0.5)
    row = lax.broadcasted_iota(jnp.int32, fresh.shape, 0)
    col = lax.broadcasted_iota(jnp.int32, fresh.shape, 1)
    seen = (lax.div(row, per_row) == lax.div(col, steps)) & (lax.rem(col, steps) <= lax.rem(row, steps))
    top = jnp.max(jnp.where(seen, fresh, -jnp.inf), -1, keepdims=True)
    expo = jnp.where(seen, jnp.exp(jnp.where(seen, fresh - top, 0.0)), 0.0)
    vec[...] = jnp.dot(expo.astype(BF16), vals, preferred_element_type=F32)
    stat[0] = jnp.broadcast_to(top, stat.shape[1:])
    stat[1] = jnp.broadcast_to(jnp.sum(expo, -1, keepdims=True), stat.shape[1:])

    @pl.when(used > most)
    def _():
        cached(most, slots)

    for i in range(slots):
        at = (i % PAIR) * per_row
        back[i // PAIR, at : at + per_row, :] = vectors[places[i]]
    pack_statistics(tops, sums, places, back)


def units(own, groups):
    index = lax.axis_index("tensor")
    y, core = lax.div(index, 2), lax.rem(index, 2)
    core = core if own else 1 - core
    return [2 * lax.rem(y + k, groups) + core for k in (*range(1, groups), 0)]


def product(wide, w, block, tokens, column):
    at = pl.multiple_of(block * column, column)
    return jnp.dot(wide, w[:, pl.ds(at, column)], preferred_element_type=F32)[:tokens]


def widen(heads):
    return jnp.concatenate([heads[...]] * max(1, 128 // heads.shape[0]), 0)


def project(heads, w, out, own):
    away, tokens, column = out.shape
    wide = widen(heads)
    for k, block in enumerate(units(own, away + 1)[:away]):
        out[k] = product(wide, w, block, tokens, column).astype(BF16)


def merge_kernel(anc, recv, vec, stat, w, out, heads, grid_ref, sums, lined, count):
    devices, chunk, head_dim = recv.shape
    per_row = (chunk - MORE) // PAIR
    rows = vec.shape[0] // per_row
    steps = heads.shape[0] // rows
    pieces = per_row // MORE
    quarter = head_dim // (PAIR * pieces)
    for d in range(devices):
        count[d] = 0
    part_of = lax.div(lax.broadcasted_iota(jnp.int32, (MORE, head_dim), 1), quarter)
    for r in range(rows):
        source, rank = slot_of(anc, r, rows, count)
        at = pl.multiple_of(rank * per_row, per_row)
        grid_ref[pl.ds(r * per_row, per_row), :] = recv[source, pl.ds(at, per_row), :].astype(F32)
        parts = recv[source, PAIR * per_row :, :].astype(F32)
        sums[pl.ds(r * per_row, per_row), :] = jnp.concatenate(
            [jnp.where(part_of == rank * pieces + g, parts, 0.0) for g in range(pieces)], 0
        ).astype(BF16)
    lane_from = lax.rem(lax.broadcasted_iota(jnp.int32, (head_dim, 2 * head_dim), 0), quarter)
    lane_to = lax.broadcasted_iota(jnp.int32, (head_dim, 2 * head_dim), 1)
    first = jnp.where(lane_from < 3, 1.0, 0.0)
    second = jnp.where((lane_from >= 4) & (lane_from < 7), 1.0, 0.0)
    spread = jnp.where(lane_to < head_dim, first, second)
    both = jnp.dot(sums[...], spread.astype(BF16), preferred_element_type=F32)
    top_c, sum_c = both[:, :head_dim], both[:, head_dim:]
    top_f, sum_f = stat[0], stat[1]
    top = jnp.maximum(top_c, top_f)
    factor_c = sum_c * jnp.exp(top_c - top)
    factor_f = jnp.exp(top_f - top)
    share = 1.0 / (factor_c + sum_f * factor_f)
    grid_ref[...] = (grid_ref[...] * factor_c + vec[...] * factor_f) * share
    for h in range(per_row // steps):
        for s in range(steps):
            lined[h, pl.ds(s, rows, stride=steps), :] = grid_ref[pl.ds(h * steps + s, rows, stride=per_row), :]
        heads[:, pl.ds(h * head_dim, head_dim)] = lined[h].astype(BF16)
    project(heads, w, out, False)


def second_kernel(heads, w, out):
    project(heads, w, out, True)


def add_kernel(mine, given, *outs):
    for k, out in enumerate(outs):
        out[...] = (mine[k].astype(F32) + given[k].astype(F32)).astype(BF16)


def last_kernel(heads, w, arrived, keep, crossing):
    tokens, column = keep.shape
    groups = w.shape[1] // column // 2
    wide = widen(heads)
    crossing[...] = product(wide, w, units(False, groups)[-1], tokens, column).astype(BF16)
    keep[...] = product(wide, w, units(True, groups)[-1], tokens, column) + arrived[...].astype(F32)


def shards(inputs, norm_gain, query_proj, w_key, w_value, w_out, kv_cache, ancestors):
    rows, steps, width = inputs.shape
    context = kv_cache.shape[2]
    head_dim = kv_cache.shape[3] // 2
    local = query_proj.shape[2]
    heads = local // head_dim
    per_row = heads * steps
    devices = lax.axis_size("particle")
    tensor = lax.axis_size("tensor")
    column = width // tensor
    cosine, sine = rotary_tables(context, steps, head_dim)
    tables = np.stack([np.tile(cosine, (heads, 1)), np.tile(sine, (heads, 1))])
    smem = pl.BlockSpec(memory_space=pltpu.SMEM)
    vmem = pl.BlockSpec(memory_space=pltpu.VMEM)
    stay = pl.BlockSpec(memory_space=pl.ANY)
    hbm = lambda x: pltpu.with_memory_space_constraint(x, pltpu.HBM)
    tables = jnp.asarray(tables)

    packed = (devices, PAIR * per_row + MORE, head_dim)
    send, queries, tables, gain = pl.pallas_call(
        pack_kernel,
        out_shape=(
            jax.ShapeDtypeStruct(packed, BF16),
            jax.ShapeDtypeStruct((rows, per_row, head_dim), BF16),
            jax.ShapeDtypeStruct((2, per_row, head_dim), F32),
            jax.ShapeDtypeStruct((1, width), F32),
        ),
        in_specs=[stay] * 4,
        out_specs=(vmem,) * 4,
        scratch_shapes=[
            pltpu.VMEM((rows, per_row, head_dim), F32),
            pltpu.VMEM((rows, steps, local), BF16),
            pltpu.SMEM((rows,), jnp.int32),
            pltpu.SMEM((devices,), jnp.int32),
            pltpu.SMEM((devices * PAIR,), jnp.int32),
            pltpu.SemaphoreType.DMA((4,)),
        ],
        compiler_params=pltpu.CompilerParams(vmem_limit_bytes=4 * MIB),
        cost_estimate=pl.CostEstimate(flops=10_000_000_000, bytes_accessed=MIB, transcendentals=0),
        name="pack_queries",
    )(hbm(ancestors), hbm(query_proj), hbm(tables), hbm(norm_gain.reshape(1, width)))

    recv = lax.all_to_all(send, "particle", split_axis=0, concat_axis=0, tiled=True)

    slots = devices * PAIR
    back, vec, stat = pl.pallas_call(
        attend_kernel,
        out_shape=(
            jax.ShapeDtypeStruct(packed, BF16),
            jax.ShapeDtypeStruct((rows * per_row, head_dim), F32),
            jax.ShapeDtypeStruct((2, rows * per_row, head_dim), F32),
        ),
        in_specs=[vmem] * 8,
        out_specs=(vmem,) * 3,
        scratch_shapes=[
            pltpu.VMEM((slots, per_row, context), F32),
            pltpu.VMEM((slots, per_row, context), BF16),
            pltpu.VMEM((slots, per_row, head_dim), F32),
            pltpu.VMEM((slots, per_row, head_dim), F32),
            pltpu.VMEM((slots, per_row, head_dim), BF16),
            pltpu.VMEM((rows * steps, width), BF16),
            pltpu.SMEM((slots,), jnp.int32),
            pltpu.SMEM((slots,), jnp.int32),
        ],
        compiler_params=pltpu.CompilerParams(vmem_limit_bytes=12 * MIB),
        cost_estimate=pl.CostEstimate(
            flops=10_000_000_000, bytes_accessed=5 * MIB, transcendentals=0
        ),
        name="attention",
    )(
        recv,
        kv_cache,
        inputs,
        gain,
        w_key,
        w_value,
        queries,
        tables,
    )
    home = lax.all_to_all(back, "particle", split_axis=0, concat_axis=0, tiled=True)

    groups = tensor // 2
    away = groups - 1
    block = jax.ShapeDtypeStruct((away, rows * steps, column), BF16)
    one = jax.ShapeDtypeStruct((rows * steps, column), BF16)
    params = pltpu.CompilerParams(vmem_limit_bytes=8 * MIB)
    cost = pl.CostEstimate(
        flops=rows * steps * local * width, bytes_accessed=local * width, transcendentals=0
    )
    other, heads_out = pl.pallas_call(
        merge_kernel,
        out_shape=(
            block,
            jax.ShapeDtypeStruct((rows * steps, local), BF16),
        ),
        in_specs=[smem, vmem, vmem, vmem, vmem],
        out_specs=(vmem, vmem),
        scratch_shapes=[
            pltpu.VMEM((rows * per_row, head_dim), F32),
            pltpu.VMEM((rows * per_row, head_dim), BF16),
            pltpu.VMEM((heads, rows * steps, head_dim), F32),
            pltpu.SMEM((devices,), jnp.int32),
        ],
        compiler_params=params,
        cost_estimate=cost,
        name="merge_project_sibling",
    )(ancestors, home, vec, stat, w_out)
    sibling = [(i, i ^ 1) for i in range(tensor)]
    given = lax.ppermute(other, "tensor", sibling)
    mine = pl.pallas_call(
        second_kernel,
        out_shape=block,
        in_specs=[vmem, vmem],
        out_specs=vmem,
        compiler_params=params,
        cost_estimate=cost,
        name="project_own",
    )(heads_out, w_out)
    pair = pl.pallas_call(
        add_kernel,
        out_shape=(one,) * away,
        in_specs=[vmem, vmem],
        out_specs=(vmem,) * away,
        compiler_params=params,
        name="add_sibling",
    )(mine, given)
    arrived = []
    for k in range(1, groups):
        ring = [(i, ((i // 2 + k) % groups) * 2 + i % 2) for i in range(tensor)]
        arrived.append(lax.ppermute(pair[k - 1], "tensor", ring))
    keep, crossing = pl.pallas_call(
        last_kernel,
        out_shape=(jax.ShapeDtypeStruct(one.shape, F32), one),
        in_specs=[vmem, vmem, vmem],
        out_specs=(vmem, vmem),
        compiler_params=params,
        cost_estimate=cost,
        name="project_last",
    )(heads_out, w_out, arrived[0])
    total = keep + lax.ppermute(crossing, "tensor", sibling).astype(F32)
    for part in arrived[1:]:
        total = total + part.astype(F32)
    return total.astype(BF16).reshape(rows, steps, column)


def solution(mesh):
    in_specs = (
        P("particle", None, None),
        P(),
        P("particle", None, "tensor"),
        P(None, "tensor"),
        P(None, "tensor"),
        P("tensor", None),
        P("particle", "tensor", None, None),
        P("particle"),
    )
    out_specs = P("particle", None, "tensor")
    return jax.shard_map(shards, mesh=mesh, in_specs=in_specs, out_specs=out_specs, check_vma=False)
```

```python
import jax
import jax.numpy as jnp
import numpy as np
from jax import lax
from jax.experimental import pallas as pl
from jax.experimental.pallas import tpu as pltpu
from jax.sharding import PartitionSpec as P

PAIR = 2
MORE = 8
THETA = 500000.0
EPSILON = 1e-05
F32 = jnp.float32
BF16 = jnp.bfloat16
MIB = 1 << 20
NT = (((1,), (1,)), ((), ()))


def rotary_tables(context, steps, head_dim):
    half = head_dim // 2
    freqs = np.float32(THETA) ** (-np.arange(half, dtype=np.float32) * np.float32(2.0) / np.float32(head_dim))
    position = (np.float32(context) + np.arange(steps, dtype=np.float32)).reshape(steps, 1)
    angles = (position * freqs.astype(np.float32)).astype(np.float32)
    cosine, sine = np.cos(angles), np.sin(angles)
    return (
        np.concatenate([cosine, cosine], 1).astype(np.float32),
        np.concatenate([-sine, sine], 1).astype(np.float32),
    )


def slot_of(anc, row, rows, count):
    source = lax.div(anc[row], rows)
    rank = count[source]
    count[source] = rank + 1
    return source, rank


def pack_kernel(
    anc_hbm, qp_hbm, tables_hbm, gain_hbm, send, queries, tables, gain, grid_ref, qp, anc, count, spots, sems
):
    pairs = ((anc_hbm, anc), (qp_hbm, qp), (tables_hbm, tables), (gain_hbm, gain))
    copies = [pltpu.make_async_copy(src, dst, sems.at[i]) for i, (src, dst) in enumerate(pairs)]
    for copy in copies:
        copy.start()
    rows, steps, width = qp.shape
    _, per_row, head_dim = tables.shape
    devices = send.shape[0]

    def clear(d, _):
        send[d] = jnp.zeros(send.shape[1:], BF16)
        count[d] = 0
        for j in range(PAIR):
            spots[PAIR * d + j] = -1
        return 0

    lax.fori_loop(0, devices, clear, 0)
    for copy in copies:
        copy.wait()
    for h in range(width // head_dim):
        grid_ref[:, steps * h : steps * (h + 1), :] = qp[:, :, head_dim * h : head_dim * (h + 1)].astype(F32)
    for r in range(rows):
        source, rank = slot_of(anc, r, rows, count)
        spots[source * PAIR + rank] = lax.rem(anc[r], rows)
        plain = grid_ref[r]
        turned = (plain * tables[0] + pltpu.roll(plain, head_dim // 2, 1) * tables[1]).astype(BF16)
        queries[r] = turned
        send[source, pl.ds(pl.multiple_of(rank * per_row, per_row), per_row), :] = turned
    lane = lax.broadcasted_iota(jnp.int32, (MORE, head_dim), 1)
    for d in range(devices):
        send[d, PAIR * per_row :, :] = jnp.where(
            lane < head_dim // PAIR, spots[PAIR * d].astype(F32), spots[PAIR * d + 1].astype(F32)
        ).astype(BF16)


def pack_statistics(tops, sums, places, back):
    devices, _, head_dim = back.shape
    per_row = tops.shape[1]
    pieces = per_row // MORE
    lane = lax.broadcasted_iota(jnp.int32, (MORE, head_dim), 1)
    quarter = head_dim // (PAIR * pieces)
    piece_of, is_top, part_of = lax.div(lane, quarter), lax.rem(lane, quarter) < 4, lax.rem(lane, 4)
    for d in range(devices):
        value = jnp.zeros(lane.shape, F32)
        for j in range(PAIR):
            place = places[d * PAIR + j]
            for g in range(pieces):
                at = slice(g * MORE, (g + 1) * MORE)
                both = jnp.where(is_top, tops[place, at, :], sums[place, at, :])
                value = jnp.where(piece_of == j * pieces + g, both, value)
        first = value.astype(BF16).astype(F32)
        second = (value - first).astype(BF16).astype(F32)
        third = value - first - second
        back[d, PAIR * per_row :, :] = jnp.where(
            part_of == 0, first, jnp.where(part_of == 1, second, third)
        ).astype(BF16)


def attend_kernel(
    recv, kv, x, gain, wk, wv, queries, tables, back, vec, stat, *scratch
):
    scores, expos, tops, sums, vectors, normed, chosen, row_of = scratch
    devices, _, head_dim = recv.shape
    per_row = queries.shape[1]
    lane = lax.broadcasted_iota(jnp.int32, (per_row, head_dim), 1)
    rows, steps, width = x.shape
    tokens = rows * steps
    floats = x[...].reshape(tokens, width).astype(F32)
    inverse = lax.rsqrt(jnp.mean(floats * floats, -1, keepdims=True) + EPSILON)
    normed[...] = (floats * inverse * gain[...]).astype(BF16)
    repeat = tokens // per_row
    cosine, sine = (jnp.concatenate([tables[i]] * repeat, 0) for i in range(2))
    keys = jnp.dot(normed[...], wk[...], preferred_element_type=F32)
    keys = (keys * cosine + pltpu.roll(keys, head_dim // 2, 1) * sine).astype(BF16)
    vals = jnp.dot(normed[...], wv[...], preferred_element_type=F32).astype(BF16)
    flat = queries[...].reshape(rows * per_row, head_dim)
    fresh = lax.dot_general(flat, keys, NT, preferred_element_type=F32) * head_dim ** (-0.5)
    row = lax.broadcasted_iota(jnp.int32, fresh.shape, 0)
    col = lax.broadcasted_iota(jnp.int32, fresh.shape, 1)
    seen = (lax.div(row, per_row) == lax.div(col, steps)) & (lax.rem(col, steps) <= lax.rem(row, steps))
    top = jnp.max(jnp.where(seen, fresh, -jnp.inf), -1, keepdims=True)
    expo = jnp.where(seen, jnp.exp(jnp.where(seen, fresh - top, 0.0)), 0.0)
    vec[...] = jnp.dot(expo.astype(BF16), vals, preferred_element_type=F32)
    stat[0] = jnp.broadcast_to(top, stat.shape[1:])
    stat[1] = jnp.broadcast_to(jnp.sum(expo, -1, keepdims=True), stat.shape[1:])
    slots = devices * PAIR
    for k in range(slots):
        chosen[k] = 0
        row_of[k] = 0
    used = jnp.int32(0)
    places = []
    for d in range(devices):
        spot = recv[d, PAIR * per_row :, :].astype(F32)
        for j in range(PAIR):
            row = spot[0, j * (head_dim // PAIR)].astype(jnp.int32)
            chosen[used] = d * PAIR + j
            row_of[used] = jnp.maximum(row, 0)
            places.append(used)
            used = used + jnp.where(row >= 0, 1, 0)

    def cached(first, last):
        for k in range(first, last):
            d = lax.shift_right_logical(chosen[k], PAIR.bit_length() - 1)
            j = lax.bitwise_and(chosen[k], PAIR - 1)
            asked = recv[d, pl.ds(pl.multiple_of(j * per_row, per_row), per_row), :]
            scores[k] = lax.dot_general(
                asked, kv[row_of[k], 0, :, :head_dim], NT, preferred_element_type=F32
            ) * head_dim ** (-0.5)
        for k in range(first, last):
            top = jnp.max(scores[k], -1, keepdims=True)
            expo = jnp.exp(scores[k] - top)
            expos[k] = expo.astype(BF16)
            tops[k] = jnp.broadcast_to(top, lane.shape)
            sums[k] = jnp.broadcast_to(jnp.sum(expo, -1, keepdims=True), lane.shape)
        for k in range(first, last):
            vector = jnp.dot(expos[k], kv[row_of[k], 0, :, head_dim:], preferred_element_type=F32)
            vectors[k] = (vector / sums[k]).astype(BF16)

    most = slots * 3 // 4
    cached(0, most)

    @pl.when(used > most)
    def _():
        cached(most, slots)

    for i in range(slots):
        at = (i % PAIR) * per_row
        back[i // PAIR, at : at + per_row, :] = vectors[places[i]]
    pack_statistics(tops, sums, places, back)


def units(own, groups):
    index = lax.axis_index("tensor")
    y, core = lax.div(index, 2), lax.rem(index, 2)
    core = core if own else 1 - core
    return [2 * lax.rem(y + k, groups) + core for k in (*range(1, groups), 0)]


def product(wide, w, block, tokens, column):
    at = pl.multiple_of(block * column, column)
    return jnp.dot(wide, w[:, pl.ds(at, column)], preferred_element_type=F32)[:tokens]


def widen(heads):
    return jnp.concatenate([heads[...]] * max(1, 128 // heads.shape[0]), 0)


def project(heads, w, out, own):
    away, tokens, column = out.shape
    wide = widen(heads)
    for k, block in enumerate(units(own, away + 1)[:away]):
        out[k] = product(wide, w, block, tokens, column).astype(BF16)


def merge_kernel(anc, recv, vec, stat, w, out, heads, grid_ref, sums, count):
    devices, chunk, head_dim = recv.shape
    per_row = (chunk - MORE) // PAIR
    rows = vec.shape[0] // per_row
    steps = heads.shape[0] // rows
    pieces = per_row // MORE
    quarter = head_dim // (PAIR * pieces)
    for d in range(devices):
        count[d] = 0
    part_of = lax.div(lax.broadcasted_iota(jnp.int32, (MORE, head_dim), 1), quarter)
    for r in range(rows):
        source, rank = slot_of(anc, r, rows, count)
        at = pl.multiple_of(rank * per_row, per_row)
        grid_ref[pl.ds(r * per_row, per_row), :] = recv[source, pl.ds(at, per_row), :].astype(F32)
        parts = recv[source, PAIR * per_row :, :].astype(F32)
        sums[pl.ds(r * per_row, per_row), :] = jnp.concatenate(
            [jnp.where(part_of == rank * pieces + g, parts, 0.0) for g in range(pieces)], 0
        ).astype(BF16)
    lane_from = lax.rem(lax.broadcasted_iota(jnp.int32, (head_dim, 2 * head_dim), 0), quarter)
    lane_to = lax.broadcasted_iota(jnp.int32, (head_dim, 2 * head_dim), 1)
    first = jnp.where(lane_from < 3, 1.0, 0.0)
    second = jnp.where((lane_from >= 4) & (lane_from < 7), 1.0, 0.0)
    spread = jnp.where(lane_to < head_dim, first, second)
    both = jnp.dot(sums[...], spread.astype(BF16), preferred_element_type=F32)
    top_c, sum_c = both[:, :head_dim], both[:, head_dim:]
    top_f, sum_f = stat[0], stat[1]
    top = jnp.maximum(top_c, top_f)
    factor_c = sum_c * jnp.exp(top_c - top)
    factor_f = jnp.exp(top_f - top)
    share = 1.0 / (factor_c + sum_f * factor_f)
    grid_ref[...] = (grid_ref[...] * factor_c + vec[...] * factor_f) * share
    for h in range(per_row // steps):
        for s in range(steps):
            heads[pl.ds(s * rows, rows), pl.ds(h * head_dim, head_dim)] = grid_ref[
                pl.ds(h * steps + s, rows, stride=per_row), :
            ].astype(BF16)
    project(heads, w, out, False)


def second_kernel(heads, w, out):
    project(heads, w, out, True)


def add_kernel(mine, given, *outs):
    for k, out in enumerate(outs):
        out[...] = (mine[k].astype(F32) + given[k].astype(F32)).astype(BF16)


def last_kernel(heads, w, arrived, keep, crossing):
    tokens, column = keep.shape
    groups = w.shape[1] // column // 2
    wide = widen(heads)
    crossing[...] = product(wide, w, units(False, groups)[-1], tokens, column).astype(BF16)
    keep[...] = product(wide, w, units(True, groups)[-1], tokens, column) + arrived[...].astype(F32)


def shards(inputs, norm_gain, query_proj, w_key, w_value, w_out, kv_cache, ancestors):
    rows, steps, width = inputs.shape
    context = kv_cache.shape[2]
    head_dim = kv_cache.shape[3] // 2
    local = query_proj.shape[2]
    heads = local // head_dim
    per_row = heads * steps
    devices = lax.axis_size("particle")
    tensor = lax.axis_size("tensor")
    column = width // tensor
    cosine, sine = rotary_tables(context, steps, head_dim)
    tables = np.stack([np.tile(cosine, (heads, 1)), np.tile(sine, (heads, 1))])
    smem = pl.BlockSpec(memory_space=pltpu.SMEM)
    vmem = pl.BlockSpec(memory_space=pltpu.VMEM)
    stay = pl.BlockSpec(memory_space=pl.ANY)
    hbm = lambda x: pltpu.with_memory_space_constraint(x, pltpu.HBM)
    tables = jnp.asarray(tables)

    packed = (devices, PAIR * per_row + MORE, head_dim)
    send, queries, tables, gain = pl.pallas_call(
        pack_kernel,
        out_shape=(
            jax.ShapeDtypeStruct(packed, BF16),
            jax.ShapeDtypeStruct((rows, per_row, head_dim), BF16),
            jax.ShapeDtypeStruct((2, per_row, head_dim), F32),
            jax.ShapeDtypeStruct((1, width), F32),
        ),
        in_specs=[stay] * 4,
        out_specs=(vmem,) * 4,
        scratch_shapes=[
            pltpu.VMEM((rows, per_row, head_dim), F32),
            pltpu.VMEM((rows, steps, local), BF16),
            pltpu.SMEM((rows,), jnp.int32),
            pltpu.SMEM((devices,), jnp.int32),
            pltpu.SMEM((devices * PAIR,), jnp.int32),
            pltpu.SemaphoreType.DMA((4,)),
        ],
        compiler_params=pltpu.CompilerParams(vmem_limit_bytes=4 * MIB),
        cost_estimate=pl.CostEstimate(flops=10_000_000_000, bytes_accessed=MIB, transcendentals=0),
        name="pack_queries",
    )(hbm(ancestors), hbm(query_proj), hbm(tables), hbm(norm_gain.reshape(1, width)))

    recv = lax.all_to_all(send, "particle", split_axis=0, concat_axis=0, tiled=True)

    slots = devices * PAIR
    back, vec, stat = pl.pallas_call(
        attend_kernel,
        out_shape=(
            jax.ShapeDtypeStruct(packed, BF16),
            jax.ShapeDtypeStruct((rows * per_row, head_dim), F32),
            jax.ShapeDtypeStruct((2, rows * per_row, head_dim), F32),
        ),
        in_specs=[vmem] * 8,
        out_specs=(vmem,) * 3,
        scratch_shapes=[
            pltpu.VMEM((slots, per_row, context), F32),
            pltpu.VMEM((slots, per_row, context), BF16),
            pltpu.VMEM((slots, per_row, head_dim), F32),
            pltpu.VMEM((slots, per_row, head_dim), F32),
            pltpu.VMEM((slots, per_row, head_dim), BF16),
            pltpu.VMEM((rows * steps, width), BF16),
            pltpu.SMEM((slots,), jnp.int32),
            pltpu.SMEM((slots,), jnp.int32),
        ],
        compiler_params=pltpu.CompilerParams(vmem_limit_bytes=12 * MIB),
        cost_estimate=pl.CostEstimate(
            flops=10_000_000_000, bytes_accessed=5 * MIB, transcendentals=0
        ),
        name="attention",
    )(
        recv,
        kv_cache,
        inputs,
        gain,
        w_key,
        w_value,
        queries,
        tables,
    )
    home = lax.all_to_all(back, "particle", split_axis=0, concat_axis=0, tiled=True)

    groups = tensor // 2
    away = groups - 1
    block = jax.ShapeDtypeStruct((away, rows * steps, column), BF16)
    one = jax.ShapeDtypeStruct((rows * steps, column), BF16)
    params = pltpu.CompilerParams(vmem_limit_bytes=8 * MIB)
    cost = pl.CostEstimate(
        flops=rows * steps * local * width, bytes_accessed=local * width, transcendentals=0
    )
    other, heads_out = pl.pallas_call(
        merge_kernel,
        out_shape=(
            block,
            jax.ShapeDtypeStruct((rows * steps, local), BF16),
        ),
        in_specs=[smem, vmem, vmem, vmem, vmem],
        out_specs=(vmem, vmem),
        scratch_shapes=[
            pltpu.VMEM((rows * per_row, head_dim), F32),
            pltpu.VMEM((rows * per_row, head_dim), BF16),
            pltpu.SMEM((devices,), jnp.int32),
        ],
        compiler_params=params,
        cost_estimate=cost,
        name="merge_project_sibling",
    )(ancestors, home, vec, stat, w_out)
    sibling = [(i, i ^ 1) for i in range(tensor)]
    given = lax.ppermute(other, "tensor", sibling)
    mine = pl.pallas_call(
        second_kernel,
        out_shape=block,
        in_specs=[vmem, vmem],
        out_specs=vmem,
        compiler_params=params,
        cost_estimate=cost,
        name="project_own",
    )(heads_out, w_out)
    pair = pl.pallas_call(
        add_kernel,
        out_shape=(one,) * away,
        in_specs=[vmem, vmem],
        out_specs=(vmem,) * away,
        compiler_params=params,
        name="add_sibling",
    )(mine, given)
    arrived = []
    for k in range(1, groups):
        ring = [(i, ((i // 2 + k) % groups) * 2 + i % 2) for i in range(tensor)]
        arrived.append(lax.ppermute(pair[k - 1], "tensor", ring))
    keep, crossing = pl.pallas_call(
        last_kernel,
        out_shape=(jax.ShapeDtypeStruct(one.shape, F32), one),
        in_specs=[vmem, vmem, vmem],
        out_specs=(vmem, vmem),
        compiler_params=params,
        cost_estimate=cost,
        name="project_last",
    )(heads_out, w_out, arrived[0])
    total = keep + lax.ppermute(crossing, "tensor", sibling).astype(F32)
    for part in arrived[1:]:
        total = total + part.astype(F32)
    return total.astype(BF16).reshape(steps, rows, column).swapaxes(0, 1)


def solution(mesh):
    in_specs = (
        P("particle", None, None),
        P(),
        P("particle", None, "tensor"),
        P(None, "tensor"),
        P(None, "tensor"),
        P("tensor", None),
        P("particle", "tensor", None, None),
        P("particle"),
    )
    out_specs = P("particle", None, "tensor")
    return jax.shard_map(shards, mesh=mesh, in_specs=in_specs, out_specs=out_specs, check_vma=False)
```

```python
import jax
import jax.numpy as jnp
import numpy as np
from jax import lax
from jax.experimental import pallas as pl
from jax.experimental.pallas import tpu as pltpu
from jax.sharding import PartitionSpec as P

PAIR = 2
PARTNERS = (3, 2, 1)
MORE = 8
THETA = 500000.0
EPSILON = 1e-05
F32 = jnp.float32
BF16 = jnp.bfloat16
MIB = 1 << 20
NT = (((1,), (1,)), ((), ()))


def rotary_tables(context, steps, head_dim):
    half = head_dim // 2
    freqs = np.float32(THETA) ** (-np.arange(half, dtype=np.float32) * np.float32(2.0) / np.float32(head_dim))
    position = (np.float32(context) + np.arange(steps, dtype=np.float32)).reshape(steps, 1)
    angles = (position * freqs.astype(np.float32)).astype(np.float32)
    cosine, sine = np.cos(angles), np.sin(angles)
    return (
        np.concatenate([cosine, cosine], 1).astype(np.float32),
        np.concatenate([-sine, sine], 1).astype(np.float32),
    )


def slot_of(anc, row, rows, count):
    source = lax.div(anc[row], rows)
    rank = count[source]
    count[source] = rank + 1
    return source, rank


def pack_kernel(
    anc_hbm, qp_hbm, tables_hbm, gain_hbm, send, queries, tables, gain, grid_ref, qp, anc, count, spots, sems
):
    pairs = ((anc_hbm, anc), (qp_hbm, qp), (tables_hbm, tables), (gain_hbm, gain))
    copies = [pltpu.make_async_copy(src, dst, sems.at[i]) for i, (src, dst) in enumerate(pairs)]
    for copy in copies:
        copy.start()
    rows, steps, width = qp.shape
    _, per_row, head_dim = tables.shape
    devices = send.shape[0]

    def clear(d, _):
        send[d] = jnp.zeros(send.shape[1:], BF16)
        count[d] = 0
        for j in range(PAIR):
            spots[PAIR * d + j] = -1
        return 0

    lax.fori_loop(0, devices, clear, 0)
    for copy in copies:
        copy.wait()
    for h in range(width // head_dim):
        grid_ref[:, steps * h : steps * (h + 1), :] = qp[:, :, head_dim * h : head_dim * (h + 1)].astype(F32)
    for r in range(rows):
        source, rank = slot_of(anc, r, rows, count)
        spots[source * PAIR + rank] = lax.rem(anc[r], rows)
        plain = grid_ref[r]
        turned = (plain * tables[0] + pltpu.roll(plain, head_dim // 2, 1) * tables[1]).astype(BF16)
        queries[r] = turned
        send[source, pl.ds(pl.multiple_of(rank * per_row, per_row), per_row), :] = turned
    lane = lax.broadcasted_iota(jnp.int32, (MORE, head_dim), 1)
    for d in range(devices):
        send[d, PAIR * per_row :, :] = jnp.where(
            lane < head_dim // PAIR, spots[PAIR * d].astype(F32), spots[PAIR * d + 1].astype(F32)
        ).astype(BF16)


def pack_statistics(tops, sums, places, back):
    devices, _, head_dim = back.shape
    per_row = tops.shape[1]
    pieces = per_row // MORE
    lane = lax.broadcasted_iota(jnp.int32, (MORE, head_dim), 1)
    quarter = head_dim // (PAIR * pieces)
    piece_of, is_top, part_of = lax.div(lane, quarter), lax.rem(lane, quarter) < 4, lax.rem(lane, 4)
    for d in range(devices):
        value = jnp.zeros(lane.shape, F32)
        for j in range(PAIR):
            place = places[d * PAIR + j]
            for g in range(pieces):
                at = slice(g * MORE, (g + 1) * MORE)
                both = jnp.where(is_top, tops[place, at, :], sums[place, at, :])
                value = jnp.where(piece_of == j * pieces + g, both, value)
        first = value.astype(BF16).astype(F32)
        second = (value - first).astype(BF16).astype(F32)
        third = value - first - second
        back[d, PAIR * per_row :, :] = jnp.where(
            part_of == 0, first, jnp.where(part_of == 1, second, third)
        ).astype(BF16)


def attend_kernel(
    recv, kv, x, gain, wk, wv, queries, tables, back, vec, stat, *scratch
):
    scores, expos, tops, sums, vectors, normed, chosen, row_of = scratch
    devices, _, head_dim = recv.shape
    per_row = queries.shape[1]
    lane = lax.broadcasted_iota(jnp.int32, (per_row, head_dim), 1)
    rows, steps, width = x.shape
    tokens = rows * steps
    floats = x[...].reshape(tokens, width).astype(F32)
    inverse = lax.rsqrt(jnp.mean(floats * floats, -1, keepdims=True) + EPSILON)
    normed[...] = (floats * inverse * gain[...]).astype(BF16)
    repeat = tokens // per_row
    cosine, sine = (jnp.concatenate([tables[i]] * repeat, 0) for i in range(2))
    keys = jnp.dot(normed[...], wk[...], preferred_element_type=F32)
    keys = (keys * cosine + pltpu.roll(keys, head_dim // 2, 1) * sine).astype(BF16)
    vals = jnp.dot(normed[...], wv[...], preferred_element_type=F32).astype(BF16)
    flat = queries[...].reshape(rows * per_row, head_dim)
    fresh = lax.dot_general(flat, keys, NT, preferred_element_type=F32) * head_dim ** (-0.5)
    row = lax.broadcasted_iota(jnp.int32, fresh.shape, 0)
    col = lax.broadcasted_iota(jnp.int32, fresh.shape, 1)
    seen = (lax.div(row, per_row) == lax.div(col, steps)) & (lax.rem(col, steps) <= lax.rem(row, steps))
    top = jnp.max(jnp.where(seen, fresh, -jnp.inf), -1, keepdims=True)
    expo = jnp.where(seen, jnp.exp(jnp.where(seen, fresh - top, 0.0)), 0.0)
    vec[...] = jnp.dot(expo.astype(BF16), vals, preferred_element_type=F32)
    stat[0] = jnp.broadcast_to(top, stat.shape[1:])
    stat[1] = jnp.broadcast_to(jnp.sum(expo, -1, keepdims=True), stat.shape[1:])
    slots = devices * PAIR
    for k in range(slots):
        chosen[k] = 0
        row_of[k] = 0
    used = jnp.int32(0)
    places = []
    for d in range(devices):
        spot = recv[d, PAIR * per_row :, :].astype(F32)
        for j in range(PAIR):
            row = spot[0, j * (head_dim // PAIR)].astype(jnp.int32)
            chosen[used] = d * PAIR + j
            row_of[used] = jnp.maximum(row, 0)
            places.append(used)
            used = used + jnp.where(row >= 0, 1, 0)

    def cached(first, last):
        for k in range(first, last):
            d = lax.shift_right_logical(chosen[k], PAIR.bit_length() - 1)
            j = lax.bitwise_and(chosen[k], PAIR - 1)
            asked = recv[d, pl.ds(pl.multiple_of(j * per_row, per_row), per_row), :]
            scores[k] = lax.dot_general(
                asked, kv[row_of[k], 0, :, :head_dim], NT, preferred_element_type=F32
            ) * head_dim ** (-0.5)
        for k in range(first, last):
            top = jnp.max(scores[k], -1, keepdims=True)
            expo = jnp.exp(scores[k] - top)
            expos[k] = expo.astype(BF16)
            tops[k] = jnp.broadcast_to(top, lane.shape)
            sums[k] = jnp.broadcast_to(jnp.sum(expo, -1, keepdims=True), lane.shape)
        for k in range(first, last):
            vector = jnp.dot(expos[k], kv[row_of[k], 0, :, head_dim:], preferred_element_type=F32)
            vectors[k] = (vector / sums[k]).astype(BF16)

    most = slots * 3 // 4
    cached(0, most)

    @pl.when(used > most)
    def _():
        cached(most, slots)

    for i in range(slots):
        at = (i % PAIR) * per_row
        back[i // PAIR, at : at + per_row, :] = vectors[places[i]]
    pack_statistics(tops, sums, places, back)


def units(own):
    index = lax.axis_index("tensor")
    y, core = lax.div(index, 2), lax.rem(index, 2)
    core = core if own else 1 - core
    return [2 * lax.bitwise_xor(y, k) + core for k in (*PARTNERS, 0)]


def product(wide, w, block, tokens, column):
    at = pl.multiple_of(block * column, column)
    return jnp.dot(wide, w[:, pl.ds(at, column)], preferred_element_type=F32)[:tokens]


def widen(heads):
    return jnp.concatenate([heads[...]] * max(1, 128 // heads.shape[0]), 0)


def project(heads, w, out, own):
    away, tokens, column = out.shape
    wide = widen(heads)
    for k, block in enumerate(units(own)[:away]):
        out[k] = product(wide, w, block, tokens, column).astype(BF16)


def merge_kernel(anc, recv, vec, stat, w, out, heads, grid_ref, sums, count):
    devices, chunk, head_dim = recv.shape
    per_row = (chunk - MORE) // PAIR
    rows = vec.shape[0] // per_row
    steps = heads.shape[0] // rows
    pieces = per_row // MORE
    quarter = head_dim // (PAIR * pieces)
    for d in range(devices):
        count[d] = 0
    part_of = lax.div(lax.broadcasted_iota(jnp.int32, (MORE, head_dim), 1), quarter)
    for r in range(rows):
        source, rank = slot_of(anc, r, rows, count)
        at = pl.multiple_of(rank * per_row, per_row)
        grid_ref[pl.ds(r * per_row, per_row), :] = recv[source, pl.ds(at, per_row), :].astype(F32)
        parts = recv[source, PAIR * per_row :, :].astype(F32)
        sums[pl.ds(r * per_row, per_row), :] = jnp.concatenate(
            [jnp.where(part_of == rank * pieces + g, parts, 0.0) for g in range(pieces)], 0
        ).astype(BF16)
    lane_from = lax.rem(lax.broadcasted_iota(jnp.int32, (head_dim, 2 * head_dim), 0), quarter)
    lane_to = lax.broadcasted_iota(jnp.int32, (head_dim, 2 * head_dim), 1)
    first = jnp.where(lane_from < 3, 1.0, 0.0)
    second = jnp.where((lane_from >= 4) & (lane_from < 7), 1.0, 0.0)
    spread = jnp.where(lane_to < head_dim, first, second)
    both = jnp.dot(sums[...], spread.astype(BF16), preferred_element_type=F32)
    top_c, sum_c = both[:, :head_dim], both[:, head_dim:]
    top_f, sum_f = stat[0], stat[1]
    top = jnp.maximum(top_c, top_f)
    factor_c = sum_c * jnp.exp(top_c - top)
    factor_f = jnp.exp(top_f - top)
    share = 1.0 / (factor_c + sum_f * factor_f)
    grid_ref[...] = (grid_ref[...] * factor_c + vec[...] * factor_f) * share
    for h in range(per_row // steps):
        for s in range(steps):
            heads[pl.ds(s * rows, rows), pl.ds(h * head_dim, head_dim)] = grid_ref[
                pl.ds(h * steps + s, rows, stride=per_row), :
            ].astype(BF16)
    project(heads, w, out, False)


def second_kernel(heads, w, out):
    project(heads, w, out, True)


def add_kernel(mine, given, *outs):
    for k, out in enumerate(outs):
        out[...] = (mine[k].astype(F32) + given[k].astype(F32)).astype(BF16)


def last_kernel(heads, w, arrived, keep, crossing):
    tokens, column = keep.shape
    wide = widen(heads)
    crossing[...] = product(wide, w, units(False)[-1], tokens, column).astype(BF16)
    keep[...] = product(wide, w, units(True)[-1], tokens, column) + arrived[...].astype(F32)


def shards(inputs, norm_gain, query_proj, w_key, w_value, w_out, kv_cache, ancestors):
    rows, steps, width = inputs.shape
    context = kv_cache.shape[2]
    head_dim = kv_cache.shape[3] // 2
    local = query_proj.shape[2]
    heads = local // head_dim
    per_row = heads * steps
    devices = lax.axis_size("particle")
    tensor = lax.axis_size("tensor")
    column = width // tensor
    cosine, sine = rotary_tables(context, steps, head_dim)
    tables = np.stack([np.tile(cosine, (heads, 1)), np.tile(sine, (heads, 1))])
    smem = pl.BlockSpec(memory_space=pltpu.SMEM)
    vmem = pl.BlockSpec(memory_space=pltpu.VMEM)
    stay = pl.BlockSpec(memory_space=pl.ANY)
    hbm = lambda x: pltpu.with_memory_space_constraint(x, pltpu.HBM)
    tables = jnp.asarray(tables)

    packed = (devices, PAIR * per_row + MORE, head_dim)
    send, queries, tables, gain = pl.pallas_call(
        pack_kernel,
        out_shape=(
            jax.ShapeDtypeStruct(packed, BF16),
            jax.ShapeDtypeStruct((rows, per_row, head_dim), BF16),
            jax.ShapeDtypeStruct((2, per_row, head_dim), F32),
            jax.ShapeDtypeStruct((1, width), F32),
        ),
        in_specs=[stay] * 4,
        out_specs=(vmem,) * 4,
        scratch_shapes=[
            pltpu.VMEM((rows, per_row, head_dim), F32),
            pltpu.VMEM((rows, steps, local), BF16),
            pltpu.SMEM((rows,), jnp.int32),
            pltpu.SMEM((devices,), jnp.int32),
            pltpu.SMEM((devices * PAIR,), jnp.int32),
            pltpu.SemaphoreType.DMA((4,)),
        ],
        compiler_params=pltpu.CompilerParams(vmem_limit_bytes=4 * MIB),
        cost_estimate=pl.CostEstimate(flops=10_000_000_000, bytes_accessed=MIB, transcendentals=0),
        name="pack_queries",
    )(hbm(ancestors), hbm(query_proj), hbm(tables), hbm(norm_gain.reshape(1, width)))

    recv = lax.all_to_all(send, "particle", split_axis=0, concat_axis=0, tiled=True)

    slots = devices * PAIR
    back, vec, stat = pl.pallas_call(
        attend_kernel,
        out_shape=(
            jax.ShapeDtypeStruct(packed, BF16),
            jax.ShapeDtypeStruct((rows * per_row, head_dim), F32),
            jax.ShapeDtypeStruct((2, rows * per_row, head_dim), F32),
        ),
        in_specs=[vmem] * 8,
        out_specs=(vmem,) * 3,
        scratch_shapes=[
            pltpu.VMEM((slots, per_row, context), F32),
            pltpu.VMEM((slots, per_row, context), BF16),
            pltpu.VMEM((slots, per_row, head_dim), F32),
            pltpu.VMEM((slots, per_row, head_dim), F32),
            pltpu.VMEM((slots, per_row, head_dim), BF16),
            pltpu.VMEM((rows * steps, width), BF16),
            pltpu.SMEM((slots,), jnp.int32),
            pltpu.SMEM((slots,), jnp.int32),
        ],
        compiler_params=pltpu.CompilerParams(vmem_limit_bytes=12 * MIB),
        cost_estimate=pl.CostEstimate(
            flops=10_000_000_000, bytes_accessed=5 * MIB, transcendentals=0
        ),
        name="attention",
    )(
        recv,
        kv_cache,
        inputs,
        gain,
        w_key,
        w_value,
        queries,
        tables,
    )
    home = lax.all_to_all(back, "particle", split_axis=0, concat_axis=0, tiled=True)

    away = len(PARTNERS)
    block = jax.ShapeDtypeStruct((away, rows * steps, column), BF16)
    one = jax.ShapeDtypeStruct((rows * steps, column), BF16)
    params = pltpu.CompilerParams(vmem_limit_bytes=8 * MIB)
    cost = pl.CostEstimate(
        flops=rows * steps * local * width, bytes_accessed=local * width, transcendentals=0
    )
    other, heads_out = pl.pallas_call(
        merge_kernel,
        out_shape=(
            block,
            jax.ShapeDtypeStruct((rows * steps, local), BF16),
        ),
        in_specs=[smem, vmem, vmem, vmem, vmem],
        out_specs=(vmem, vmem),
        scratch_shapes=[
            pltpu.VMEM((rows * per_row, head_dim), F32),
            pltpu.VMEM((rows * per_row, head_dim), BF16),
            pltpu.SMEM((devices,), jnp.int32),
        ],
        compiler_params=params,
        cost_estimate=cost,
        name="merge_project_sibling",
    )(ancestors, home, vec, stat, w_out)
    sibling = [(i, i ^ 1) for i in range(tensor)]
    given = lax.ppermute(other, "tensor", sibling)
    mine = pl.pallas_call(
        second_kernel,
        out_shape=block,
        in_specs=[vmem, vmem],
        out_specs=vmem,
        compiler_params=params,
        cost_estimate=cost,
        name="project_own",
    )(heads_out, w_out)
    pair = pl.pallas_call(
        add_kernel,
        out_shape=(one,) * away,
        in_specs=[vmem, vmem],
        out_specs=(vmem,) * away,
        compiler_params=params,
        name="add_sibling",
    )(mine, given)
    arrived = []
    for part, k in zip(pair, PARTNERS):
        exchange = [(i, ((i // 2) ^ k) * 2 + i % 2) for i in range(tensor)]
        arrived.append(lax.ppermute(part, "tensor", exchange))
    keep, crossing = pl.pallas_call(
        last_kernel,
        out_shape=(jax.ShapeDtypeStruct(one.shape, F32), one),
        in_specs=[vmem, vmem, vmem],
        out_specs=(vmem, vmem),
        compiler_params=params,
        cost_estimate=cost,
        name="project_last",
    )(heads_out, w_out, arrived[0])
    total = keep + lax.ppermute(crossing, "tensor", sibling).astype(F32)
    for part in arrived[1:]:
        total = total + part.astype(F32)
    return total.astype(BF16).reshape(steps, rows, column).swapaxes(0, 1)


def solution(mesh):
    in_specs = (
        P("particle", None, None),
        P(),
        P("particle", None, "tensor"),
        P(None, "tensor"),
        P(None, "tensor"),
        P("tensor", None),
        P("particle", "tensor", None, None),
        P("particle"),
    )
    out_specs = P("particle", None, "tensor")
    return jax.shard_map(shards, mesh=mesh, in_specs=in_specs, out_specs=out_specs, check_vma=False)
```

```python
import jax
import jax.numpy as jnp
import numpy as np
from jax import lax
from jax.experimental import pallas as pl
from jax.experimental.pallas import tpu as pltpu
from jax.sharding import PartitionSpec as P

PAIR = 2
MORE = 8
THETA = 500000.0
EPSILON = 1e-05
F32 = jnp.float32
BF16 = jnp.bfloat16
MIB = 1 << 20
NT = (((1,), (1,)), ((), ()))


def rotary_tables(context, steps, head_dim):
    half = head_dim // 2
    freqs = np.float32(THETA) ** (-np.arange(half, dtype=np.float32) * np.float32(2.0) / np.float32(head_dim))
    position = (np.float32(context) + np.arange(steps, dtype=np.float32)).reshape(steps, 1)
    angles = (position * freqs.astype(np.float32)).astype(np.float32)
    cosine, sine = np.cos(angles), np.sin(angles)
    return (
        np.concatenate([cosine, cosine], 1).astype(np.float32),
        np.concatenate([-sine, sine], 1).astype(np.float32),
    )


def slot_of(anc, row, rows, count):
    source = lax.div(anc[row], rows)
    rank = count[source]
    count[source] = rank + 1
    return source, rank


def pack_kernel(
    anc_hbm, qp_hbm, tables_hbm, gain_hbm, send, queries, tables, gain, grid_ref, qp, anc, count, spots, sems
):
    pairs = ((anc_hbm, anc), (qp_hbm, qp), (tables_hbm, tables), (gain_hbm, gain))
    copies = [pltpu.make_async_copy(src, dst, sems.at[i]) for i, (src, dst) in enumerate(pairs)]
    for copy in copies:
        copy.start()
    rows, steps, width = qp.shape
    _, per_row, head_dim = tables.shape
    devices = send.shape[0]

    def clear(d, _):
        send[d] = jnp.zeros(send.shape[1:], BF16)
        count[d] = 0
        for j in range(PAIR):
            spots[PAIR * d + j] = -1
        return 0

    lax.fori_loop(0, devices, clear, 0)
    for copy in copies:
        copy.wait()
    for h in range(width // head_dim):
        grid_ref[:, steps * h : steps * (h + 1), :] = qp[:, :, head_dim * h : head_dim * (h + 1)].astype(F32)
    for r in range(rows):
        source, rank = slot_of(anc, r, rows, count)
        spots[source * PAIR + rank] = lax.rem(anc[r], rows)
        plain = grid_ref[r]
        turned = (plain * tables[0] + pltpu.roll(plain, head_dim // 2, 1) * tables[1]).astype(BF16)
        queries[r] = turned
        send[source, pl.ds(pl.multiple_of(rank * per_row, per_row), per_row), :] = turned
    lane = lax.broadcasted_iota(jnp.int32, (MORE, head_dim), 1)
    for d in range(devices):
        send[d, PAIR * per_row :, :] = jnp.where(
            lane < head_dim // PAIR, spots[PAIR * d].astype(F32), spots[PAIR * d + 1].astype(F32)
        ).astype(BF16)


def pack_statistics(tops, sums, places, back):
    devices, _, head_dim = back.shape
    per_row = tops.shape[1]
    pieces = per_row // MORE
    lane = lax.broadcasted_iota(jnp.int32, (MORE, head_dim), 1)
    quarter = head_dim // (PAIR * pieces)
    piece_of, is_top, part_of = lax.div(lane, quarter), lax.rem(lane, quarter) < 4, lax.rem(lane, 4)
    for d in range(devices):
        value = jnp.zeros(lane.shape, F32)
        for j in range(PAIR):
            place = places[d * PAIR + j]
            for g in range(pieces):
                at = slice(g * MORE, (g + 1) * MORE)
                both = jnp.where(is_top, tops[place, at, :], sums[place, at, :])
                value = jnp.where(piece_of == j * pieces + g, both, value)
        first = value.astype(BF16).astype(F32)
        second = (value - first).astype(BF16).astype(F32)
        third = value - first - second
        back[d, PAIR * per_row :, :] = jnp.where(
            part_of == 0, first, jnp.where(part_of == 1, second, third)
        ).astype(BF16)


def attend_kernel(
    recv, kv, x, gain, wk, wv, queries, tables, back, vec, stat, *scratch
):
    scores, expos, tops, sums, vectors, normed, chosen, row_of = scratch
    devices, _, head_dim = recv.shape
    per_row = queries.shape[1]
    lane = lax.broadcasted_iota(jnp.int32, (per_row, head_dim), 1)
    rows, steps, width = x.shape
    tokens = rows * steps
    floats = x[...].reshape(tokens, width).astype(F32)
    inverse = lax.rsqrt(jnp.mean(floats * floats, -1, keepdims=True) + EPSILON)
    normed[...] = (floats * inverse * gain[...]).astype(BF16)
    repeat = tokens // per_row
    cosine, sine = (jnp.concatenate([tables[i]] * repeat, 0) for i in range(2))
    keys = jnp.dot(normed[...], wk[...], preferred_element_type=F32)
    keys = (keys * cosine + pltpu.roll(keys, head_dim // 2, 1) * sine).astype(BF16)
    vals = jnp.dot(normed[...], wv[...], preferred_element_type=F32).astype(BF16)
    flat = queries[...].reshape(rows * per_row, head_dim)
    fresh = lax.dot_general(flat, keys, NT, preferred_element_type=F32) * head_dim ** (-0.5)
    row = lax.broadcasted_iota(jnp.int32, fresh.shape, 0)
    col = lax.broadcasted_iota(jnp.int32, fresh.shape, 1)
    seen = (lax.div(row, per_row) == lax.div(col, steps)) & (lax.rem(col, steps) <= lax.rem(row, steps))
    top = jnp.max(jnp.where(seen, fresh, -jnp.inf), -1, keepdims=True)
    expo = jnp.where(seen, jnp.exp(jnp.where(seen, fresh - top, 0.0)), 0.0)
    vec[...] = jnp.dot(expo.astype(BF16), vals, preferred_element_type=F32)
    stat[0] = jnp.broadcast_to(top, stat.shape[1:])
    stat[1] = jnp.broadcast_to(jnp.sum(expo, -1, keepdims=True), stat.shape[1:])
    slots = devices * PAIR
    for k in range(slots):
        chosen[k] = 0
        row_of[k] = 0
    used = jnp.int32(0)
    places = []
    for d in range(devices):
        spot = recv[d, PAIR * per_row :, :].astype(F32)
        for j in range(PAIR):
            row = spot[0, j * (head_dim // PAIR)].astype(jnp.int32)
            chosen[used] = d * PAIR + j
            row_of[used] = jnp.maximum(row, 0)
            places.append(used)
            used = used + jnp.where(row >= 0, 1, 0)

    def cached(first, last):
        for k in range(first, last):
            d = lax.shift_right_logical(chosen[k], PAIR.bit_length() - 1)
            j = lax.bitwise_and(chosen[k], PAIR - 1)
            asked = recv[d, pl.ds(pl.multiple_of(j * per_row, per_row), per_row), :]
            scores[k] = lax.dot_general(
                asked, kv[row_of[k], 0, :, :head_dim], NT, preferred_element_type=F32
            ) * head_dim ** (-0.5)
        for k in range(first, last):
            top = jnp.max(scores[k], -1, keepdims=True)
            expo = jnp.exp(scores[k] - top)
            expos[k] = expo.astype(BF16)
            tops[k] = jnp.broadcast_to(top, lane.shape)
            sums[k] = jnp.broadcast_to(jnp.sum(expo, -1, keepdims=True), lane.shape)
        for k in range(first, last):
            vector = jnp.dot(expos[k], kv[row_of[k], 0, :, head_dim:], preferred_element_type=F32)
            vectors[k] = (vector / sums[k]).astype(BF16)

    most = slots * 3 // 4
    cached(0, most)

    @pl.when(used > most)
    def _():
        cached(most, slots)

    for i in range(slots):
        at = (i % PAIR) * per_row
        back[i // PAIR, at : at + per_row, :] = vectors[places[i]]
    pack_statistics(tops, sums, places, back)


def units(own, groups):
    index = lax.axis_index("tensor")
    y, core = lax.div(index, 2), lax.rem(index, 2)
    core = core if own else 1 - core
    return [2 * lax.rem(y + k, groups) + core for k in (*range(1, groups), 0)]


def product(wide, w, block, tokens, column):
    at = pl.multiple_of(block * column, column)
    return jnp.dot(wide, w[:, pl.ds(at, column)], preferred_element_type=F32)[:tokens]


def widen(heads):
    return jnp.concatenate([heads[...]] * max(1, 128 // heads.shape[0]), 0)


def project(heads, w, out, own):
    away, tokens, column = out.shape
    wide = widen(heads)
    for k, block in enumerate(units(own, away + 1)[:away]):
        out[k] = product(wide, w, block, tokens, column).astype(BF16)


def merge_kernel(anc, recv, vec, stat, w, out, heads, grid_ref, sums, count):
    devices, chunk, head_dim = recv.shape
    per_row = (chunk - MORE) // PAIR
    rows = vec.shape[0] // per_row
    steps = heads.shape[0] // rows
    pieces = per_row // MORE
    quarter = head_dim // (PAIR * pieces)
    for d in range(devices):
        count[d] = 0
    part_of = lax.div(lax.broadcasted_iota(jnp.int32, (MORE, head_dim), 1), quarter)
    for r in range(rows):
        source, rank = slot_of(anc, r, rows, count)
        at = pl.multiple_of(rank * per_row, per_row)
        grid_ref[pl.ds(r * per_row, per_row), :] = recv[source, pl.ds(at, per_row), :].astype(F32)
        parts = recv[source, PAIR * per_row :, :].astype(F32)
        sums[pl.ds(r * per_row, per_row), :] = jnp.concatenate(
            [jnp.where(part_of == rank * pieces + g, parts, 0.0) for g in range(pieces)], 0
        ).astype(BF16)
    lane_from = lax.rem(lax.broadcasted_iota(jnp.int32, (head_dim, 2 * head_dim), 0), quarter)
    lane_to = lax.broadcasted_iota(jnp.int32, (head_dim, 2 * head_dim), 1)
    first = jnp.where(lane_from < 3, 1.0, 0.0)
    second = jnp.where((lane_from >= 4) & (lane_from < 7), 1.0, 0.0)
    spread = jnp.where(lane_to < head_dim, first, second)
    both = jnp.dot(sums[...], spread.astype(BF16), preferred_element_type=F32)
    top_c, sum_c = both[:, :head_dim], both[:, head_dim:]
    top_f, sum_f = stat[0], stat[1]
    top = jnp.maximum(top_c, top_f)
    factor_c = sum_c * jnp.exp(top_c - top)
    factor_f = jnp.exp(top_f - top)
    share = 1.0 / (factor_c + sum_f * factor_f)
    grid_ref[...] = (grid_ref[...] * factor_c + vec[...] * factor_f) * share
    for h in range(per_row // steps):
        for s in range(steps):
            heads[pl.ds(s * rows, rows), pl.ds(h * head_dim, head_dim)] = grid_ref[
                pl.ds(h * steps + s, rows, stride=per_row), :
            ].astype(BF16)
    project(heads, w, out, False)


def second_kernel(heads, w, out):
    project(heads, w, out, True)


def add_kernel(mine, given, *outs):
    for k, out in enumerate(outs):
        out[...] = (mine[k].astype(F32) + given[k].astype(F32)).astype(BF16)


def last_kernel(heads, w, arrived, keep, crossing):
    tokens, column = keep.shape
    groups = w.shape[1] // column // 2
    wide = widen(heads)
    crossing[...] = product(wide, w, units(False, groups)[-1], tokens, column).astype(BF16)
    keep[...] = product(wide, w, units(True, groups)[-1], tokens, column) + arrived[...].astype(F32)


def shards(inputs, norm_gain, query_proj, w_key, w_value, w_out, kv_cache, ancestors):
    rows, steps, width = inputs.shape
    context = kv_cache.shape[2]
    head_dim = kv_cache.shape[3] // 2
    local = query_proj.shape[2]
    heads = local // head_dim
    per_row = heads * steps
    devices = lax.axis_size("particle")
    tensor = lax.axis_size("tensor")
    column = width // tensor
    cosine, sine = rotary_tables(context, steps, head_dim)
    tables = np.stack([np.tile(cosine, (heads, 1)), np.tile(sine, (heads, 1))])
    smem = pl.BlockSpec(memory_space=pltpu.SMEM)
    vmem = pl.BlockSpec(memory_space=pltpu.VMEM)
    stay = pl.BlockSpec(memory_space=pl.ANY)
    hbm = lambda x: pltpu.with_memory_space_constraint(x, pltpu.HBM)
    tables = jnp.asarray(tables)

    packed = (devices, PAIR * per_row + MORE, head_dim)
    send, queries, tables, gain = pl.pallas_call(
        pack_kernel,
        out_shape=(
            jax.ShapeDtypeStruct(packed, BF16),
            jax.ShapeDtypeStruct((rows, per_row, head_dim), BF16),
            jax.ShapeDtypeStruct((2, per_row, head_dim), F32),
            jax.ShapeDtypeStruct((1, width), F32),
        ),
        in_specs=[stay] * 4,
        out_specs=(vmem,) * 4,
        scratch_shapes=[
            pltpu.VMEM((rows, per_row, head_dim), F32),
            pltpu.VMEM((rows, steps, local), BF16),
            pltpu.SMEM((rows,), jnp.int32),
            pltpu.SMEM((devices,), jnp.int32),
            pltpu.SMEM((devices * PAIR,), jnp.int32),
            pltpu.SemaphoreType.DMA((4,)),
        ],
        compiler_params=pltpu.CompilerParams(vmem_limit_bytes=4 * MIB),
        cost_estimate=pl.CostEstimate(flops=10_000_000_000, bytes_accessed=MIB, transcendentals=0),
        name="pack_queries",
    )(hbm(ancestors), hbm(query_proj), hbm(tables), hbm(norm_gain.reshape(1, width)))

    recv = lax.all_to_all(send, "particle", split_axis=0, concat_axis=0, tiled=True)

    slots = devices * PAIR
    back, vec, stat = pl.pallas_call(
        attend_kernel,
        out_shape=(
            jax.ShapeDtypeStruct(packed, BF16),
            jax.ShapeDtypeStruct((rows * per_row, head_dim), F32),
            jax.ShapeDtypeStruct((2, rows * per_row, head_dim), F32),
        ),
        in_specs=[vmem] * 8,
        out_specs=(vmem,) * 3,
        scratch_shapes=[
            pltpu.VMEM((slots, per_row, context), F32),
            pltpu.VMEM((slots, per_row, context), BF16),
            pltpu.VMEM((slots, per_row, head_dim), F32),
            pltpu.VMEM((slots, per_row, head_dim), F32),
            pltpu.VMEM((slots, per_row, head_dim), BF16),
            pltpu.VMEM((rows * steps, width), BF16),
            pltpu.SMEM((slots,), jnp.int32),
            pltpu.SMEM((slots,), jnp.int32),
        ],
        compiler_params=pltpu.CompilerParams(vmem_limit_bytes=12 * MIB),
        cost_estimate=pl.CostEstimate(
            flops=10_000_000_000, bytes_accessed=5 * MIB, transcendentals=0
        ),
        name="attention",
    )(
        recv,
        kv_cache,
        inputs,
        gain,
        w_key,
        w_value,
        queries,
        tables,
    )
    home = lax.all_to_all(back, "particle", split_axis=0, concat_axis=0, tiled=True)

    groups = tensor // 2
    away = groups - 1
    block = jax.ShapeDtypeStruct((away, rows * steps, column), BF16)
    one = jax.ShapeDtypeStruct((rows * steps, column), BF16)
    params = pltpu.CompilerParams(vmem_limit_bytes=8 * MIB)
    cost = pl.CostEstimate(
        flops=rows * steps * local * width, bytes_accessed=local * width, transcendentals=0
    )
    other, heads_out = pl.pallas_call(
        merge_kernel,
        out_shape=(
            block,
            jax.ShapeDtypeStruct((rows * steps, local), BF16),
        ),
        in_specs=[smem, vmem, vmem, vmem, vmem],
        out_specs=(vmem, vmem),
        scratch_shapes=[
            pltpu.VMEM((rows * per_row, head_dim), F32),
            pltpu.VMEM((rows * per_row, head_dim), BF16),
            pltpu.SMEM((devices,), jnp.int32),
        ],
        compiler_params=params,
        cost_estimate=cost,
        name="merge_project_sibling",
    )(ancestors, home, vec, stat, w_out)
    sibling = [(i, i ^ 1) for i in range(tensor)]
    given = lax.ppermute(other, "tensor", sibling)
    mine = pl.pallas_call(
        second_kernel,
        out_shape=block,
        in_specs=[vmem, vmem],
        out_specs=vmem,
        compiler_params=params,
        cost_estimate=cost,
        name="project_own",
    )(heads_out, w_out)
    pair = pl.pallas_call(
        add_kernel,
        out_shape=(one,) * away,
        in_specs=[vmem, vmem],
        out_specs=(vmem,) * away,
        compiler_params=params,
        name="add_sibling",
    )(mine, given)
    arrived = []
    for k in range(groups - 1, 0, -1):
        ring = [(i, ((i // 2 + k) % groups) * 2 + i % 2) for i in range(tensor)]
        arrived.append(lax.ppermute(pair[k - 1], "tensor", ring))
    keep, crossing = pl.pallas_call(
        last_kernel,
        out_shape=(jax.ShapeDtypeStruct(one.shape, F32), one),
        in_specs=[vmem, vmem, vmem],
        out_specs=(vmem, vmem),
        compiler_params=params,
        cost_estimate=cost,
        name="project_last",
    )(heads_out, w_out, arrived[0])
    total = keep + lax.ppermute(crossing, "tensor", sibling).astype(F32)
    for part in arrived[1:]:
        total = total + part.astype(F32)
    return total.astype(BF16).reshape(steps, rows, column).swapaxes(0, 1)


def solution(mesh):
    in_specs = (
        P("particle", None, None),
        P(),
        P("particle", None, "tensor"),
        P(None, "tensor"),
        P(None, "tensor"),
        P("tensor", None),
        P("particle", "tensor", None, None),
        P("particle"),
    )
    out_specs = P("particle", None, "tensor")
    return jax.shard_map(shards, mesh=mesh, in_specs=in_specs, out_specs=out_specs, check_vma=False)
```

```python
import jax
import jax.numpy as jnp
import numpy as np
from jax import lax
from jax.experimental import pallas as pl
from jax.experimental.pallas import tpu as pltpu
from jax.sharding import PartitionSpec as P

PAIR = 2
MORE = 8
THETA = 500000.0
EPSILON = 1e-05
F32 = jnp.float32
BF16 = jnp.bfloat16
MIB = 1 << 20
NT = (((1,), (1,)), ((), ()))


def rotary_tables(context, steps, head_dim):
    half = head_dim // 2
    freqs = np.float32(THETA) ** (-np.arange(half, dtype=np.float32) * np.float32(2.0) / np.float32(head_dim))
    position = (np.float32(context) + np.arange(steps, dtype=np.float32)).reshape(steps, 1)
    angles = (position * freqs.astype(np.float32)).astype(np.float32)
    cosine, sine = np.cos(angles), np.sin(angles)
    return (
        np.concatenate([cosine, cosine], 1).astype(np.float32),
        np.concatenate([-sine, sine], 1).astype(np.float32),
    )


def slots_of(anc, rows):
    sources = [lax.div(anc[r], rows) for r in range(rows)]
    ranks = []
    for r in range(rows):
        rank = jnp.int32(0)
        for q in range(r):
            rank = rank + jnp.where(sources[q] == sources[r], 1, 0)
        ranks.append(rank)
    return list(zip(sources, ranks))


def pack_kernel(
    anc_hbm, qp_hbm, tables_hbm, gain_hbm, send, queries, tables, gain, grid_ref, qp, anc, count, spots, sems
):
    pairs = ((anc_hbm, anc), (qp_hbm, qp), (tables_hbm, tables), (gain_hbm, gain))
    copies = [pltpu.make_async_copy(src, dst, sems.at[i]) for i, (src, dst) in enumerate(pairs)]
    for copy in copies:
        copy.start()
    rows, steps, width = qp.shape
    _, per_row, head_dim = tables.shape
    devices = send.shape[0]

    def clear(d, _):
        send[d] = jnp.zeros(send.shape[1:], BF16)
        count[d] = 0
        for j in range(PAIR):
            spots[PAIR * d + j] = -1
        return 0

    lax.fori_loop(0, devices, clear, 0)
    for copy in copies:
        copy.wait()
    for h in range(width // head_dim):
        grid_ref[:, steps * h : steps * (h + 1), :] = qp[:, :, head_dim * h : head_dim * (h + 1)].astype(F32)
    for r, (source, rank) in enumerate(slots_of(anc, rows)):
        spots[source * PAIR + rank] = lax.rem(anc[r], rows)
        plain = grid_ref[r]
        turned = (plain * tables[0] + pltpu.roll(plain, head_dim // 2, 1) * tables[1]).astype(BF16)
        queries[r] = turned
        send[source, pl.ds(pl.multiple_of(rank * per_row, per_row), per_row), :] = turned
    lane = lax.broadcasted_iota(jnp.int32, (MORE, head_dim), 1)
    for d in range(devices):
        send[d, PAIR * per_row :, :] = jnp.where(
            lane < head_dim // PAIR, spots[PAIR * d].astype(F32), spots[PAIR * d + 1].astype(F32)
        ).astype(BF16)


def pack_statistics(tops, sums, places, back):
    devices, _, head_dim = back.shape
    per_row = tops.shape[1]
    pieces = per_row // MORE
    lane = lax.broadcasted_iota(jnp.int32, (MORE, head_dim), 1)
    quarter = head_dim // (PAIR * pieces)
    piece_of, is_top, part_of = lax.div(lane, quarter), lax.rem(lane, quarter) < 4, lax.rem(lane, 4)
    for d in range(devices):
        value = jnp.zeros(lane.shape, F32)
        for j in range(PAIR):
            place = places[d * PAIR + j]
            for g in range(pieces):
                at = slice(g * MORE, (g + 1) * MORE)
                both = jnp.where(is_top, tops[place, at, :], sums[place, at, :])
                value = jnp.where(piece_of == j * pieces + g, both, value)
        first = value.astype(BF16).astype(F32)
        second = (value - first).astype(BF16).astype(F32)
        third = value - first - second
        back[d, PAIR * per_row :, :] = jnp.where(
            part_of == 0, first, jnp.where(part_of == 1, second, third)
        ).astype(BF16)


def attend_kernel(
    recv, kv, x, gain, wk, wv, queries, tables, back, vec, stat, *scratch
):
    scores, expos, tops, sums, vectors, normed, chosen, row_of = scratch
    devices, _, head_dim = recv.shape
    per_row = queries.shape[1]
    lane = lax.broadcasted_iota(jnp.int32, (per_row, head_dim), 1)
    rows, steps, width = x.shape
    tokens = rows * steps
    floats = x[...].reshape(tokens, width).astype(F32)
    inverse = lax.rsqrt(jnp.mean(floats * floats, -1, keepdims=True) + EPSILON)
    normed[...] = (floats * inverse * gain[...]).astype(BF16)
    repeat = tokens // per_row
    cosine, sine = (jnp.concatenate([tables[i]] * repeat, 0) for i in range(2))
    keys = jnp.dot(normed[...], wk[...], preferred_element_type=F32)
    keys = (keys * cosine + pltpu.roll(keys, head_dim // 2, 1) * sine).astype(BF16)
    vals = jnp.dot(normed[...], wv[...], preferred_element_type=F32).astype(BF16)
    flat = queries[...].reshape(rows * per_row, head_dim)
    fresh = lax.dot_general(flat, keys, NT, preferred_element_type=F32) * head_dim ** (-0.5)
    row = lax.broadcasted_iota(jnp.int32, fresh.shape, 0)
    col = lax.broadcasted_iota(jnp.int32, fresh.shape, 1)
    seen = (lax.div(row, per_row) == lax.div(col, steps)) & (lax.rem(col, steps) <= lax.rem(row, steps))
    top = jnp.max(jnp.where(seen, fresh, -jnp.inf), -1, keepdims=True)
    expo = jnp.where(seen, jnp.exp(jnp.where(seen, fresh - top, 0.0)), 0.0)
    vec[...] = jnp.dot(expo.astype(BF16), vals, preferred_element_type=F32)
    stat[0] = jnp.broadcast_to(top, stat.shape[1:])
    stat[1] = jnp.broadcast_to(jnp.sum(expo, -1, keepdims=True), stat.shape[1:])
    slots = devices * PAIR
    for k in range(slots):
        chosen[k] = 0
        row_of[k] = 0
    used = jnp.int32(0)
    places = []
    for d in range(devices):
        spot = recv[d, PAIR * per_row :, :].astype(F32)
        for j in range(PAIR):
            row = spot[0, j * (head_dim // PAIR)].astype(jnp.int32)
            chosen[used] = d * PAIR + j
            row_of[used] = jnp.maximum(row, 0)
            places.append(used)
            used = used + jnp.where(row >= 0, 1, 0)

    def cached(first, last):
        for k in range(first, last):
            d = lax.shift_right_logical(chosen[k], PAIR.bit_length() - 1)
            j = lax.bitwise_and(chosen[k], PAIR - 1)
            asked = recv[d, pl.ds(pl.multiple_of(j * per_row, per_row), per_row), :]
            scores[k] = lax.dot_general(
                asked, kv[row_of[k], 0, :, :head_dim], NT, preferred_element_type=F32
            ) * head_dim ** (-0.5)
        for k in range(first, last):
            top = jnp.max(scores[k], -1, keepdims=True)
            expo = jnp.exp(scores[k] - top)
            expos[k] = expo.astype(BF16)
            tops[k] = jnp.broadcast_to(top, lane.shape)
            sums[k] = jnp.broadcast_to(jnp.sum(expo, -1, keepdims=True), lane.shape)
        for k in range(first, last):
            vector = jnp.dot(expos[k], kv[row_of[k], 0, :, head_dim:], preferred_element_type=F32)
            vectors[k] = (vector / sums[k]).astype(BF16)

    most = slots * 3 // 4
    cached(0, most)

    @pl.when(used > most)
    def _():
        cached(most, slots)

    for i in range(slots):
        at = (i % PAIR) * per_row
        back[i // PAIR, at : at + per_row, :] = vectors[places[i]]
    pack_statistics(tops, sums, places, back)


def units(own, groups):
    index = lax.axis_index("tensor")
    y, core = lax.div(index, 2), lax.rem(index, 2)
    core = core if own else 1 - core
    return [2 * lax.rem(y + k, groups) + core for k in (*range(1, groups), 0)]


def product(wide, w, block, tokens, column):
    at = pl.multiple_of(block * column, column)
    return jnp.dot(wide, w[:, pl.ds(at, column)], preferred_element_type=F32)[:tokens]


def widen(heads):
    return jnp.concatenate([heads[...]] * max(1, 128 // heads.shape[0]), 0)


def project(heads, w, out, own):
    away, tokens, column = out.shape
    wide = widen(heads)
    for k, block in enumerate(units(own, away + 1)[:away]):
        out[k] = product(wide, w, block, tokens, column).astype(BF16)


def merge_kernel(anc, recv, vec, stat, w, out, heads, grid_ref, sums, count):
    devices, chunk, head_dim = recv.shape
    per_row = (chunk - MORE) // PAIR
    rows = vec.shape[0] // per_row
    steps = heads.shape[0] // rows
    pieces = per_row // MORE
    quarter = head_dim // (PAIR * pieces)
    for d in range(devices):
        count[d] = 0
    part_of = lax.div(lax.broadcasted_iota(jnp.int32, (MORE, head_dim), 1), quarter)
    for r, (source, rank) in enumerate(slots_of(anc, rows)):
        at = pl.multiple_of(rank * per_row, per_row)
        grid_ref[pl.ds(r * per_row, per_row), :] = recv[source, pl.ds(at, per_row), :].astype(F32)
        parts = recv[source, PAIR * per_row :, :].astype(F32)
        sums[pl.ds(r * per_row, per_row), :] = jnp.concatenate(
            [jnp.where(part_of == rank * pieces + g, parts, 0.0) for g in range(pieces)], 0
        ).astype(BF16)
    lane_from = lax.rem(lax.broadcasted_iota(jnp.int32, (head_dim, 2 * head_dim), 0), quarter)
    lane_to = lax.broadcasted_iota(jnp.int32, (head_dim, 2 * head_dim), 1)
    first = jnp.where(lane_from < 3, 1.0, 0.0)
    second = jnp.where((lane_from >= 4) & (lane_from < 7), 1.0, 0.0)
    spread = jnp.where(lane_to < head_dim, first, second)
    both = jnp.dot(sums[...], spread.astype(BF16), preferred_element_type=F32)
    top_c, sum_c = both[:, :head_dim], both[:, head_dim:]
    top_f, sum_f = stat[0], stat[1]
    top = jnp.maximum(top_c, top_f)
    factor_c = sum_c * jnp.exp(top_c - top)
    factor_f = jnp.exp(top_f - top)
    share = 1.0 / (factor_c + sum_f * factor_f)
    grid_ref[...] = (grid_ref[...] * factor_c + vec[...] * factor_f) * share
    for h in range(per_row // steps):
        for s in range(steps):
            heads[pl.ds(s * rows, rows), pl.ds(h * head_dim, head_dim)] = grid_ref[
                pl.ds(h * steps + s, rows, stride=per_row), :
            ].astype(BF16)
    project(heads, w, out, False)


def second_kernel(heads, w, out):
    project(heads, w, out, True)


def add_kernel(mine, given, *outs):
    for k, out in enumerate(outs):
        out[...] = (mine[k].astype(F32) + given[k].astype(F32)).astype(BF16)


def last_kernel(heads, w, arrived, keep, crossing):
    tokens, column = keep.shape
    groups = w.shape[1] // column // 2
    wide = widen(heads)
    crossing[...] = product(wide, w, units(False, groups)[-1], tokens, column).astype(BF16)
    keep[...] = product(wide, w, units(True, groups)[-1], tokens, column) + arrived[...].astype(F32)


def shards(inputs, norm_gain, query_proj, w_key, w_value, w_out, kv_cache, ancestors):
    rows, steps, width = inputs.shape
    context = kv_cache.shape[2]
    head_dim = kv_cache.shape[3] // 2
    local = query_proj.shape[2]
    heads = local // head_dim
    per_row = heads * steps
    devices = lax.axis_size("particle")
    tensor = lax.axis_size("tensor")
    column = width // tensor
    cosine, sine = rotary_tables(context, steps, head_dim)
    tables = np.stack([np.tile(cosine, (heads, 1)), np.tile(sine, (heads, 1))])
    smem = pl.BlockSpec(memory_space=pltpu.SMEM)
    vmem = pl.BlockSpec(memory_space=pltpu.VMEM)
    stay = pl.BlockSpec(memory_space=pl.ANY)
    hbm = lambda x: pltpu.with_memory_space_constraint(x, pltpu.HBM)
    tables = jnp.asarray(tables)

    packed = (devices, PAIR * per_row + MORE, head_dim)
    send, queries, tables, gain = pl.pallas_call(
        pack_kernel,
        out_shape=(
            jax.ShapeDtypeStruct(packed, BF16),
            jax.ShapeDtypeStruct((rows, per_row, head_dim), BF16),
            jax.ShapeDtypeStruct((2, per_row, head_dim), F32),
            jax.ShapeDtypeStruct((1, width), F32),
        ),
        in_specs=[stay] * 4,
        out_specs=(vmem,) * 4,
        scratch_shapes=[
            pltpu.VMEM((rows, per_row, head_dim), F32),
            pltpu.VMEM((rows, steps, local), BF16),
            pltpu.SMEM((rows,), jnp.int32),
            pltpu.SMEM((devices,), jnp.int32),
            pltpu.SMEM((devices * PAIR,), jnp.int32),
            pltpu.SemaphoreType.DMA((4,)),
        ],
        compiler_params=pltpu.CompilerParams(vmem_limit_bytes=4 * MIB),
        cost_estimate=pl.CostEstimate(flops=10_000_000_000, bytes_accessed=MIB, transcendentals=0),
        name="pack_queries",
    )(hbm(ancestors), hbm(query_proj), hbm(tables), hbm(norm_gain.reshape(1, width)))

    recv = lax.all_to_all(send, "particle", split_axis=0, concat_axis=0, tiled=True)

    slots = devices * PAIR
    back, vec, stat = pl.pallas_call(
        attend_kernel,
        out_shape=(
            jax.ShapeDtypeStruct(packed, BF16),
            jax.ShapeDtypeStruct((rows * per_row, head_dim), F32),
            jax.ShapeDtypeStruct((2, rows * per_row, head_dim), F32),
        ),
        in_specs=[vmem] * 8,
        out_specs=(vmem,) * 3,
        scratch_shapes=[
            pltpu.VMEM((slots, per_row, context), F32),
            pltpu.VMEM((slots, per_row, context), BF16),
            pltpu.VMEM((slots, per_row, head_dim), F32),
            pltpu.VMEM((slots, per_row, head_dim), F32),
            pltpu.VMEM((slots, per_row, head_dim), BF16),
            pltpu.VMEM((rows * steps, width), BF16),
            pltpu.SMEM((slots,), jnp.int32),
            pltpu.SMEM((slots,), jnp.int32),
        ],
        compiler_params=pltpu.CompilerParams(vmem_limit_bytes=12 * MIB),
        cost_estimate=pl.CostEstimate(
            flops=10_000_000_000, bytes_accessed=5 * MIB, transcendentals=0
        ),
        name="attention",
    )(
        recv,
        kv_cache,
        inputs,
        gain,
        w_key,
        w_value,
        queries,
        tables,
    )
    home = lax.all_to_all(back, "particle", split_axis=0, concat_axis=0, tiled=True)

    groups = tensor // 2
    away = groups - 1
    block = jax.ShapeDtypeStruct((away, rows * steps, column), BF16)
    one = jax.ShapeDtypeStruct((rows * steps, column), BF16)
    params = pltpu.CompilerParams(vmem_limit_bytes=8 * MIB)
    cost = pl.CostEstimate(
        flops=rows * steps * local * width, bytes_accessed=local * width, transcendentals=0
    )
    other, heads_out = pl.pallas_call(
        merge_kernel,
        out_shape=(
            block,
            jax.ShapeDtypeStruct((rows * steps, local), BF16),
        ),
        in_specs=[smem, vmem, vmem, vmem, vmem],
        out_specs=(vmem, vmem),
        scratch_shapes=[
            pltpu.VMEM((rows * per_row, head_dim), F32),
            pltpu.VMEM((rows * per_row, head_dim), BF16),
            pltpu.SMEM((devices,), jnp.int32),
        ],
        compiler_params=params,
        cost_estimate=cost,
        name="merge_project_sibling",
    )(ancestors, home, vec, stat, w_out)
    sibling = [(i, i ^ 1) for i in range(tensor)]
    given = lax.ppermute(other, "tensor", sibling)
    mine = pl.pallas_call(
        second_kernel,
        out_shape=block,
        in_specs=[vmem, vmem],
        out_specs=vmem,
        compiler_params=params,
        cost_estimate=cost,
        name="project_own",
    )(heads_out, w_out)
    pair = pl.pallas_call(
        add_kernel,
        out_shape=(one,) * away,
        in_specs=[vmem, vmem],
        out_specs=(vmem,) * away,
        compiler_params=params,
        name="add_sibling",
    )(mine, given)
    arrived = []
    for k in range(1, groups):
        ring = [(i, ((i // 2 + k) % groups) * 2 + i % 2) for i in range(tensor)]
        arrived.append(lax.ppermute(pair[k - 1], "tensor", ring))
    keep, crossing = pl.pallas_call(
        last_kernel,
        out_shape=(jax.ShapeDtypeStruct(one.shape, F32), one),
        in_specs=[vmem, vmem, vmem],
        out_specs=(vmem, vmem),
        compiler_params=params,
        cost_estimate=cost,
        name="project_last",
    )(heads_out, w_out, arrived[0])
    total = keep + lax.ppermute(crossing, "tensor", sibling).astype(F32)
    for part in arrived[1:]:
        total = total + part.astype(F32)
    return total.astype(BF16).reshape(steps, rows, column).swapaxes(0, 1)


def solution(mesh):
    in_specs = (
        P("particle", None, None),
        P(),
        P("particle", None, "tensor"),
        P(None, "tensor"),
        P(None, "tensor"),
        P("tensor", None),
        P("particle", "tensor", None, None),
        P("particle"),
    )
    out_specs = P("particle", None, "tensor")
    return jax.shard_map(shards, mesh=mesh, in_specs=in_specs, out_specs=out_specs, check_vma=False)
```

```python
import jax
import jax.numpy as jnp
import numpy as np
from jax import lax
from jax.experimental import pallas as pl
from jax.experimental.pallas import tpu as pltpu
from jax.sharding import PartitionSpec as P

PAIR = 2
MORE = 8
THETA = 500000.0
EPSILON = 1e-05
F32 = jnp.float32
BF16 = jnp.bfloat16
MIB = 1 << 20
NT = (((1,), (1,)), ((), ()))


def rotary_tables(context, steps, head_dim):
    half = head_dim // 2
    freqs = np.float32(THETA) ** (-np.arange(half, dtype=np.float32) * np.float32(2.0) / np.float32(head_dim))
    position = (np.float32(context) + np.arange(steps, dtype=np.float32)).reshape(steps, 1)
    angles = (position * freqs.astype(np.float32)).astype(np.float32)
    cosine, sine = np.cos(angles), np.sin(angles)
    return (
        np.concatenate([cosine, cosine], 1).astype(np.float32),
        np.concatenate([-sine, sine], 1).astype(np.float32),
    )


def slot_of(anc, row, rows, count):
    source = lax.div(anc[row], rows)
    rank = count[source]
    count[source] = rank + 1
    return source, rank


def pack_kernel(
    anc_hbm, qp_hbm, tables_hbm, gain_hbm, send, queries, tables, gain, grid_ref, qp, anc, count, spots, sems
):
    pairs = ((anc_hbm, anc), (qp_hbm, qp), (tables_hbm, tables), (gain_hbm, gain))
    copies = [pltpu.make_async_copy(src, dst, sems.at[i]) for i, (src, dst) in enumerate(pairs)]
    for copy in copies:
        copy.start()
    rows, steps, width = qp.shape
    _, per_row, head_dim = tables.shape
    devices = send.shape[0]

    def clear(d, _):
        send[d] = jnp.zeros(send.shape[1:], BF16)
        count[d] = 0
        for j in range(PAIR):
            spots[PAIR * d + j] = -1
        return 0

    lax.fori_loop(0, devices, clear, 0)
    for copy in copies:
        copy.wait()
    for h in range(width // head_dim):
        grid_ref[:, steps * h : steps * (h + 1), :] = qp[:, :, head_dim * h : head_dim * (h + 1)].astype(F32)
    for r in range(rows):
        source, rank = slot_of(anc, r, rows, count)
        spots[source * PAIR + rank] = lax.rem(anc[r], rows)
        plain = grid_ref[r]
        turned = (plain * tables[0] + pltpu.roll(plain, head_dim // 2, 1) * tables[1]).astype(BF16)
        queries[r] = turned
        send[source, pl.ds(pl.multiple_of(rank * per_row, per_row), per_row), :] = turned
    lane = lax.broadcasted_iota(jnp.int32, (MORE, head_dim), 1)
    for d in range(devices):
        send[d, PAIR * per_row :, :] = jnp.where(
            lane < head_dim // PAIR, spots[PAIR * d].astype(F32), spots[PAIR * d + 1].astype(F32)
        ).astype(BF16)


def pack_statistics(tops, sums, places, back):
    devices, _, head_dim = back.shape
    per_row = tops.shape[1]
    pieces = per_row // MORE
    lane = lax.broadcasted_iota(jnp.int32, (MORE, head_dim), 1)
    quarter = head_dim // (PAIR * pieces)
    piece_of, is_top, part_of = lax.div(lane, quarter), lax.rem(lane, quarter) < 4, lax.rem(lane, 4)
    for d in range(devices):
        value = jnp.zeros(lane.shape, F32)
        for j in range(PAIR):
            place = places[d * PAIR + j]
            for g in range(pieces):
                at = slice(g * MORE, (g + 1) * MORE)
                both = jnp.where(is_top, tops[place, at, :], sums[place, at, :])
                value = jnp.where(piece_of == j * pieces + g, both, value)
        first = value.astype(BF16).astype(F32)
        second = (value - first).astype(BF16).astype(F32)
        third = value - first - second
        back[d, PAIR * per_row :, :] = jnp.where(
            part_of == 0, first, jnp.where(part_of == 1, second, third)
        ).astype(BF16)


def attend_kernel(
    recv, kv, x, gain, wk, wv, queries, tables, back, vec, stat, *scratch
):
    scores, expos, tops, sums, vectors, normed, chosen, row_of = scratch
    devices, _, head_dim = recv.shape
    per_row = queries.shape[1]
    lane = lax.broadcasted_iota(jnp.int32, (per_row, head_dim), 1)
    rows, steps, width = x.shape
    tokens = rows * steps
    floats = x[...].reshape(tokens, width).astype(F32)
    inverse = lax.rsqrt(jnp.mean(floats * floats, -1, keepdims=True) + EPSILON)
    normed[...] = (floats * inverse * gain[...]).astype(BF16)
    repeat = tokens // per_row
    cosine, sine = (jnp.concatenate([tables[i]] * repeat, 0) for i in range(2))
    keys = jnp.dot(normed[...], wk[...], preferred_element_type=F32)
    keys = (keys * cosine + pltpu.roll(keys, head_dim // 2, 1) * sine).astype(BF16)
    vals = jnp.dot(normed[...], wv[...], preferred_element_type=F32).astype(BF16)
    flat = queries[...].reshape(rows * per_row, head_dim)
    fresh = lax.dot_general(flat, keys, NT, preferred_element_type=F32) * head_dim ** (-0.5)
    row = lax.broadcasted_iota(jnp.int32, fresh.shape, 0)
    col = lax.broadcasted_iota(jnp.int32, fresh.shape, 1)
    seen = (lax.div(row, per_row) == lax.div(col, steps)) & (lax.rem(col, steps) <= lax.rem(row, steps))
    top = jnp.max(jnp.where(seen, fresh, -jnp.inf), -1, keepdims=True)
    expo = jnp.where(seen, jnp.exp(jnp.where(seen, fresh - top, 0.0)), 0.0)
    vec[...] = jnp.dot(expo.astype(BF16), vals, preferred_element_type=F32)
    stat[0] = jnp.broadcast_to(top, stat.shape[1:])
    stat[1] = jnp.broadcast_to(jnp.sum(expo, -1, keepdims=True), stat.shape[1:])
    slots = devices * PAIR
    for k in range(slots):
        chosen[k] = 0
        row_of[k] = 0
    used = jnp.int32(0)
    places = []
    for d in range(devices):
        spot = recv[d, PAIR * per_row :, :].astype(F32)
        for j in range(PAIR):
            row = spot[0, j * (head_dim // PAIR)].astype(jnp.int32)
            chosen[used] = d * PAIR + j
            row_of[used] = jnp.maximum(row, 0)
            places.append(used)
            used = used + jnp.where(row >= 0, 1, 0)

    def cached(first, last):
        for k in range(first, last):
            d = lax.shift_right_logical(chosen[k], PAIR.bit_length() - 1)
            j = lax.bitwise_and(chosen[k], PAIR - 1)
            asked = recv[d, pl.ds(pl.multiple_of(j * per_row, per_row), per_row), :]
            scores[k] = lax.dot_general(
                asked, kv[row_of[k], 0, :, :head_dim], NT, preferred_element_type=F32
            ) * head_dim ** (-0.5)
        for k in range(first, last):
            top = jnp.max(scores[k], -1, keepdims=True)
            expo = jnp.exp(scores[k] - top)
            expos[k] = expo.astype(BF16)
            tops[k] = jnp.broadcast_to(top, lane.shape)
            sums[k] = jnp.broadcast_to(jnp.sum(expo, -1, keepdims=True), lane.shape)
        for k in range(first, last):
            vector = jnp.dot(expos[k], kv[row_of[k], 0, :, head_dim:], preferred_element_type=F32)
            vectors[k] = (vector / sums[k]).astype(BF16)

    most = slots * 3 // 4
    cached(0, most)

    @pl.when(used > most)
    def _():
        cached(most, slots)

    for i in range(slots):
        at = (i % PAIR) * per_row
        back[i // PAIR, at : at + per_row, :] = vectors[places[i]]
    pack_statistics(tops, sums, places, back)


def units(own, groups):
    index = lax.axis_index("tensor")
    y, core = lax.div(index, 2), lax.rem(index, 2)
    core = core if own else 1 - core
    return [2 * lax.rem(y + k, groups) + core for k in (*range(1, groups), 0)]


def product(wide, w, block, tokens, column):
    at = pl.multiple_of(block * column, column)
    return jnp.dot(wide, w[:, pl.ds(at, column)], preferred_element_type=F32)[:tokens]


def widen(heads):
    return jnp.concatenate([heads[...]] * max(1, 128 // heads.shape[0]), 0)


def project(heads, w, out, own):
    away, tokens, column = out.shape
    wide = widen(heads)
    for k, block in enumerate(units(own, away + 1)[:away]):
        out[k] = product(wide, w, block, tokens, column).astype(BF16)


def merge_kernel(anc, recv, vec, stat, w, out, heads, grid_ref, sums, lined, count):
    devices, chunk, head_dim = recv.shape
    per_row = (chunk - MORE) // PAIR
    rows = vec.shape[0] // per_row
    steps = heads.shape[0] // rows
    pieces = per_row // MORE
    quarter = head_dim // (PAIR * pieces)
    for d in range(devices):
        count[d] = 0
    part_of = lax.div(lax.broadcasted_iota(jnp.int32, (MORE, head_dim), 1), quarter)
    for r in range(rows):
        source, rank = slot_of(anc, r, rows, count)
        at = pl.multiple_of(rank * per_row, per_row)
        grid_ref[pl.ds(r * per_row, per_row), :] = recv[source, pl.ds(at, per_row), :].astype(F32)
        parts = recv[source, PAIR * per_row :, :].astype(F32)
        sums[pl.ds(r * per_row, per_row), :] = jnp.concatenate(
            [jnp.where(part_of == rank * pieces + g, parts, 0.0) for g in range(pieces)], 0
        ).astype(BF16)
    lane_from = lax.rem(lax.broadcasted_iota(jnp.int32, (head_dim, 2 * head_dim), 0), quarter)
    lane_to = lax.broadcasted_iota(jnp.int32, (head_dim, 2 * head_dim), 1)
    first = jnp.where(lane_from < 3, 1.0, 0.0)
    second = jnp.where((lane_from >= 4) & (lane_from < 7), 1.0, 0.0)
    spread = jnp.where(lane_to < head_dim, first, second)
    both = jnp.dot(sums[...], spread.astype(BF16), preferred_element_type=F32)
    top_c, sum_c = both[:, :head_dim], both[:, head_dim:]
    top_f, sum_f = stat[0], stat[1]
    top = jnp.maximum(top_c, top_f)
    factor_c = sum_c * jnp.exp(top_c - top)
    factor_f = jnp.exp(top_f - top)
    share = 1.0 / (factor_c + sum_f * factor_f)
    grid_ref[...] = (grid_ref[...] * factor_c + vec[...] * factor_f) * share
    for h in range(per_row // steps):
        for s in range(steps):
            lined[h, pl.ds(s, rows, stride=steps), :] = grid_ref[pl.ds(h * steps + s, rows, stride=per_row), :]
        heads[:, pl.ds(h * head_dim, head_dim)] = lined[h].astype(BF16)
    project(heads, w, out, False)


def second_kernel(heads, w, out):
    project(heads, w, out, True)


def add_kernel(mine, given, *outs):
    for k, out in enumerate(outs):
        out[...] = (mine[k].astype(F32) + given[k].astype(F32)).astype(BF16)


def last_kernel(heads, w, arrived, keep, crossing):
    tokens, column = keep.shape
    groups = w.shape[1] // column // 2
    wide = widen(heads)
    crossing[...] = product(wide, w, units(False, groups)[-1], tokens, column).astype(BF16)
    keep[...] = product(wide, w, units(True, groups)[-1], tokens, column) + arrived[...].astype(F32)


def shards(inputs, norm_gain, query_proj, w_key, w_value, w_out, kv_cache, ancestors):
    rows, steps, width = inputs.shape
    context = kv_cache.shape[2]
    head_dim = kv_cache.shape[3] // 2
    local = query_proj.shape[2]
    heads = local // head_dim
    per_row = heads * steps
    devices = lax.axis_size("particle")
    tensor = lax.axis_size("tensor")
    column = width // tensor
    cosine, sine = rotary_tables(context, steps, head_dim)
    tables = np.stack([np.tile(cosine, (heads, 1)), np.tile(sine, (heads, 1))])
    smem = pl.BlockSpec(memory_space=pltpu.SMEM)
    vmem = pl.BlockSpec(memory_space=pltpu.VMEM)
    stay = pl.BlockSpec(memory_space=pl.ANY)
    hbm = lambda x: pltpu.with_memory_space_constraint(x, pltpu.HBM)
    tables = jnp.asarray(tables)

    packed = (devices, PAIR * per_row + MORE, head_dim)
    send, queries, tables, gain = pl.pallas_call(
        pack_kernel,
        out_shape=(
            jax.ShapeDtypeStruct(packed, BF16),
            jax.ShapeDtypeStruct((rows, per_row, head_dim), BF16),
            jax.ShapeDtypeStruct((2, per_row, head_dim), F32),
            jax.ShapeDtypeStruct((1, width), F32),
        ),
        in_specs=[stay] * 4,
        out_specs=(vmem,) * 4,
        scratch_shapes=[
            pltpu.VMEM((rows, per_row, head_dim), F32),
            pltpu.VMEM((rows, steps, local), BF16),
            pltpu.SMEM((rows,), jnp.int32),
            pltpu.SMEM((devices,), jnp.int32),
            pltpu.SMEM((devices * PAIR,), jnp.int32),
            pltpu.SemaphoreType.DMA((4,)),
        ],
        compiler_params=pltpu.CompilerParams(vmem_limit_bytes=4 * MIB),
        cost_estimate=pl.CostEstimate(flops=10_000_000_000, bytes_accessed=MIB, transcendentals=0),
        name="pack_queries",
    )(hbm(ancestors), hbm(query_proj), hbm(tables), hbm(norm_gain.reshape(1, width)))

    recv = lax.all_to_all(send, "particle", split_axis=0, concat_axis=0, tiled=True)

    slots = devices * PAIR
    back, vec, stat = pl.pallas_call(
        attend_kernel,
        out_shape=(
            jax.ShapeDtypeStruct(packed, BF16),
            jax.ShapeDtypeStruct((rows * per_row, head_dim), F32),
            jax.ShapeDtypeStruct((2, rows * per_row, head_dim), F32),
        ),
        in_specs=[vmem] * 8,
        out_specs=(vmem,) * 3,
        scratch_shapes=[
            pltpu.VMEM((slots, per_row, context), F32),
            pltpu.VMEM((slots, per_row, context), BF16),
            pltpu.VMEM((slots, per_row, head_dim), F32),
            pltpu.VMEM((slots, per_row, head_dim), F32),
            pltpu.VMEM((slots, per_row, head_dim), BF16),
            pltpu.VMEM((rows * steps, width), BF16),
            pltpu.SMEM((slots,), jnp.int32),
            pltpu.SMEM((slots,), jnp.int32),
        ],
        compiler_params=pltpu.CompilerParams(vmem_limit_bytes=12 * MIB),
        cost_estimate=pl.CostEstimate(
            flops=10_000_000_000, bytes_accessed=5 * MIB, transcendentals=0
        ),
        name="attention",
    )(
        recv,
        kv_cache,
        inputs,
        gain,
        w_key,
        w_value,
        queries,
        tables,
    )
    home = lax.all_to_all(back, "particle", split_axis=0, concat_axis=0, tiled=True)

    groups = tensor // 2
    away = groups - 1
    block = jax.ShapeDtypeStruct((away, rows * steps, column), BF16)
    one = jax.ShapeDtypeStruct((rows * steps, column), BF16)
    params = pltpu.CompilerParams(vmem_limit_bytes=8 * MIB)
    cost = pl.CostEstimate(
        flops=rows * steps * local * width, bytes_accessed=local * width, transcendentals=0
    )
    other, heads_out = pl.pallas_call(
        merge_kernel,
        out_shape=(
            block,
            jax.ShapeDtypeStruct((rows * steps, local), BF16),
        ),
        in_specs=[smem, vmem, vmem, vmem, vmem],
        out_specs=(vmem, vmem),
        scratch_shapes=[
            pltpu.VMEM((rows * per_row, head_dim), F32),
            pltpu.VMEM((rows * per_row, head_dim), BF16),
            pltpu.VMEM((heads, rows * steps, head_dim), F32),
            pltpu.SMEM((devices,), jnp.int32),
        ],
        compiler_params=params,
        cost_estimate=cost,
        name="merge_project_sibling",
    )(ancestors, home, vec, stat, w_out)
    sibling = [(i, i ^ 1) for i in range(tensor)]
    given = lax.ppermute(other, "tensor", sibling)
    mine = pl.pallas_call(
        second_kernel,
        out_shape=block,
        in_specs=[vmem, vmem],
        out_specs=vmem,
        compiler_params=params,
        cost_estimate=cost,
        name="project_own",
    )(heads_out, w_out)
    pair = pl.pallas_call(
        add_kernel,
        out_shape=(one,) * away,
        in_specs=[vmem, vmem],
        out_specs=(vmem,) * away,
        compiler_params=params,
        name="add_sibling",
    )(mine, given)
    arrived = []
    for k in range(1, groups):
        ring = [(i, ((i // 2 + k) % groups) * 2 + i % 2) for i in range(tensor)]
        arrived.append(lax.ppermute(pair[k - 1], "tensor", ring))
    keep, crossing = pl.pallas_call(
        last_kernel,
        out_shape=(jax.ShapeDtypeStruct(one.shape, F32), one),
        in_specs=[vmem, vmem, vmem],
        out_specs=(vmem, vmem),
        compiler_params=params,
        cost_estimate=cost,
        name="project_last",
    )(heads_out, w_out, arrived[0])
    total = keep + lax.ppermute(crossing, "tensor", sibling).astype(F32)
    for part in arrived[1:]:
        total = total + part.astype(F32)
    return total.astype(BF16).reshape(rows, steps, column)


def solution(mesh):
    in_specs = (
        P("particle", None, None),
        P(),
        P("particle", None, "tensor"),
        P(None, "tensor"),
        P(None, "tensor"),
        P("tensor", None),
        P("particle", "tensor", None, None),
        P("particle"),
    )
    out_specs = P("particle", None, "tensor")
    return jax.shard_map(shards, mesh=mesh, in_specs=in_specs, out_specs=out_specs, check_vma=False)
```
